512 devices in a mesh: dp: 32 (over y, x), seq: 16 (over z, core).
Axes of the slice: x: 4, y: 8, z: 8, core: 2. Of those that a mesh axis runs over, the one named last changes fastest.
Arguments:
- patches: bfloat16 [32, 768, 1408], P('dp', 'seq'), may hold values from -6 to 6
- keep_pos: int32 [32, 768], P('dp', 'seq'), may hold values from -1 to 4095, as said below
- kept_counts: int32 [32, 16], P('dp'), may hold values from 16 to 48, as said below
- enc_gain: float32 [1408], replicated, may hold values from 0.25 to 1.75
- w_qkv: bfloat16 [3, 1408, 1408], P(None, None, 'seq'), may hold values from -2 to 2
- w_out: bfloat16 [1408, 1408], P('seq'), may hold values from -12 to 12
- w_e2d: bfloat16 [1408, 512], replicated, may hold values from -0.15625 to 0.15625
- mask_token: bfloat16 [512], replicated, may hold values from -4 to 4
- dec_gain: float32 [512], replicated, may hold values from 0.25 to 1.75
- fc_in: bfloat16 [2048, 512], P('seq'), may hold values from -0.25 to 0.25
- fc_out: bfloat16 [2048, 512], P('seq'), may hold values from -0.125 to 0.125
- cotangent: bfloat16 [32, 4096, 512], P('dp', 'seq'), may hold values from -6 to 6
Outputs:
- recon: bfloat16 [32, 4096, 512], P('dp', 'seq')
- grad_qkv: bfloat16 [3, 1408, 1408], P(None, None, 'seq')
- grad_out: bfloat16 [1408, 1408], P('seq')
The draws below stay inside these ranges and needn't reach their ends.
Inputs may be any that keep to these rules, and one draw needn't show every extreme that they name: `keep_pos`: rows j < kept_counts[s] of device s's block hold distinct tube positions of the clip, the other rows -1; no device's block holds more than 3 positions of one range of 256 positions; in every clip some device holds exactly 3 in every range, and some range receives exactly 3 from every device. `kept_counts`: the counts of a clip sum to 430; some device holds exactly 48.
All inputs are finite; a program needn't handle non-finite values.
Results may differ from the reference program's by a relative error of at most 0.03.
Values may be sent and summed in bfloat16 or wider, within the bound.
No kernel may reach another device: no remote copies, remote signals or barrier semaphores. Data moves between devices by JAX's collectives and lax.ppermute only.
A program may use at most 64 MiB of HBM per device.

```python
import jax
import jax.numpy as jnp
from jax import lax

D = 1408
HEADS = 16
HD = 88
DD = 512
DH = 2048
F = 256
CAPX = 3
CAP = 48
FULL = 4096
CLIPS = 32
N_SEQ = 16


def clip_layout(key):
    k_mix, k_source, k_target, k_slots, k_order = jax.random.split(key, 5)
    rest = (N_SEQ - 1) * (N_SEQ - 1)
    span = CAPX - 1
    base = 1 + jnp.arange(rest, dtype=jnp.int32) % span
    base = jax.random.permutation(k_mix, base).reshape(N_SEQ - 1, N_SEQ - 1)
    heavy_source = jax.random.randint(k_source, (), 0, N_SEQ)
    heavy_target = jax.random.randint(k_target, (), 0, N_SEQ)
    source = jnp.arange(N_SEQ, dtype=jnp.int32)
    src_row = jnp.clip(source - (source > heavy_source).astype(jnp.int32), 0, N_SEQ - 2)
    dst_col = jnp.clip(source - (source > heavy_target).astype(jnp.int32), 0, N_SEQ - 2)
    inner = base[src_row][:, dst_col]
    heavy = (source == heavy_source)[:, None] | (source == heavy_target)[None, :]
    sends = jnp.where(heavy, CAPX, inner).astype(jnp.int32)
    counts = jnp.sum(sends, axis=1).astype(jnp.int32)
    slots = jax.vmap(lambda k: jax.random.permutation(k, F))(jax.random.split(k_slots, N_SEQ)).astype(jnp.int32)
    col_start = jnp.cumsum(sends, axis=0) - sends
    row_off = jnp.cumsum(sends, axis=1) - sends
    place = jnp.arange(CAP, dtype=jnp.int32)
    dest = jnp.sum((row_off[:, None, :] <= place[None, :, None]).astype(jnp.int32), axis=2) - 1
    offset_in = place[None, :] - jnp.take_along_axis(row_off, dest, axis=1)
    slot_index = jnp.clip(jnp.take_along_axis(col_start, dest, axis=1) + offset_in, 0, F - 1)
    positions = dest * F + slots[dest, slot_index]
    live = place[None, :] < counts[:, None]
    scores = jax.random.randint(k_order, (N_SEQ, CAP), 0, 2 ** 16) * CAP + place[None, :]
    scores = jnp.where(live, scores, 2 ** 30 + place[None, :])
    order = jnp.argsort(scores, axis=1, stable=True)
    positions = jnp.where(live, jnp.take_along_axis(positions, order, axis=1), -1)
    return (positions.reshape(-1).astype(jnp.int32), counts)


def draw_keep_pos(key, part):
    keys = jax.random.split(key, CLIPS)
    positions, counts = jax.vmap(clip_layout)(keys)
    return positions


def draw_kept_counts(key, part):
    keys = jax.random.split(key, CLIPS)
    positions, counts = jax.vmap(clip_layout)(keys)
    return counts


def draw_patches(key, part):
    key = jax.random.fold_in(key, 3)
    k_base = jax.random.fold_in(key, 0)
    shape = (CLIPS, N_SEQ * CAP, D)
    noise = jnp.clip(jax.random.normal(k_base, shape, jnp.float32), -6.0, 6.0)
    return noise.astype(jnp.bfloat16)


def draw_w_qkv(key, part):
    key = jax.random.fold_in(key, 5)
    k_base = jax.random.fold_in(key, 0)
    width = HEADS * HD
    base = jnp.clip(jax.random.normal(k_base, (3, D, width), jnp.float32), -6.0, 6.0) * D ** (-0.5)
    return base.astype(jnp.bfloat16)


def draw_w_out(key, part):
    key = jax.random.fold_in(key, 11)
    width = HEADS * HD
    base = jnp.clip(jax.random.normal(key, (width, D), jnp.float32), -6.0, 6.0)
    return (base * 12.0 * width ** (-0.5)).astype(jnp.bfloat16)


def level_of(rng, dims, pieces, least, high):
    loudness = 1.0
    for position, shards_of in pieces:
        steps = jax.random.uniform(jax.random.fold_in(jax.random.fold_in(rng, 6), position), (shards_of,), jnp.float32, least / len(pieces), high / len(pieces))
        loudness = loudness * jnp.repeat(jnp.exp(steps), dims[position] // shards_of).reshape((-1,) + (1,) * (len(dims) - 1 - position))
    return loudness


def bell_draw(stream_key, extent, scale, reach, pieces=(), kind=jnp.bfloat16):
    drawn = jax.random.normal(stream_key, extent, jnp.float32) * scale
    if len(pieces) > 0:
        drawn = level_of(stream_key, extent, pieces, -0.22, 0.18) * drawn
    return jnp.clip(drawn, min=-reach, max=reach).astype(kind)


def setup_inputs(seed: int = 0) -> dict:
    splits = jax.random.split(jax.random.key(seed), 13)
    patches = draw_patches(jax.random.fold_in(splits[12], 71), 0)
    keep_pos = draw_keep_pos(jax.random.fold_in(splits[12], 71), 0)
    kept_counts = draw_kept_counts(jax.random.fold_in(splits[12], 71), 0)
    enc_gain = jnp.clip(1.0 + 0.15 * jax.random.normal(splits[3], (D,), jnp.float32), 0.25, 1.75)
    w_qkv = draw_w_qkv(jax.random.fold_in(splits[12], 71), 0)
    w_out = draw_w_out(jax.random.fold_in(splits[12], 71), 0)
    w_e2d = bell_draw(splits[6], (D, DD), D ** -0.5, 0.15625)
    mask_token = bell_draw(splits[7], (DD,), 1.0, 4.0)
    dec_gain = jnp.clip(1.0 + 0.15 * jax.random.normal(splits[8], (DD,), jnp.float32), 0.25, 1.75)
    fc_in = bell_draw(splits[9], (DH, DD), DD ** -0.5, 0.25, ((0, 16),))
    fc_out = bell_draw(splits[10], (DH, DD), DH ** -0.5, 0.125, ((0, 16),))
    cotangent = bell_draw(splits[11], (CLIPS, FULL, DD), 1.0, 6.0, ((0, 32), (1, 16)))
    return {"patches": patches, "keep_pos": keep_pos, "kept_counts": kept_counts, "enc_gain": enc_gain, "w_qkv": w_qkv, "w_out": w_out, "w_e2d": w_e2d, "mask_token": mask_token, "dec_gain": dec_gain, "fc_in": fc_in, "fc_out": fc_out, "cotangent": cotangent}


def layer_norm(values, gain):
    mean = lax.optimization_barrier(jnp.mean(values, axis=-1, keepdims=True))
    centred = values - mean
    var = lax.optimization_barrier(jnp.mean(centred * centred, axis=-1, keepdims=True))
    return centred * lax.rsqrt(var + 1e-06) * gain

def layer_norm_back(values, gain, upstream):
    mean = lax.optimization_barrier(jnp.mean(values, axis=-1, keepdims=True))
    centred = values - mean
    var = lax.optimization_barrier(jnp.mean(centred * centred, axis=-1, keepdims=True))
    inv_std = lax.rsqrt(var + 1e-06)
    normed = centred * inv_std
    scaled = upstream * gain
    first = lax.optimization_barrier(jnp.mean(scaled, axis=-1, keepdims=True))
    second = lax.optimization_barrier(jnp.mean(scaled * normed, axis=-1, keepdims=True))
    return inv_std * (scaled - first - normed * second)

def gelu_slope(h):
    cdf = 0.5 * (1.0 + jax.scipy.special.erf(h * 0.7071067811865476))
    pdf = jnp.exp(-0.5 * h * h) * 0.3989422804014327
    return cdf + h * pdf

def position_table(positions, width):
    half = width // 2
    freq = 10000.0 ** (-(jnp.arange(half, dtype=jnp.float32) * 2.0 / width))
    angle = positions[:, None] * freq[None, :]
    return jnp.concatenate([jnp.sin(angle), jnp.cos(angle)], axis=1)

def reference(patches, keep_pos, kept_counts, enc_gain, w_qkv, w_out, w_e2d, mask_token, dec_gain, fc_in, fc_out, cotangent):
    rows = N_SEQ * CAP
    width = HEADS * HD
    scale = HD ** (-0.5)
    full = F * N_SEQ
    table = position_table(jnp.arange(full, dtype=jnp.float32), DD)

    def one_clip(carry, inputs):
        acc_qkv, acc_out = carry
        clip_x, clip_keep, clip_counts, clip_cot = inputs
        index = jnp.arange(rows)
        live = index % CAP < clip_counts[index // CAP]
        xf = clip_x.astype(jnp.float32)
        xn = layer_norm(xf, enc_gain).astype(jnp.bfloat16)
        query = (jnp.dot(xn, w_qkv[0], preferred_element_type=jnp.float32) * scale).astype(jnp.bfloat16)
        keys = jnp.dot(xn, w_qkv[1], preferred_element_type=jnp.float32).astype(jnp.bfloat16)
        values = jnp.dot(xn, w_qkv[2], preferred_element_type=jnp.float32).astype(jnp.bfloat16)
        q3 = query.reshape(rows, HEADS, HD).astype(jnp.float32)
        k3 = keys.reshape(rows, HEADS, HD).astype(jnp.float32)
        v3 = values.reshape(rows, HEADS, HD).astype(jnp.float32)
        scores = jnp.einsum('qhd,khd->hqk', q3, k3)
        scores = jnp.where(live[None, None, :], scores, -jnp.inf)
        top = lax.optimization_barrier(jnp.max(scores, axis=-1, keepdims=True))
        expo = jnp.exp(scores - top)
        probs = expo / lax.optimization_barrier(jnp.sum(expo, axis=-1, keepdims=True))
        probs_b = probs.astype(jnp.bfloat16)
        ctx = jnp.einsum('hqk,khd->qhd', probs_b.astype(jnp.float32), v3).astype(jnp.bfloat16)
        ctx = ctx.reshape(rows, width)
        groups = N_SEQ
        ctx_g = ctx.reshape(rows, groups, width // groups).astype(jnp.float32)
        out_g = w_out.reshape(groups, width // groups, D).astype(jnp.float32)
        parts = jnp.einsum('rgc,gcd->grd', ctx_g, out_g).astype(jnp.bfloat16)
        enc = xf + lax.optimization_barrier(jnp.sum(parts.astype(jnp.float32), axis=0))
        vis = jnp.dot(enc.astype(jnp.bfloat16), w_e2d, preferred_element_type=jnp.float32).astype(jnp.bfloat16)
        target = jnp.where(live, clip_keep, full).astype(jnp.int32)
        dec_vis = jnp.zeros((full, DD), jnp.float32).at[target].set(vis.astype(jnp.float32), mode='drop')
        seen = jnp.zeros((full,), jnp.float32).at[target].set(1.0, mode='drop')
        dec_x = jnp.where(seen[:, None] > 0.5, dec_vis, mask_token.astype(jnp.float32)[None, :]) + table
        dn = layer_norm(dec_x, dec_gain).astype(jnp.bfloat16)
        hidden = jnp.dot(dn, fc_in.T, preferred_element_type=jnp.float32)
        act = jax.nn.gelu(hidden, approximate=False).astype(jnp.bfloat16)
        recon = (dec_x + jnp.dot(act, fc_out, preferred_element_type=jnp.float32)).astype(jnp.bfloat16)
        dact = jnp.dot(clip_cot, fc_out.T, preferred_element_type=jnp.float32)
        dhidden = (dact * gelu_slope(hidden)).astype(jnp.bfloat16)
        ddn = jnp.dot(dhidden, fc_in, preferred_element_type=jnp.float32)
        ddec = clip_cot.astype(jnp.float32) + layer_norm_back(dec_x, dec_gain, ddn)
        ddec_b = ddec.astype(jnp.bfloat16)
        picked = ddec_b[jnp.clip(clip_keep, 0, full - 1).astype(jnp.int32)]
        dvis = jnp.where(live[:, None], picked, jnp.zeros_like(picked))
        denc = jnp.dot(dvis, w_e2d.T, preferred_element_type=jnp.float32)
        dy = jnp.where(live[:, None], denc, 0.0).astype(jnp.bfloat16)
        dctx = jnp.dot(dy, w_out.T, preferred_element_type=jnp.float32).astype(jnp.bfloat16)
        grad_o = jnp.dot(ctx.T, dy, preferred_element_type=jnp.float32)
        dc3 = dctx.reshape(rows, HEADS, HD).astype(jnp.float32)
        dprob = jnp.einsum('qhd,khd->hqk', dc3, v3)
        inner = lax.optimization_barrier(jnp.sum(probs * dprob, axis=-1, keepdims=True))
        dscore = (probs * (dprob - inner)).astype(jnp.bfloat16).astype(jnp.float32)
        dq = (jnp.einsum('hqk,khd->qhd', dscore, k3) * scale).astype(jnp.bfloat16)
        dk = jnp.einsum('hqk,qhd->khd', dscore, q3).astype(jnp.bfloat16)
        dv = jnp.einsum('hqk,qhd->khd', probs_b.astype(jnp.float32), dc3).astype(jnp.bfloat16)
        grad_q = jnp.stack([jnp.dot(xn.T, term.reshape(rows, width), preferred_element_type=jnp.float32) for term in (dq, dk, dv)])
        return ((acc_qkv + grad_q, acc_out + grad_o), recon)
    start = (jnp.zeros((3, D, width), jnp.float32), jnp.zeros((width, D), jnp.float32))
    totals, recon = lax.scan(one_clip, start, (patches, keep_pos, kept_counts, cotangent))
    return (recon, totals[0].astype(jnp.bfloat16), totals[1].astype(jnp.bfloat16))
```

```python
import jax
import jax.numpy as jnp
from jax import lax
from jax.experimental import pallas as pl
from jax.experimental.pallas import tpu as pltpu
from jax.sharding import PartitionSpec as P

HD = 88
HP = 96
DD = 512
NZ = 8
NX = 4
NY = 8
CAP = 48
ROWS = 768
SLOTS = 3
HID = 128
FDEV = 256
DEAD = 1024.0
GRAD_ROWS = 3328
SCALE = HD ** (-0.5)
F32 = jnp.float32
BF16 = jnp.bfloat16


def dot(a, b):
    return jnp.dot(a, b, preferred_element_type=F32)


def dot_nt(a, b):
    return lax.dot_general(a, b, (((1,), (1,)), ((), ())), preferred_element_type=F32)


def layer_norm(values, gain):
    mean = jnp.mean(values, axis=-1, keepdims=True)
    centred = values - mean
    var = jnp.mean(centred * centred, axis=-1, keepdims=True)
    return centred * lax.rsqrt(var + 1e-06) * gain


def call(body, outs, scratch, cost, grant, *args):
    return pl.pallas_call(
        body,
        out_shape=[jax.ShapeDtypeStruct(shape, dtype) for shape, dtype in outs],
        in_specs=[pl.BlockSpec(memory_space=pltpu.VMEM)] * len(args),
        out_specs=[pl.BlockSpec(memory_space=pltpu.VMEM)] * len(outs),
        scratch_shapes=scratch,
        compiler_params=pltpu.CompilerParams(vmem_limit_bytes=grant << 20),
        cost_estimate=pl.CostEstimate(flops=cost, bytes_accessed=8 << 20, transcendentals=1 << 20),
    )(*args)


def prep_body(keep, patches, gain, xn, x_slot, offsets):
    at_row = lax.broadcasted_iota(jnp.int32, (CAP, CAP), 0)
    at_col = lax.broadcasted_iota(jnp.int32, (CAP, CAP), 1)
    own = jnp.broadcast_to(keep[...], (CAP, CAP))
    owner = lax.shift_right_arithmetic(own, 8)
    owner_col = jnp.sum(jnp.where(at_row == at_col, owner, 0), axis=1, keepdims=True)
    same = (owner_col == owner) & (at_row < at_col)
    rank = jnp.sum(same.astype(jnp.int32), axis=0, keepdims=True)
    slot = jnp.where(own >= 0, owner * SLOTS + rank, -1)
    pick = at_row == slot
    live = jnp.sum(pick.astype(F32), axis=1, keepdims=True) > 0.5
    spot = jnp.sum(jnp.where(pick, own - owner * FDEV, 0).astype(F32), axis=1, keepdims=True)
    rows = dot(pick.astype(F32).astype(BF16), patches[...])
    x_slot[...] = rows.astype(BF16)
    lane = lax.broadcasted_iota(jnp.int32, rows.shape, 1)
    dead_row = jnp.where(lane == 0, DEAD, 0.0)
    xn[...] = jnp.where(live, layer_norm(rows, gain[...]), dead_row).astype(BF16)
    offsets[...] = jnp.broadcast_to(jnp.where(live, spot, -1.0), (CAP, 128)).astype(BF16)


def prep(keep, patches, gain):
    return call(
        prep_body, [((CAP, patches.shape[1]), BF16), ((CAP, patches.shape[1]), BF16), ((CAP, 128), BF16)],
        [], 1 << 20, 8, keep, patches, gain)


def join_body(*refs):
    blocks, out, sems = refs[:NZ], refs[NZ], refs[NZ + 1]
    copies = [pltpu.make_async_copy(blocks[k], out.at[pl.ds(CAP * k, CAP)], sems.at[k]) for k in range(NZ)]
    for copy in copies:
        copy.start()
    for copy in copies:
        copy.wait()


def join(blocks):
    rows, width = blocks[0].shape
    return pl.pallas_call(
        join_body,
        out_shape=jax.ShapeDtypeStruct((NZ * rows, width), blocks[0].dtype),
        in_specs=[pl.BlockSpec(memory_space=pl.ANY)] * NZ,
        out_specs=pl.BlockSpec(memory_space=pl.ANY),
        scratch_shapes=[pltpu.SemaphoreType.DMA((NZ,))],
        compiler_params=pltpu.CompilerParams(vmem_limit_bytes=4 << 20),
        cost_estimate=pl.CostEstimate(flops=0, bytes_accessed=4 << 20, transcendentals=0),
    )(*blocks)


def attend_body(mine, other, w_t, swap, extra, sent, q_out, k_out, kt_out, v_out, stats, live_out, ctx_out):
    def heads(x):
        qkv = dot_nt(w_t[...], x[...])
        pad = jnp.zeros((HP - HD, qkv.shape[1]), F32)
        return [jnp.concatenate([qkv[i * HD:(i + 1) * HD], pad], axis=0) for i in range(3)]

    q, k, v = [jnp.concatenate(pair, axis=1) for pair in zip(heads(mine), heads(other))]
    q = (q * SCALE).astype(BF16)
    vt = v.astype(BF16)
    k_rows = k.T.astype(BF16)
    live = jnp.concatenate([mine[:, 0:128], other[:, 0:128]], axis=0).astype(F32)[:, 0:1] < 0.5 * DEAD
    q_out[...] = q
    k_out[...] = k_rows
    kt_out[...] = k.astype(BF16)
    v_out[...] = v.T.astype(BF16)
    live_out[...] = jnp.where(live, 0.0, -jnp.inf).astype(F32)
    ctx = []
    for i in range(3):
        cols = slice(256 * i, 256 * (i + 1))
        scores = jnp.where(live, dot(k_rows, q[:, cols]), -jnp.inf)
        top = jnp.max(scores, axis=0, keepdims=True)
        expo = jnp.exp(scores - top)
        total = jnp.sum(expo, axis=0, keepdims=True)
        stats[0:1, cols] = top
        stats[1:2, cols] = total
        ctx.append(dot(vt, (expo / total).astype(BF16)))
    ctx = jnp.concatenate(ctx, axis=1)
    ctx = jnp.concatenate([ctx, jnp.zeros((128 - HP, ROWS), F32)], axis=0).astype(BF16)
    sent[:, 0:CAP, :] = dot_nt(swap[...], ctx).astype(BF16).reshape(16, CAP, 128)
    sent[:, CAP:, :] = extra[...]
    ctx_out[...] = dot_nt(ctx, swap[...])[0:HP].astype(BF16)


def attend(mine, other, w_t, swap, extra):
    return call(
        attend_body,
        [((16, 64, 128), BF16), ((HP, ROWS), BF16), ((ROWS, HP), BF16), ((HP, ROWS), BF16), ((ROWS, HP), BF16),
         ((8, ROWS), F32), ((ROWS, 1), F32), ((HP, ROWS), BF16)],
        [], 1700 << 20, 20, mine, other, w_t, swap, extra)


def decode_body(came, weights, mask, gain, cot, table, recon, dvis, mixed, grad):
    flat = came[...].reshape(16 * 64, 128)
    vis = jnp.zeros((CAP, DD), F32)
    for g in range(16):
        vis += dot(came[g, 0:CAP, 0:HP], weights[g, 2 * HID:2 * HID + HP, :])
    row = lax.broadcasted_iota(jnp.int32, (CAP, 1024), 0)
    col = lax.broadcasted_iota(jnp.int32, (CAP, 1024), 1)
    source = jnp.zeros((CAP, 1024), jnp.int32)
    for g in range(1, 16):
        source += (row >= SLOTS * g).astype(jnp.int32)
    slot = row - SLOTS * source
    base = 64 * source + CAP
    x_part = jnp.concatenate(
        [dot((col == base + 4 * slot + i).astype(F32).astype(BF16), flat) for i in range(4)], axis=1)
    vis = (vis + x_part).astype(BF16)
    spots = dot((col == base + 12).astype(F32).astype(BF16), flat)
    lane = lax.broadcasted_iota(jnp.int32, (CAP, 128), 1)
    spot = jnp.sum(jnp.where(lane == slot[:, 0:128], spots, 0.0), axis=1, keepdims=True)
    spot = jnp.concatenate([spot, jnp.full((128 - CAP, 1), -1.0, F32)], axis=0)
    vis = jnp.concatenate([vis.astype(F32), jnp.zeros((128 - CAP, DD), F32)], axis=0).astype(BF16)
    where_col = lax.broadcasted_iota(jnp.int32, (128, FDEV), 1).astype(F32)
    picker = (spot == where_col).astype(F32)
    placer = picker.T
    seen = jnp.sum(placer, axis=1, keepdims=True)
    dec_vis = dot(placer.astype(BF16), vis)
    dec_x = jnp.where(seen > 0.5, dec_vis, mask[...].astype(F32)) + table[...]
    mean = jnp.mean(dec_x, axis=-1, keepdims=True)
    centred = dec_x - mean
    var = jnp.mean(centred * centred, axis=-1, keepdims=True)
    inv_std = lax.rsqrt(var + 1e-06)
    normed = centred * inv_std
    dn = (normed * gain[...]).astype(BF16)
    cot_b = cot[...]
    mixed[...] = dec_x
    for i in range(8):
        fin = jnp.concatenate([weights[2 * i, 0:HID, :], weights[2 * i + 1, 0:HID, :]], axis=0)
        fout = jnp.concatenate([weights[2 * i, HID:2 * HID, :], weights[2 * i + 1, HID:2 * HID, :]], axis=0)
        hidden = dot_nt(dn, fin)
        dact = dot_nt(cot_b, fout)
        cdf = 0.5 * (1.0 + lax.erf(hidden * 0.7071067811865476))
        pdf = jnp.exp(-0.5 * hidden * hidden) * 0.3989422804014327
        act = (hidden * cdf).astype(BF16)
        dhidden = (dact * (cdf + hidden * pdf)).astype(BF16)
        mixed[...] += dot(act, fout)
        if i == 0:
            grad[...] = dot(dhidden, fin)
        else:
            grad[...] += dot(dhidden, fin)
    recon[...] = mixed[...].astype(BF16)
    scaled = grad[...] * gain[...]
    first = jnp.mean(scaled, axis=-1, keepdims=True)
    second = jnp.mean(scaled * normed, axis=-1, keepdims=True)
    ddec = (cot_b.astype(F32) + inv_std * (scaled - first - normed * second)).astype(BF16)
    dvis[...] = dot(picker[0:CAP].astype(BF16), ddec).astype(BF16)


def decode(came, weights, mask, gain, cot, table):
    return call(
        decode_body, [((FDEV, DD), BF16), ((CAP, DD), BF16)],
        [pltpu.VMEM((FDEV, DD), F32), pltpu.VMEM((FDEV, DD), F32)], 2300 << 20, 20,
        came, weights, mask, gain, cot, table)


def back_body(dvis, w_oe, swap, q, k, kt, v, stats, dead, ctx, mine, other, parts, ds_all, pb_all):
    dctx = dot(dot_nt(w_oe[...], dvis[...]).astype(BF16), swap[...]).astype(BF16)
    grad_oe = dot(ctx[...], dvis[...])[0:HD]
    dq = []
    for i in range(3):
        cols = slice(256 * i, 256 * (i + 1))
        scores = dot(k[...], q[:, cols]) + dead[...]
        probs = jnp.exp(scores - stats[0:1, cols]) / stats[1:2, cols]
        dprob = dot(v[...], dctx[:, cols])
        inner = jnp.sum(probs * dprob, axis=0, keepdims=True)
        ds = (probs * (dprob - inner)).astype(BF16)
        ds_all[:, cols] = ds
        pb_all[:, cols] = probs.astype(BF16)
        dq.append(dot(kt[...], ds) * SCALE)
    dq = jnp.concatenate(dq, axis=1)[0:HD]
    dk = dot_nt(q[...], ds_all[...])[0:HD]
    dv = dot_nt(dctx, pb_all[...])[0:HD]
    dqkv = jnp.concatenate([dq, dk, dv], axis=0).astype(BF16)
    grad = dot(dqkv[:, 0:ROWS // 2], mine[...]) + dot(dqkv[:, ROWS // 2:], other[...])
    wide = grad.shape[1] // 128
    pieces = [grad[:, 128 * j:128 * (j + 1)] for j in range(wide)]
    pieces += [grad_oe[:, 128 * j:128 * (j + 1)] for j in range(DD // 128)]
    done = sum(p.shape[0] for p in pieces)
    pieces.append(jnp.zeros((GRAD_ROWS - done, 128), F32))
    parts[...] = jnp.concatenate(pieces, axis=0).astype(BF16)


def back(*args):
    return call(
        back_body, [((GRAD_ROWS, 128), BF16)],
        [pltpu.VMEM((ROWS, ROWS), BF16), pltpu.VMEM((ROWS, ROWS), BF16)], 2500 << 20, 20, *args)[0]


def position_table(positions, width):
    half = width // 2
    freq = 10000.0 ** (-(jnp.arange(half, dtype=F32) * 2.0 / width))
    angle = positions[:, None] * freq[None, :]
    return jnp.concatenate([jnp.sin(angle), jnp.cos(angle)], axis=1)


Z_GROUPS = [[2 * z + c for z in range(NZ)] for c in range(2)]
X_GROUPS = [[NX * y + x for x in range(NX)] for y in range(NY)]
Y_GROUPS = [[NX * y + x for y in range(NY)] for x in range(NX)]


def exchange(block, axis, groups):
    return lax.all_to_all(block, axis, 0, 0, axis_index_groups=groups, tiled=True)


def spread(block, axis, groups):
    count = len(groups[0])
    copies = jnp.broadcast_to(block[None], (count,) + block.shape)
    return exchange(copies, axis, groups)


def z_shift(block, step):
    return lax.ppermute(block, "seq", [(s, (s + 2 * step) % 16) for s in range(16)])


def ring(block):
    got = {0: block, 8: block}
    for step in range(1, 5):
        got[step] = z_shift(got[step - 1], 1)
        if step < 4:
            got[8 - step] = z_shift(got[9 - step], -1)
    return [got[k] for k in range(NZ)]


def swap_core(block):
    return lax.ppermute(block, "seq", [(s, s ^ 1) for s in range(16)])


def local(
    patches,
    keep_pos,
    kept_counts,
    enc_gain,
    w_qkv,
    w_out,
    w_e2d,
    mask_token,
    dec_gain,
    fc_in,
    fc_out,
    cotangent,
):
    me = lax.axis_index("seq")
    my_c = me % 2
    fdev = cotangent.shape[1]
    my_z = me // 2
    cot = cotangent[0]
    cap = keep_pos.shape[1]
    rows = 16 * cap

    xn_own, x_slot, offsets = prep(keep_pos, patches[0], enc_gain[None])
    mine = join(ring(xn_own))
    other = swap_core(mine)

    x_vis = dot(x_slot, w_e2d).astype(BF16)
    places = jnp.pad(offsets[:, 0].reshape(16, 1, SLOTS), ((0, 0), (0, 0), (0, 128 - SLOTS)))
    extra = jnp.concatenate(
        [x_vis.reshape(16, 12, 128), places, jnp.zeros((16, 3, 128), BF16)], axis=1)

    w_oe_own = jnp.pad(dot(w_out, w_e2d).astype(BF16), ((0, HP - HD), (0, 0)))
    weights = lax.all_gather(jnp.concatenate([fc_in, fc_out, w_oe_own], axis=0), "seq", axis=0)

    tok = jnp.arange(rows, dtype=jnp.int32)
    block = tok // cap
    source = (my_z - block % NZ) % NZ * 2 + (my_c ^ (block // NZ))
    inside = tok % cap
    dest = inside // SLOTS * cap + source * SLOTS + inside % SLOTS
    swap = (dest[None, :] == tok[:, None]).astype(BF16)
    table = position_table((me * fdev + jnp.arange(fdev, dtype=jnp.int32)).astype(F32), DD)

    w_t = w_qkv.transpose(0, 2, 1).reshape(3 * HD, -1)
    sent, q, k, k_t, v, stats, dead, ctx = attend(mine, other, w_t, swap, extra)
    came = lax.all_to_all(sent, "seq", 0, 0, tiled=True)
    recon, dvis_own = decode(came, weights, mask_token[None], dec_gain[None], cot, table)
    dvis = lax.all_gather(dvis_own, "seq", axis=0, tiled=True)
    parts = back(dvis, w_oe_own, swap, q, k, k_t, v, stats, dead, ctx, mine, other)

    parts = jnp.sum(exchange(parts.reshape(NX, 832, 128), "dp", X_GROUPS).astype(F32), axis=0).astype(BF16)
    parts = jnp.sum(exchange(parts.reshape(NY, 104, 128), "dp", Y_GROUPS).astype(F32), axis=0).astype(BF16)
    parts = spread(parts, "dp", Y_GROUPS).reshape(832, 128)
    total = spread(parts, "dp", X_GROUPS).reshape(GRAD_ROWS, 128)
    wide = w_qkv.shape[1] // 128
    cut = 3 * HD * wide
    grad_q = total[:cut].reshape(wide, 3 * HD, 128).transpose(1, 0, 2).reshape(3, HD, wide * 128).transpose(0, 2, 1)
    grad_oe = total[cut:cut + 4 * HD].reshape(4, HD, 128).transpose(1, 0, 2).reshape(HD, DD)
    grad_o = dot_nt(grad_oe, w_e2d).astype(BF16)
    return (recon[None], grad_q, grad_o)


def solution(mesh):
    placed = (
        P("dp", "seq", None),
        P("dp", "seq"),
        P("dp", None),
        P(),
        P(None, None, "seq"),
        P("seq", None),
        P(),
        P(),
        P(),
        P("seq", None),
        P("seq", None),
        P("dp", "seq", None),
    )
    return jax.shard_map(
        local,
        mesh=mesh,
        in_specs=placed,
        out_specs=(P("dp", "seq", None), P(None, None, "seq"), P("seq", None)),
        check_vma=False,
    )
```

```python
import jax
import jax.numpy as jnp
from jax import lax
from jax.experimental import pallas as pl
from jax.experimental.pallas import tpu as pltpu
from jax.sharding import PartitionSpec as P

HD = 88
HP = 96
HL = 128
DD = 512
NZ = 8
NX = 4
NY = 8
CAP = 48
ROWS = 768
SLOTS = 3
HID = 128
FDEV = 256
DEAD = 1024.0
GRAD_ROWS = 3328
SCALE = HD ** (-0.5)
F32 = jnp.float32
BF16 = jnp.bfloat16


def dot(a, b):
    return jnp.dot(a, b, preferred_element_type=F32)


def dot_nt(a, b):
    return lax.dot_general(a, b, (((1,), (1,)), ((), ())), preferred_element_type=F32)


def layer_norm(values, gain):
    mean = jnp.mean(values, axis=-1, keepdims=True)
    centred = values - mean
    var = jnp.mean(centred * centred, axis=-1, keepdims=True)
    return centred * lax.rsqrt(var + 1e-06) * gain


def call(body, outs, scratch, cost, grant, *args):
    return pl.pallas_call(
        body,
        out_shape=[jax.ShapeDtypeStruct(shape, dtype) for shape, dtype in outs],
        in_specs=[pl.BlockSpec(memory_space=pltpu.VMEM)] * len(args),
        out_specs=[pl.BlockSpec(memory_space=pltpu.VMEM)] * len(outs),
        scratch_shapes=scratch,
        compiler_params=pltpu.CompilerParams(vmem_limit_bytes=grant << 20),
        cost_estimate=pl.CostEstimate(flops=cost, bytes_accessed=8 << 20, transcendentals=1 << 20),
    )(*args)


def prep_body(keep, patches, gain, xn, x_slot, offsets):
    at_row = lax.broadcasted_iota(jnp.int32, (CAP, CAP), 0)
    at_col = lax.broadcasted_iota(jnp.int32, (CAP, CAP), 1)
    own = jnp.broadcast_to(keep[...], (CAP, CAP))
    owner = lax.shift_right_arithmetic(own, 8)
    owner_col = jnp.sum(jnp.where(at_row == at_col, owner, 0), axis=1, keepdims=True)
    same = (owner_col == owner) & (at_row < at_col)
    rank = jnp.sum(same.astype(jnp.int32), axis=0, keepdims=True)
    slot = jnp.where(own >= 0, owner * SLOTS + rank, -1)
    pick = at_row == slot
    live = jnp.sum(pick.astype(F32), axis=1, keepdims=True) > 0.5
    spot = jnp.sum(jnp.where(pick, own - owner * FDEV, 0).astype(F32), axis=1, keepdims=True)
    rows = dot(pick.astype(F32).astype(BF16), patches[...])
    x_slot[...] = rows.astype(BF16)
    lane = lax.broadcasted_iota(jnp.int32, rows.shape, 1)
    dead_row = jnp.where(lane == 0, DEAD, 0.0)
    xn[...] = jnp.where(live, layer_norm(rows, gain[...]), dead_row).astype(BF16)
    offsets[...] = jnp.broadcast_to(jnp.where(live, spot, -1.0), (CAP, 128)).astype(BF16)


def prep(keep, patches, gain):
    width = patches.shape[1]
    return call(
        prep_body, [((CAP, width), BF16), ((CAP, width), BF16), ((CAP, 128), BF16)],
        [], 1 << 20, 8, keep, patches, gain)


def join_body(*refs):
    blocks, out, sems = refs[:NZ], refs[NZ], refs[NZ + 1]
    copies = [pltpu.make_async_copy(blocks[k], out.at[pl.ds(CAP * k, CAP)], sems.at[k]) for k in range(NZ)]
    for copy in copies:
        copy.start()
    for copy in copies:
        copy.wait()


def join(blocks):
    rows, width = blocks[0].shape
    return pl.pallas_call(
        join_body,
        out_shape=jax.ShapeDtypeStruct((NZ * rows, width), blocks[0].dtype),
        in_specs=[pl.BlockSpec(memory_space=pl.ANY)] * NZ,
        out_specs=pl.BlockSpec(memory_space=pl.ANY),
        scratch_shapes=[pltpu.SemaphoreType.DMA((NZ,))],
        compiler_params=pltpu.CompilerParams(vmem_limit_bytes=4 << 20),
        cost_estimate=pl.CostEstimate(flops=0, bytes_accessed=4 << 20, transcendentals=0),
    )(*blocks)


def attend_body(mine, other, w, swap, extra, sent, saved, stats, xs, out, keep, keep_stats, sems):
    half = ROWS // 2
    loads = [
        pltpu.make_async_copy(mine, xs.at[pl.ds(0, half)], sems.at[0]),
        pltpu.make_async_copy(other, xs.at[pl.ds(half, half)], sems.at[1])]
    for load in loads:
        load.start()
    parts = []
    for i in range(2):
        loads[i].wait()
        parts.append(dot_nt(xs[half * i:half * (i + 1), :], w[...]))
    qkv = jnp.concatenate(parts, axis=0)
    k_rows = qkv[:, HL:2 * HL].astype(BF16)
    q = (qkv[:, 0:HL] * SCALE).T.astype(BF16)
    vt = qkv[:, 2 * HL:].T.astype(BF16)
    keep[0:HL, :] = q
    keep[HL:2 * HL, :] = qkv[:, HL:2 * HL].T.astype(BF16)
    keep[2 * HL:3 * HL, :] = vt
    heads = pltpu.make_async_copy(keep.at[pl.ds(0, 3 * HL)], saved.at[pl.ds(0, 3 * HL)], sems.at[2])
    heads.start()
    dead = jnp.where(xs[:, 0:128].astype(F32)[:, 0:1] < 0.5 * DEAD, 0.0, -jnp.inf)
    ctx = []
    for i in range(3):
        cols = slice(256 * i, 256 * (i + 1))
        scores = dot(k_rows, q[:, cols]) + dead
        top = jnp.max(scores, axis=0, keepdims=True)
        expo = jnp.exp(scores - top)
        total = jnp.sum(expo, axis=0, keepdims=True)
        keep_stats[0:1, cols] = top
        keep_stats[1:2, cols] = total
        ctx.append(dot(vt, (expo / total).astype(BF16)))
    sums = pltpu.make_async_copy(keep_stats, stats, sems.at[3])
    sums.start()
    ctx = jnp.concatenate(ctx, axis=1).astype(BF16)
    out[:, 0:CAP, :] = dot_nt(swap[...], ctx).astype(BF16).reshape(16, CAP, 128)
    out[:, CAP:, :] = extra[...]
    send = pltpu.make_async_copy(out, sent, sems.at[4])
    send.start()
    keep[3 * HL:, :] = dot_nt(ctx, swap[...]).astype(BF16)
    last = pltpu.make_async_copy(keep.at[pl.ds(3 * HL, HL)], saved.at[pl.ds(3 * HL, HL)], sems.at[5])
    last.start()
    for copy in (heads, sums, send, last):
        copy.wait()


def attend(*args):
    vmem = pl.BlockSpec(memory_space=pltpu.VMEM)
    hbm = pl.BlockSpec(memory_space=pltpu.HBM)
    return pl.pallas_call(
        attend_body,
        out_shape=[pltpu.HBM((16, 64, 128), BF16), pltpu.HBM((4 * HL, ROWS), BF16), pltpu.HBM((8, ROWS), F32)],
        in_specs=[hbm, hbm, vmem, vmem, vmem],
        out_specs=[hbm, hbm, hbm],
        scratch_shapes=[pltpu.VMEM((ROWS, args[0].shape[1]), BF16), pltpu.VMEM((16, 64, 128), BF16),
                        pltpu.VMEM((4 * HL, ROWS), BF16), pltpu.VMEM((8, ROWS), F32), pltpu.SemaphoreType.DMA((6,))],
        compiler_params=pltpu.CompilerParams(vmem_limit_bytes=24 << 20),
        cost_estimate=pl.CostEstimate(flops=1700 << 20, bytes_accessed=8 << 20, transcendentals=1 << 20),
    )(*args)


def decode_body(came, weights, cot, mask, gain, table, recon, dvis, mixed, grad, w_oe, w_fc, cots, sems):
    loads = [
        pltpu.make_async_copy(
            weights.at[pl.ds(2 * i, 2), pl.ds(0, 2 * HID)], w_fc.at[pl.ds(2 * i, 2)], sems.at[i])
        for i in range(8)]
    oe = pltpu.make_async_copy(weights.at[:, pl.ds(2 * HID, HP)], w_oe, sems.at[8])
    up = pltpu.make_async_copy(cot, cots, sems.at[9])
    for load in (oe, up, loads[0]):
        load.start()
    flat = came[...].reshape(16 * 64, 128)
    vis = jnp.zeros((CAP, DD), F32)
    oe.wait()
    for load in loads[1:]:
        load.start()
    for g in range(16):
        vis += dot(came[g, 0:CAP, 0:HP], w_oe[g])
    row = lax.broadcasted_iota(jnp.int32, (CAP, 1024), 0)
    col = lax.broadcasted_iota(jnp.int32, (CAP, 1024), 1)
    source = jnp.zeros((CAP, 1024), jnp.int32)
    for g in range(1, 16):
        source += (row >= SLOTS * g).astype(jnp.int32)
    slot = row - SLOTS * source
    base = 64 * source + CAP
    x_part = jnp.concatenate(
        [dot((col == base + 4 * slot + i).astype(F32).astype(BF16), flat) for i in range(4)], axis=1)
    vis = (vis + x_part).astype(BF16)
    spots = dot((col == base + 12).astype(F32).astype(BF16), flat)
    lane = lax.broadcasted_iota(jnp.int32, (CAP, 128), 1)
    spot = jnp.sum(jnp.where(lane == slot[:, 0:128], spots, 0.0), axis=1, keepdims=True)
    spot = jnp.concatenate([spot, jnp.full((128 - CAP, 1), -1.0, F32)], axis=0)
    vis = jnp.concatenate([vis.astype(F32), jnp.zeros((128 - CAP, DD), F32)], axis=0).astype(BF16)
    where_col = lax.broadcasted_iota(jnp.int32, (128, FDEV), 1).astype(F32)
    picker = (spot == where_col).astype(F32)
    placer = picker.T
    seen = jnp.sum(placer, axis=1, keepdims=True)
    dec_vis = dot(placer.astype(BF16), vis)
    dec_x = jnp.where(seen > 0.5, dec_vis, mask[...].astype(F32)) + table[...]
    mean = jnp.mean(dec_x, axis=-1, keepdims=True)
    centred = dec_x - mean
    var = jnp.mean(centred * centred, axis=-1, keepdims=True)
    inv_std = lax.rsqrt(var + 1e-06)
    normed = centred * inv_std
    dn = (normed * gain[...]).astype(BF16)
    up.wait()
    cot_b = cots[...]
    mixed[...] = dec_x
    for i in range(8):
        loads[i].wait()
        fin = jnp.concatenate([w_fc[2 * i, 0:HID, :], w_fc[2 * i + 1, 0:HID, :]], axis=0)
        fout = jnp.concatenate([w_fc[2 * i, HID:2 * HID, :], w_fc[2 * i + 1, HID:2 * HID, :]], axis=0)
        hidden = dot_nt(dn, fin)
        dact = dot_nt(cot_b, fout)
        cdf = 0.5 * (1.0 + lax.erf(hidden * 0.7071067811865476))
        pdf = jnp.exp(-0.5 * hidden * hidden) * 0.3989422804014327
        act = (hidden * cdf).astype(BF16)
        dhidden = (dact * (cdf + hidden * pdf)).astype(BF16)
        mixed[...] += dot(act, fout)
        if i == 0:
            grad[...] = dot(dhidden, fin)
        else:
            grad[...] += dot(dhidden, fin)
    recon[...] = mixed[...].astype(BF16)
    scaled = grad[...] * gain[...]
    first = jnp.mean(scaled, axis=-1, keepdims=True)
    second = jnp.mean(scaled * normed, axis=-1, keepdims=True)
    ddec = (cot_b.astype(F32) + inv_std * (scaled - first - normed * second)).astype(BF16)
    dvis[...] = dot(picker[0:CAP].astype(BF16), ddec).astype(BF16)


def decode(came, weights, cot, *args):
    vmem = pl.BlockSpec(memory_space=pltpu.VMEM)
    hbm = pl.BlockSpec(memory_space=pltpu.HBM)
    return pl.pallas_call(
        decode_body,
        out_shape=[jax.ShapeDtypeStruct((FDEV, DD), BF16), jax.ShapeDtypeStruct((CAP, DD), BF16)],
        in_specs=[vmem, hbm, hbm] + [vmem] * len(args),
        out_specs=[vmem, vmem],
        scratch_shapes=[pltpu.VMEM((FDEV, DD), F32), pltpu.VMEM((FDEV, DD), F32),
                        pltpu.VMEM((16, HP, DD), BF16), pltpu.VMEM((16, 2 * HID, DD), BF16),
                        pltpu.VMEM((FDEV, DD), BF16), pltpu.SemaphoreType.DMA((10,))],
        compiler_params=pltpu.CompilerParams(vmem_limit_bytes=24 << 20),
        cost_estimate=pl.CostEstimate(flops=2300 << 20, bytes_accessed=8 << 20, transcendentals=1 << 20),
    )(came, pltpu.with_memory_space_constraint(weights, pltpu.HBM),
      pltpu.with_memory_space_constraint(cot, pltpu.HBM), *args)


def back_body(dvis, w_oe, swap, saved, stats, mine, other, parts, ds_all, pb_all, keep, keep_stats, xs, sems):
    loads = [
        pltpu.make_async_copy(saved, keep, sems.at[0]),
        pltpu.make_async_copy(stats, keep_stats, sems.at[1]),
        pltpu.make_async_copy(mine, xs.at[pl.ds(0, ROWS // 2)], sems.at[2]),
        pltpu.make_async_copy(other, xs.at[pl.ds(ROWS // 2, ROWS // 2)], sems.at[3])]
    for load in loads:
        load.start()
    dctx = dot(dot_nt(w_oe[...], dvis[...]).astype(BF16), swap[...])
    dctx = jnp.concatenate([dctx, jnp.zeros((HL - HP, ROWS), F32)], axis=0).astype(BF16)
    for load in loads:
        load.wait()
    x = xs[...]
    grad_oe = dot(keep[3 * HL:, :], dvis[...])[0:HD]
    q, kt = keep[0:HL, :], keep[HL:2 * HL, :]
    k = kt.astype(F32).T.astype(BF16)
    v = keep[2 * HL:3 * HL, :].astype(F32).T.astype(BF16)
    dead = jnp.where(x[:, 0:128].astype(F32)[:, 0:1] < 0.5 * DEAD, 0.0, -jnp.inf)
    dq = []
    for i in range(3):
        cols = slice(256 * i, 256 * (i + 1))
        scores = dot(k, q[:, cols]) + dead
        probs = jnp.exp(scores - keep_stats[0:1, cols]) / keep_stats[1:2, cols]
        dprob = dot(v, dctx[:, cols])
        inner = jnp.sum(probs * dprob, axis=0, keepdims=True)
        ds = (probs * (dprob - inner)).astype(BF16)
        ds_all[:, cols] = ds
        pb_all[:, cols] = probs.astype(BF16)
        dq.append(dot(kt, ds) * SCALE)
    dq = jnp.concatenate(dq, axis=1)[0:HD]
    dk = dot_nt(q, ds_all[...])[0:HD]
    dv = dot_nt(dctx, pb_all[...])[0:HD]
    dqkv = jnp.concatenate([dq, dk, dv], axis=0).astype(BF16)
    grad = dot(dqkv, x)
    wide = grad.shape[1] // 128
    pieces = [grad[:, 128 * j:128 * (j + 1)] for j in range(wide)]
    pieces += [grad_oe[:, 128 * j:128 * (j + 1)] for j in range(DD // 128)]
    done = sum(p.shape[0] for p in pieces)
    pieces.append(jnp.zeros((GRAD_ROWS - done, 128), F32))
    parts[...] = jnp.concatenate(pieces, axis=0).astype(BF16)


def back(dvis, w_oe, swap, saved, stats, mine, other):
    vmem = pl.BlockSpec(memory_space=pltpu.VMEM)
    hbm = pl.BlockSpec(memory_space=pltpu.HBM)
    return pl.pallas_call(
        back_body,
        out_shape=jax.ShapeDtypeStruct((GRAD_ROWS, 128), BF16),
        in_specs=[vmem, vmem, vmem, hbm, hbm, hbm, hbm],
        out_specs=vmem,
        scratch_shapes=[pltpu.VMEM((ROWS, ROWS), BF16), pltpu.VMEM((ROWS, ROWS), BF16),
                        pltpu.VMEM((4 * HL, ROWS), BF16), pltpu.VMEM((8, ROWS), F32),
                        pltpu.VMEM((ROWS, mine.shape[1]), BF16), pltpu.SemaphoreType.DMA((4,))],
        compiler_params=pltpu.CompilerParams(vmem_limit_bytes=24 << 20),
        cost_estimate=pl.CostEstimate(flops=2500 << 20, bytes_accessed=8 << 20, transcendentals=1 << 20),
    )(dvis, w_oe, swap, saved, stats, mine, other)


def finish_body(total, w_e2d, grad_q, grad_o):
    rows = total[...].astype(F32)
    wide = grad_q.shape[1] // 128
    tall = 3 * HD
    for j in range(wide):
        grad_q[:, 128 * j:128 * (j + 1)] = rows[tall * j:tall * (j + 1)].astype(BF16)
    at = tall * wide
    grad_oe = jnp.concatenate([rows[at + HD * j:at + HD * (j + 1)] for j in range(DD // 128)], axis=1)
    grad_o[...] = dot_nt(grad_oe.astype(BF16), w_e2d[...]).astype(BF16)


def finish(total, w_e2d):
    width = w_e2d.shape[0]
    return call(
        finish_body, [((3 * HD, width), BF16), ((HD, width), BF16)], [], 130 << 20, 12, total, w_e2d)


def position_table(positions, width):
    half = width // 2
    freq = 10000.0 ** (-(jnp.arange(half, dtype=F32) * 2.0 / width))
    angle = positions[:, None] * freq[None, :]
    return jnp.concatenate([jnp.sin(angle), jnp.cos(angle)], axis=1)


Z_GROUPS = [[2 * z + c for z in range(NZ)] for c in range(2)]
X_GROUPS = [[NX * y + x for x in range(NX)] for y in range(NY)]
Y_GROUPS = [[NX * y + x for y in range(NY)] for x in range(NX)]


def exchange(block, axis, groups):
    return lax.all_to_all(block, axis, 0, 0, axis_index_groups=groups, tiled=True)


def spread(block, axis, groups):
    count = len(groups[0])
    copies = jnp.broadcast_to(block[None], (count,) + block.shape)
    return exchange(copies, axis, groups)


def z_shift(block, step):
    return lax.ppermute(block, "seq", [(s, (s + 2 * step) % 16) for s in range(16)])


def around(block):
    got = {0: block}
    for step in (1, -1, 2, -2):
        got[step % NZ] = z_shift(block, step)
    got[3] = z_shift(got[2], 1)
    got[5] = z_shift(got[6], -1)
    got[4] = z_shift(got[2], 2)
    return [got[k] for k in range(NZ)]


def swap_core(block):
    return lax.ppermute(block, "seq", [(s, s ^ 1) for s in range(16)])


def local(
    patches,
    keep_pos,
    kept_counts,
    enc_gain,
    w_qkv,
    w_out,
    w_e2d,
    mask_token,
    dec_gain,
    fc_in,
    fc_out,
    cotangent,
):
    me = lax.axis_index("seq")
    my_z, my_c = me // 2, me % 2
    fdev = cotangent.shape[1]
    cot = cotangent[0]
    cap = keep_pos.shape[1]
    rows = 16 * cap

    xn_own, x_slot, offsets = prep(keep_pos, patches[0], enc_gain[None])
    mine = join(around(xn_own))
    other = swap_core(mine)

    x_vis = dot(x_slot, w_e2d).astype(BF16)
    places = jnp.pad(offsets[:, 0].reshape(16, 1, SLOTS), ((0, 0), (0, 0), (0, 128 - SLOTS)))
    extra = jnp.concatenate(
        [x_vis.reshape(16, 12, 128), places, jnp.zeros((16, 3, 128), BF16)], axis=1)

    w_oe_own = jnp.pad(dot(w_out, w_e2d).astype(BF16), ((0, HP - HD), (0, 0)))
    weights = lax.all_gather(jnp.concatenate([fc_in, fc_out, w_oe_own], axis=0), "seq", axis=0)

    tok = jnp.arange(rows, dtype=jnp.int32)
    block = tok // cap
    source = (my_z - block % NZ) % NZ * 2 + (my_c ^ (block // NZ))
    inside = tok % cap
    dest = inside // SLOTS * cap + source * SLOTS + inside % SLOTS
    swap = (dest[None, :] == tok[:, None]).astype(BF16)
    table = position_table((me * fdev + jnp.arange(fdev, dtype=jnp.int32)).astype(F32), DD)

    w = jnp.pad(w_qkv.transpose(0, 2, 1), ((0, 0), (0, HL - HD), (0, 0))).reshape(3 * HL, -1)
    sent, saved, stats = attend(mine, other, w, swap, extra)
    came = lax.all_to_all(sent, "seq", 0, 0, tiled=True)
    recon, dvis_own = decode(came, weights, cot, mask_token[None], dec_gain[None], table)
    dvis = lax.all_gather(dvis_own, "seq", axis=0, tiled=True)
    parts = back(dvis, w_oe_own, swap, saved, stats, mine, other)

    parts = jnp.sum(exchange(parts.reshape(NX, 832, 128), "dp", X_GROUPS).astype(F32), axis=0).astype(BF16)
    parts = jnp.sum(exchange(parts.reshape(NY, 104, 128), "dp", Y_GROUPS).astype(F32), axis=0).astype(BF16)
    parts = spread(parts, "dp", Y_GROUPS).reshape(832, 128)
    total = spread(parts, "dp", X_GROUPS).reshape(GRAD_ROWS, 128)
    grad_q, grad_o = finish(total, w_e2d)
    grad_q = grad_q.reshape(3, HD, -1).transpose(0, 2, 1)
    return (recon[None], grad_q, grad_o)


def solution(mesh):
    placed = (
        P("dp", "seq", None),
        P("dp", "seq"),
        P("dp", None),
        P(),
        P(None, None, "seq"),
        P("seq", None),
        P(),
        P(),
        P(),
        P("seq", None),
        P("seq", None),
        P("dp", "seq", None),
    )
    return jax.shard_map(
        local,
        mesh=mesh,
        in_specs=placed,
        out_specs=(P("dp", "seq", None), P(None, None, "seq"), P("seq", None)),
        check_vma=False,
    )
```

```python
import jax
import jax.numpy as jnp
from jax import lax
from jax.experimental import pallas as pl
from jax.experimental.pallas import tpu as pltpu
from jax.sharding import PartitionSpec as P

HD = 88
HP = 96
HL = 128
DD = 512
NZ = 8
NX = 4
NY = 8
CAP = 48
ROWS = 768
SLOTS = 3
HID = 128
FDEV = 256
DEAD = 1024.0
GRAD_ROWS = 3328
SCALE = HD ** (-0.5)
F32 = jnp.float32
BF16 = jnp.bfloat16


def dot(a, b):
    return jnp.dot(a, b, preferred_element_type=F32)


def dot_nt(a, b):
    return lax.dot_general(a, b, (((1,), (1,)), ((), ())), preferred_element_type=F32)


def layer_norm(values, gain):
    mean = jnp.mean(values, axis=-1, keepdims=True)
    centred = values - mean
    var = jnp.mean(centred * centred, axis=-1, keepdims=True)
    return centred * lax.rsqrt(var + 1e-06) * gain


def call(body, outs, scratch, cost, grant, *args):
    return pl.pallas_call(
        body,
        out_shape=[jax.ShapeDtypeStruct(shape, dtype) for shape, dtype in outs],
        in_specs=[pl.BlockSpec(memory_space=pltpu.VMEM)] * len(args),
        out_specs=[pl.BlockSpec(memory_space=pltpu.VMEM)] * len(outs),
        scratch_shapes=scratch,
        compiler_params=pltpu.CompilerParams(vmem_limit_bytes=grant << 20),
        cost_estimate=pl.CostEstimate(flops=cost, bytes_accessed=8 << 20, transcendentals=1 << 20),
    )(*args)


def prep_body(keep, gain, patches, w_out, w_e2d, fc_in, fc_out, xn, x_vis, offsets, w_oe, pack,
              x_in, out_in, e2d_in, packed, sems):
    loads = [
        pltpu.make_async_copy(patches, x_in, sems.at[0]),
        pltpu.make_async_copy(w_out, out_in, sems.at[1]),
        pltpu.make_async_copy(w_e2d, e2d_in, sems.at[2]),
        pltpu.make_async_copy(fc_in, packed.at[pl.ds(0, HID)], sems.at[3]),
        pltpu.make_async_copy(fc_out, packed.at[pl.ds(HID, HID)], sems.at[4])]
    for copy in loads:
        copy.start()
    at_row = lax.broadcasted_iota(jnp.int32, (CAP, CAP), 0)
    at_col = lax.broadcasted_iota(jnp.int32, (CAP, CAP), 1)
    own = jnp.broadcast_to(keep[...], (CAP, CAP))
    owner = lax.shift_right_arithmetic(own, 8)
    owner_col = jnp.sum(jnp.where(at_row == at_col, owner, 0), axis=1, keepdims=True)
    same = (owner_col == owner) & (at_row < at_col)
    rank = jnp.sum(same.astype(jnp.int32), axis=0, keepdims=True)
    slot = jnp.where(own >= 0, owner * SLOTS + rank, -1)
    pick = at_row == slot
    live = jnp.sum(pick.astype(F32), axis=1, keepdims=True) > 0.5
    spot = jnp.sum(jnp.where(pick, own - owner * FDEV, 0).astype(F32), axis=1, keepdims=True)
    loads[0].wait()
    rows = dot(pick.astype(F32).astype(BF16), x_in[...])
    lane = lax.broadcasted_iota(jnp.int32, rows.shape, 1)
    dead_row = jnp.where(lane == 0, DEAD, 0.0)
    xn[...] = jnp.where(live, layer_norm(rows, gain[...]), dead_row).astype(BF16)
    offsets[...] = jnp.broadcast_to(jnp.where(live, spot, -1.0), (CAP, 128)).astype(BF16)
    for copy in loads[1:]:
        copy.wait()
    both = jnp.concatenate([dot(out_in[...], e2d_in[...]), jnp.zeros((HP - HD, DD), F32)], axis=0).astype(BF16)
    w_oe[...] = both
    packed[2 * HID:, :] = both
    done = pltpu.make_async_copy(packed, pack, sems.at[5])
    done.start()
    x_vis[...] = dot(rows.astype(BF16), e2d_in[...]).astype(BF16)
    done.wait()


def prep(keep, gain, *args):
    width = gain.shape[1]
    vmem = pl.BlockSpec(memory_space=pltpu.VMEM)
    hbm = pl.BlockSpec(memory_space=pltpu.HBM)
    return pl.pallas_call(
        prep_body,
        out_shape=[jax.ShapeDtypeStruct((CAP, width), BF16), jax.ShapeDtypeStruct((CAP, DD), BF16),
                   jax.ShapeDtypeStruct((CAP, 128), BF16), jax.ShapeDtypeStruct((HP, DD), BF16),
                   pltpu.HBM((2 * HID + HP, DD), BF16)],
        in_specs=[vmem, vmem] + [hbm] * len(args),
        out_specs=[vmem, vmem, vmem, vmem, hbm],
        scratch_shapes=[pltpu.VMEM((CAP, width), BF16), pltpu.VMEM((HD, width), BF16), pltpu.VMEM((width, DD), BF16),
                        pltpu.VMEM((2 * HID + HP, DD), BF16), pltpu.SemaphoreType.DMA((6,))],
        compiler_params=pltpu.CompilerParams(vmem_limit_bytes=12 << 20),
        cost_estimate=pl.CostEstimate(flops=200 << 20, bytes_accessed=3 << 20, transcendentals=0),
    )(keep, gain, *[pltpu.with_memory_space_constraint(arg, pltpu.HBM) for arg in args])


def turn_body(w_t, w):
    rows = w_t[...].astype(F32)
    gap = jnp.zeros((HL - HD, rows.shape[1]), F32)
    heads = [part for i in range(3) for part in (rows[HD * i:HD * (i + 1)], gap)]
    w[...] = jnp.concatenate(heads, axis=0).T.astype(BF16)


def turn(w_t):
    return call(turn_body, [((w_t.shape[1], 3 * HL), BF16)], [], 1 << 20, 16, w_t)[0]


def join_body(*refs):
    blocks, out, sems = refs[:NZ], refs[NZ], refs[NZ + 1]
    copies = [pltpu.make_async_copy(blocks[k], out.at[pl.ds(CAP * k, CAP)], sems.at[k]) for k in range(NZ)]
    for copy in copies:
        copy.start()
    for copy in copies:
        copy.wait()


def join(blocks):
    rows, width = blocks[0].shape
    return pl.pallas_call(
        join_body,
        out_shape=jax.ShapeDtypeStruct((NZ * rows, width), blocks[0].dtype),
        in_specs=[pl.BlockSpec(memory_space=pl.ANY)] * NZ,
        out_specs=pl.BlockSpec(memory_space=pl.ANY),
        scratch_shapes=[pltpu.SemaphoreType.DMA((NZ,))],
        compiler_params=pltpu.CompilerParams(vmem_limit_bytes=4 << 20),
        cost_estimate=pl.CostEstimate(flops=0, bytes_accessed=4 << 20, transcendentals=0),
    )(*blocks)


def attend_body(mine, other, w, swap, extra, sent, saved, stats, xs, out, keep, keep_stats, sems):
    half = ROWS // 2
    loads = [
        pltpu.make_async_copy(mine, xs.at[pl.ds(0, half)], sems.at[0]),
        pltpu.make_async_copy(other, xs.at[pl.ds(half, half)], sems.at[1])]
    for load in loads:
        load.start()
    parts = []
    for i in range(2):
        loads[i].wait()
        parts.append(dot(xs[half * i:half * (i + 1), :], w[...]))
    qkv = jnp.concatenate(parts, axis=0)
    k_rows = qkv[:, HL:2 * HL].astype(BF16)
    q = (qkv[:, 0:HL] * SCALE).T.astype(BF16)
    vt = qkv[:, 2 * HL:].T.astype(BF16)
    keep[0:HL, :] = q
    keep[HL:2 * HL, :] = qkv[:, HL:2 * HL].T.astype(BF16)
    keep[2 * HL:3 * HL, :] = vt
    heads = pltpu.make_async_copy(keep.at[pl.ds(0, 3 * HL)], saved.at[pl.ds(0, 3 * HL)], sems.at[2])
    heads.start()
    dead = jnp.where(xs[:, 0:128].astype(F32)[:, 0:1] < 0.5 * DEAD, 0.0, -jnp.inf)
    ctx = []
    for i in range(3):
        cols = slice(256 * i, 256 * (i + 1))
        scores = dot(k_rows, q[:, cols]) + dead
        top = jnp.max(scores, axis=0, keepdims=True)
        expo = jnp.exp(scores - top)
        total = jnp.sum(expo, axis=0, keepdims=True)
        keep_stats[0:1, cols] = top
        keep_stats[1:2, cols] = total
        ctx.append(dot(vt, (expo / total).astype(BF16)))
    sums = pltpu.make_async_copy(keep_stats, stats, sems.at[3])
    sums.start()
    ctx = jnp.concatenate(ctx, axis=1).astype(BF16)
    out[:, 0:CAP, :] = dot_nt(swap[...], ctx).astype(BF16).reshape(16, CAP, 128)
    out[:, CAP:, :] = extra[...]
    send = pltpu.make_async_copy(out, sent, sems.at[4])
    send.start()
    keep[3 * HL:, :] = dot_nt(ctx, swap[...]).astype(BF16)
    last = pltpu.make_async_copy(keep.at[pl.ds(3 * HL, HL)], saved.at[pl.ds(3 * HL, HL)], sems.at[5])
    last.start()
    for copy in (heads, sums, send, last):
        copy.wait()


def attend(*args):
    vmem = pl.BlockSpec(memory_space=pltpu.VMEM)
    hbm = pl.BlockSpec(memory_space=pltpu.HBM)
    return pl.pallas_call(
        attend_body,
        out_shape=[pltpu.HBM((16, 64, 128), BF16), pltpu.HBM((4 * HL, ROWS), BF16), pltpu.HBM((8, ROWS), F32)],
        in_specs=[hbm, hbm, vmem, vmem, vmem],
        out_specs=[hbm, hbm, hbm],
        scratch_shapes=[pltpu.VMEM((ROWS, args[0].shape[1]), BF16), pltpu.VMEM((16, 64, 128), BF16),
                        pltpu.VMEM((4 * HL, ROWS), BF16), pltpu.VMEM((8, ROWS), F32), pltpu.SemaphoreType.DMA((6,))],
        compiler_params=pltpu.CompilerParams(vmem_limit_bytes=24 << 20),
        cost_estimate=pl.CostEstimate(flops=1700 << 20, bytes_accessed=8 << 20, transcendentals=1 << 20),
    )(*args)


def load_body(weights, cot, w_oe, w_fc, dact, sems):
    loads = [
        pltpu.make_async_copy(
            weights.at[pl.ds(2 * i, 2), pl.ds(0, 2 * HID)], w_fc.at[pl.ds(2 * i, 2)], sems.at[i])
        for i in range(8)]
    oe = pltpu.make_async_copy(weights.at[:, pl.ds(2 * HID, HP)], w_oe, sems.at[8])
    for copy in (*loads, oe):
        copy.start()
    for i in range(8):
        loads[i].wait()
        fout = jnp.concatenate([w_fc[2 * i, HID:2 * HID, :], w_fc[2 * i + 1, HID:2 * HID, :]], axis=0)
        dact[:, 2 * HID * i:2 * HID * (i + 1)] = dot_nt(cot[...], fout)
    oe.wait()


def load(weights, cot):
    vmem = pl.BlockSpec(memory_space=pltpu.VMEM)
    return pl.pallas_call(
        load_body,
        out_shape=[pltpu.VMEM((16, HP, DD), BF16), pltpu.VMEM((16, 2 * HID, DD), BF16), pltpu.VMEM((FDEV, 16 * HID), F32)],
        in_specs=[pl.BlockSpec(memory_space=pltpu.HBM), vmem],
        out_specs=[vmem] * 3,
        scratch_shapes=[pltpu.SemaphoreType.DMA((9,))],
        compiler_params=pltpu.CompilerParams(vmem_limit_bytes=24 << 20),
        cost_estimate=pl.CostEstimate(flops=540 << 20, bytes_accessed=8 << 20, transcendentals=0),
    )(pltpu.with_memory_space_constraint(weights, pltpu.HBM), cot)


def decode_body(came, w_oe, w_fc, dact_in, cot, mask, gain, table, recon, dvis, mixed, grad):
    flat = came[...].reshape(16 * 64, 128)
    vis = jnp.zeros((CAP, DD), F32)
    for g in range(16):
        vis += dot(came[g, 0:CAP, 0:HP], w_oe[g])
    row = lax.broadcasted_iota(jnp.int32, (CAP, 1024), 0)
    col = lax.broadcasted_iota(jnp.int32, (CAP, 1024), 1)
    source = jnp.zeros((CAP, 1024), jnp.int32)
    for g in range(1, 16):
        source += (row >= SLOTS * g).astype(jnp.int32)
    slot = row - SLOTS * source
    base = 64 * source + CAP
    x_part = jnp.concatenate(
        [dot((col == base + 4 * slot + i).astype(F32).astype(BF16), flat) for i in range(4)], axis=1)
    vis = (vis + x_part).astype(BF16)
    spots = dot((col == base + 12).astype(F32).astype(BF16), flat)
    lane = lax.broadcasted_iota(jnp.int32, (CAP, 128), 1)
    spot = jnp.sum(jnp.where(lane == slot[:, 0:128], spots, 0.0), axis=1, keepdims=True)
    spot = jnp.concatenate([spot, jnp.full((128 - CAP, 1), -1.0, F32)], axis=0)
    vis = jnp.concatenate([vis.astype(F32), jnp.zeros((128 - CAP, DD), F32)], axis=0).astype(BF16)
    where_col = lax.broadcasted_iota(jnp.int32, (128, FDEV), 1).astype(F32)
    picker = (spot == where_col).astype(F32)
    placer = picker.T
    seen = jnp.sum(placer, axis=1, keepdims=True)
    dec_vis = dot(placer.astype(BF16), vis)
    dec_x = jnp.where(seen > 0.5, dec_vis, mask[...].astype(F32)) + table[...]
    mean = jnp.mean(dec_x, axis=-1, keepdims=True)
    centred = dec_x - mean
    var = jnp.mean(centred * centred, axis=-1, keepdims=True)
    inv_std = lax.rsqrt(var + 1e-06)
    normed = centred * inv_std
    dn = (normed * gain[...]).astype(BF16)
    cot_b = cot[...]
    mixed[...] = dec_x
    for i in range(8):
        fin = jnp.concatenate([w_fc[2 * i, 0:HID, :], w_fc[2 * i + 1, 0:HID, :]], axis=0)
        fout = jnp.concatenate([w_fc[2 * i, HID:2 * HID, :], w_fc[2 * i + 1, HID:2 * HID, :]], axis=0)
        hidden = dot_nt(dn, fin)
        dact = dact_in[:, 2 * HID * i:2 * HID * (i + 1)]
        cdf = 0.5 * (1.0 + lax.erf(hidden * 0.7071067811865476))
        pdf = jnp.exp(-0.5 * hidden * hidden) * 0.3989422804014327
        act = (hidden * cdf).astype(BF16)
        dhidden = (dact * (cdf + hidden * pdf)).astype(BF16)
        mixed[...] += dot(act, fout)
        if i == 0:
            grad[...] = dot(dhidden, fin)
        else:
            grad[...] += dot(dhidden, fin)
    recon[...] = mixed[...].astype(BF16)
    scaled = grad[...] * gain[...]
    first = jnp.mean(scaled, axis=-1, keepdims=True)
    second = jnp.mean(scaled * normed, axis=-1, keepdims=True)
    ddec = (cot_b.astype(F32) + inv_std * (scaled - first - normed * second)).astype(BF16)
    dvis[...] = dot(picker[0:CAP].astype(BF16), ddec).astype(BF16)


def decode(*args):
    return call(
        decode_body, [((FDEV, DD), BF16), ((CAP, DD), BF16)],
        [pltpu.VMEM((FDEV, DD), F32), pltpu.VMEM((FDEV, DD), F32)], 1800 << 20, 24, *args)


def back_body(dvis, w_oe, swap, saved, stats, mine, other, parts, ds_all, pb_all, keep, keep_stats, xs, sems):
    loads = [
        pltpu.make_async_copy(saved, keep, sems.at[0]),
        pltpu.make_async_copy(stats, keep_stats, sems.at[1]),
        pltpu.make_async_copy(mine, xs.at[pl.ds(0, ROWS // 2)], sems.at[2]),
        pltpu.make_async_copy(other, xs.at[pl.ds(ROWS // 2, ROWS // 2)], sems.at[3])]
    for load in loads:
        load.start()
    dctx = dot(dot_nt(w_oe[...], dvis[...]).astype(BF16), swap[...])
    dctx = jnp.concatenate([dctx, jnp.zeros((HL - HP, ROWS), F32)], axis=0).astype(BF16)
    for load in loads:
        load.wait()
    x = xs[...]
    grad_oe = dot(keep[3 * HL:, :], dvis[...])[0:HD]
    q, kt = keep[0:HL, :], keep[HL:2 * HL, :]
    k = kt.astype(F32).T.astype(BF16)
    v = keep[2 * HL:3 * HL, :].astype(F32).T.astype(BF16)
    dead = jnp.where(x[:, 0:128].astype(F32)[:, 0:1] < 0.5 * DEAD, 0.0, -jnp.inf)
    dq = []
    for i in range(3):
        cols = slice(256 * i, 256 * (i + 1))
        scores = dot(k, q[:, cols]) + dead
        probs = jnp.exp(scores - keep_stats[0:1, cols]) / keep_stats[1:2, cols]
        dprob = dot(v, dctx[:, cols])
        inner = jnp.sum(probs * dprob, axis=0, keepdims=True)
        ds = (probs * (dprob - inner)).astype(BF16)
        ds_all[:, cols] = ds
        pb_all[:, cols] = probs.astype(BF16)
        dq.append(dot(kt, ds) * SCALE)
    dq = jnp.concatenate(dq, axis=1)[0:HD]
    dk = dot_nt(q, ds_all[...])[0:HD]
    dv = dot_nt(dctx, pb_all[...])[0:HD]
    dqkv = jnp.concatenate([dq, dk, dv], axis=0).astype(BF16)
    grad = dot(dqkv, x)
    wide = grad.shape[1] // 128
    pieces = [grad[:, 128 * j:128 * (j + 1)] for j in range(wide)]
    pieces += [grad_oe[:, 128 * j:128 * (j + 1)] for j in range(DD // 128)]
    done = sum(p.shape[0] for p in pieces)
    pieces.append(jnp.zeros((GRAD_ROWS - done, 128), F32))
    parts[...] = jnp.concatenate(pieces, axis=0).astype(BF16)


def back(dvis, w_oe, swap, saved, stats, mine, other):
    vmem = pl.BlockSpec(memory_space=pltpu.VMEM)
    hbm = pl.BlockSpec(memory_space=pltpu.HBM)
    return pl.pallas_call(
        back_body,
        out_shape=jax.ShapeDtypeStruct((GRAD_ROWS, 128), BF16),
        in_specs=[vmem, vmem, vmem, hbm, hbm, hbm, hbm],
        out_specs=vmem,
        scratch_shapes=[pltpu.VMEM((ROWS, ROWS), BF16), pltpu.VMEM((ROWS, ROWS), BF16),
                        pltpu.VMEM((4 * HL, ROWS), BF16), pltpu.VMEM((8, ROWS), F32),
                        pltpu.VMEM((ROWS, mine.shape[1]), BF16), pltpu.SemaphoreType.DMA((4,))],
        compiler_params=pltpu.CompilerParams(vmem_limit_bytes=24 << 20),
        cost_estimate=pl.CostEstimate(flops=2500 << 20, bytes_accessed=8 << 20, transcendentals=1 << 20),
    )(dvis, w_oe, swap, saved, stats, mine, other)


def finish_body(total, w_e2d, grad_q, grad_o):
    rows = total[...].astype(F32)
    wide = grad_q.shape[1] // 128
    tall = 3 * HD
    for j in range(wide):
        grad_q[:, 128 * j:128 * (j + 1)] = rows[tall * j:tall * (j + 1)].astype(BF16)
    at = tall * wide
    grad_oe = jnp.concatenate([rows[at + HD * j:at + HD * (j + 1)] for j in range(DD // 128)], axis=1)
    grad_o[...] = dot_nt(grad_oe.astype(BF16), w_e2d[...]).astype(BF16)


def finish(total, w_e2d):
    width = w_e2d.shape[0]
    return call(
        finish_body, [((3 * HD, width), BF16), ((HD, width), BF16)], [], 130 << 20, 12, total, w_e2d)


def position_table(positions, width):
    half = width // 2
    freq = 10000.0 ** (-(jnp.arange(half, dtype=F32) * 2.0 / width))
    angle = positions[:, None] * freq[None, :]
    return jnp.concatenate([jnp.sin(angle), jnp.cos(angle)], axis=1)


Z_GROUPS = [[2 * z + c for z in range(NZ)] for c in range(2)]
X_GROUPS = [[NX * y + x for x in range(NX)] for y in range(NY)]
Y_GROUPS = [[NX * y + x for y in range(NY)] for x in range(NX)]


def exchange(block, axis, groups):
    return lax.all_to_all(block, axis, 0, 0, axis_index_groups=groups, tiled=True)


def spread(block, axis, groups):
    count = len(groups[0])
    copies = jnp.broadcast_to(block[None], (count,) + block.shape)
    return exchange(copies, axis, groups)


def z_shift(block, step):
    return lax.ppermute(block, "seq", [(s, (s + 2 * step) % 16) for s in range(16)])


def around(block):
    got = {0: block}
    for step in (1, -1, 2, -2):
        got[step % NZ] = z_shift(block, step)
    got[3] = z_shift(got[2], 1)
    got[5] = z_shift(got[6], -1)
    got[4] = z_shift(got[6], -2)
    return [got[k] for k in range(NZ)]


def swap_core(block):
    return lax.ppermute(block, "seq", [(s, s ^ 1) for s in range(16)])


def local(
    patches,
    keep_pos,
    kept_counts,
    enc_gain,
    w_qkv,
    w_out,
    w_e2d,
    mask_token,
    dec_gain,
    fc_in,
    fc_out,
    cotangent,
):
    me = lax.axis_index("seq")
    my_z, my_c = me // 2, me % 2
    fdev = cotangent.shape[1]
    cot = cotangent[0]
    cap = keep_pos.shape[1]
    rows = 16 * cap

    xn_own, x_vis, offsets, w_oe_own, pack = prep(
        keep_pos, enc_gain[None], patches[0], w_out, w_e2d, fc_in, fc_out)
    weights = lax.all_gather(pack, "seq", axis=0)

    places = jnp.pad(offsets[:, 0].reshape(16, 1, SLOTS), ((0, 0), (0, 0), (0, 128 - SLOTS)))
    extra = jnp.concatenate(
        [x_vis.reshape(16, 12, 128), places, jnp.zeros((16, 3, 128), BF16)], axis=1)

    tok = jnp.arange(rows, dtype=jnp.int32)
    block = tok // cap
    source = (my_z - block % NZ) % NZ * 2 + (my_c ^ (block // NZ))
    inside = tok % cap
    dest = inside // SLOTS * cap + source * SLOTS + inside % SLOTS
    swap = (dest[None, :] == tok[:, None]).astype(BF16)
    table = position_table((me * fdev + jnp.arange(fdev, dtype=jnp.int32)).astype(F32), DD)

    w = turn(w_qkv.transpose(0, 2, 1).reshape(3 * HD, -1))
    blocks = around(xn_own)
    blocks[4], w, swap, extra, table = lax.optimization_barrier((blocks[4], w, swap, extra, table))
    mine = join(blocks)
    other = swap_core(mine)
    sent, saved, stats = attend(mine, other, w, swap, extra)
    came = lax.all_to_all(sent, "seq", 0, 0, tiled=True)
    weights, stats = lax.optimization_barrier((weights, stats))
    w_oe, w_fc, dact = load(weights, cot)
    recon, dvis_own = decode(came, w_oe, w_fc, dact, cot, mask_token[None], dec_gain[None], table)
    dvis = lax.all_gather(dvis_own, "seq", axis=0, tiled=True)
    parts = back(dvis, w_oe_own, swap, saved, stats, mine, other)

    parts = jnp.sum(exchange(parts.reshape(NX, 832, 128), "dp", X_GROUPS).astype(F32), axis=0).astype(BF16)
    parts = jnp.sum(exchange(parts.reshape(NY, 104, 128), "dp", Y_GROUPS).astype(F32), axis=0).astype(BF16)
    parts = spread(parts, "dp", Y_GROUPS).reshape(832, 128)
    total = spread(parts, "dp", X_GROUPS).reshape(GRAD_ROWS, 128)
    grad_q, grad_o = finish(total, w_e2d)
    grad_q = grad_q.reshape(3, HD, -1).transpose(0, 2, 1)
    return (recon[None], grad_q, grad_o)


def solution(mesh):
    placed = (
        P("dp", "seq", None),
        P("dp", "seq"),
        P("dp", None),
        P(),
        P(None, None, "seq"),
        P("seq", None),
        P(),
        P(),
        P(),
        P("seq", None),
        P("seq", None),
        P("dp", "seq", None),
    )
    return jax.shard_map(
        local,
        mesh=mesh,
        in_specs=placed,
        out_specs=(P("dp", "seq", None), P(None, None, "seq"), P("seq", None)),
        check_vma=False,
    )
```

```python
import functools

import jax
import jax.numpy as jnp
from jax import lax
from jax.experimental import pallas as pl
from jax.experimental.pallas import tpu as pltpu
from jax.sharding import PartitionSpec as P

HD = 88
HP = 96
HL = 128
DD = 512
NZ = 8
NX = 4
NY = 8
CAP = 48
ROWS = 768
SLOTS = 3
HID = 128
FDEV = 256
DEAD = 1024.0
GRAD_ROWS = 3328
SCALE = HD ** (-0.5)
F32 = jnp.float32
BF16 = jnp.bfloat16


def dot(a, b):
    return jnp.dot(a, b, preferred_element_type=F32)


def dot_nt(a, b):
    return lax.dot_general(a, b, (((1,), (1,)), ((), ())), preferred_element_type=F32)


def layer_norm(values, gain):
    mean = jnp.mean(values, axis=-1, keepdims=True)
    centred = values - mean
    var = jnp.mean(centred * centred, axis=-1, keepdims=True)
    return centred * lax.rsqrt(var + 1e-06) * gain


def call(body, outs, scratch, cost, grant, *args):
    return pl.pallas_call(
        body,
        out_shape=[jax.ShapeDtypeStruct(shape, dtype) for shape, dtype in outs],
        in_specs=[pl.BlockSpec(memory_space=pltpu.VMEM)] * len(args),
        out_specs=[pl.BlockSpec(memory_space=pltpu.VMEM)] * len(outs),
        scratch_shapes=scratch,
        compiler_params=pltpu.CompilerParams(vmem_limit_bytes=grant << 20),
        cost_estimate=pl.CostEstimate(flops=cost, bytes_accessed=8 << 20, transcendentals=1 << 20),
    )(*args)


def prep_body(keep, gain, patches, xn, x_slot, offsets, x_in, sem):
    fetch = pltpu.make_async_copy(patches, x_in, sem.at[0])
    fetch.start()
    at_row = lax.broadcasted_iota(jnp.int32, (CAP, CAP), 0)
    at_col = lax.broadcasted_iota(jnp.int32, (CAP, CAP), 1)
    own = jnp.broadcast_to(keep[...], (CAP, CAP))
    owner = lax.shift_right_arithmetic(own, 8)
    owner_col = jnp.sum(jnp.where(at_row == at_col, owner, 0), axis=1, keepdims=True)
    same = (owner_col == owner) & (at_row < at_col)
    rank = jnp.sum(same.astype(jnp.int32), axis=0, keepdims=True)
    slot = jnp.where(own >= 0, owner * SLOTS + rank, -1)
    pick = at_row == slot
    live = jnp.sum(pick.astype(F32), axis=1, keepdims=True) > 0.5
    spot = jnp.sum(jnp.where(pick, own - owner * FDEV, 0).astype(F32), axis=1, keepdims=True)
    offsets[...] = jnp.broadcast_to(jnp.where(live, spot, -1.0), (CAP, 128)).astype(BF16)
    fetch.wait()
    rows = dot(pick.astype(F32).astype(BF16), x_in[...])
    x_slot[...] = rows.astype(BF16)
    lane = lax.broadcasted_iota(jnp.int32, rows.shape, 1)
    dead_row = jnp.where(lane == 0, DEAD, 0.0)
    xn[...] = jnp.where(live, layer_norm(rows, gain[...]), dead_row).astype(BF16)


def prep(keep, gain, patches):
    cap, width = patches.shape
    vmem = pl.BlockSpec(memory_space=pltpu.VMEM)
    return pl.pallas_call(
        prep_body,
        out_shape=[jax.ShapeDtypeStruct((cap, width), BF16), jax.ShapeDtypeStruct((cap, width), BF16),
                   jax.ShapeDtypeStruct((cap, 128), BF16)],
        in_specs=[vmem, vmem, pl.BlockSpec(memory_space=pltpu.HBM)],
        out_specs=[vmem] * 3,
        scratch_shapes=[pltpu.VMEM((cap, width), BF16), pltpu.SemaphoreType.DMA((1,))],
        compiler_params=pltpu.CompilerParams(vmem_limit_bytes=8 << 20),
        cost_estimate=pl.CostEstimate(flops=10 << 20, bytes_accessed=1 << 19, transcendentals=0),
    )(keep, gain, pltpu.with_memory_space_constraint(patches, pltpu.HBM))


def pack_body(x_slot, w_out, w_e2d, fc_in, fc_out, x_vis, w_oe, pack, out_in, e2d_in, packed, sems):
    loads = [
        pltpu.make_async_copy(w_out, out_in, sems.at[0]),
        pltpu.make_async_copy(w_e2d, e2d_in, sems.at[1]),
        pltpu.make_async_copy(fc_in, packed.at[pl.ds(0, HID)], sems.at[2]),
        pltpu.make_async_copy(fc_out, packed.at[pl.ds(HID, HID)], sems.at[3])]
    for copy in loads:
        copy.start()
    for copy in loads:
        copy.wait()
    both = jnp.concatenate([dot(out_in[...], e2d_in[...]), jnp.zeros((HP - HD, DD), F32)], axis=0).astype(BF16)
    w_oe[...] = both
    packed[2 * HID:, :] = both
    done = pltpu.make_async_copy(packed, pack, sems.at[4])
    done.start()
    x_vis[...] = dot(x_slot[...], e2d_in[...]).astype(BF16)
    done.wait()


def pack_up(x_slot, *args):
    width = x_slot.shape[1]
    vmem = pl.BlockSpec(memory_space=pltpu.VMEM)
    hbm = pl.BlockSpec(memory_space=pltpu.HBM)
    return pl.pallas_call(
        pack_body,
        out_shape=[jax.ShapeDtypeStruct((CAP, DD), BF16), jax.ShapeDtypeStruct((HP, DD), BF16),
                   pltpu.HBM((2 * HID + HP, DD), BF16)],
        in_specs=[vmem] + [hbm] * len(args),
        out_specs=[vmem, vmem, hbm],
        scratch_shapes=[pltpu.VMEM((HD, width), BF16), pltpu.VMEM((width, DD), BF16),
                        pltpu.VMEM((2 * HID + HP, DD), BF16), pltpu.SemaphoreType.DMA((5,))],
        compiler_params=pltpu.CompilerParams(vmem_limit_bytes=12 << 20),
        cost_estimate=pl.CostEstimate(flops=200 << 20, bytes_accessed=3 << 20, transcendentals=0),
    )(x_slot, *[pltpu.with_memory_space_constraint(arg, pltpu.HBM) for arg in args])


def turn_body(w_t, w):
    rows = w_t[...].astype(F32)
    gap = jnp.zeros((HL - HD, rows.shape[1]), F32)
    heads = [part for i in range(3) for part in (rows[HD * i:HD * (i + 1)], gap)]
    w[...] = jnp.concatenate(heads, axis=0).T.astype(BF16)


def turn(w_t):
    return call(turn_body, [((w_t.shape[1], 3 * HL), BF16)], [], 1 << 20, 16, w_t)[0]


def join_body(places, *refs):
    blocks, out, sems = refs[:len(places)], refs[len(places)], refs[len(places) + 1]
    copies = []
    for i, (k, column) in enumerate(places):
        rows, width = blocks[i].shape
        part = out.at[pl.ds(rows * k, rows), pl.ds(column, width)]
        copies.append(pltpu.make_async_copy(blocks[i], part, sems.at[i]))
    for copy in copies:
        copy.start()
    for copy in copies:
        copy.wait()


def join(blocks):
    places = []
    for k, parts in enumerate(blocks):
        column = 0
        for part in parts:
            places.append((k, column))
            column += part.shape[1]
    flat = [part for parts in blocks for part in parts]
    return pl.pallas_call(
        functools.partial(join_body, places),
        out_shape=jax.ShapeDtypeStruct((NZ * flat[0].shape[0], flat[0].shape[1]), flat[0].dtype),
        in_specs=[pl.BlockSpec(memory_space=pl.ANY)] * len(flat),
        out_specs=pl.BlockSpec(memory_space=pl.ANY),
        scratch_shapes=[pltpu.SemaphoreType.DMA((len(flat),))],
        compiler_params=pltpu.CompilerParams(vmem_limit_bytes=4 << 20),
        cost_estimate=pl.CostEstimate(flops=0, bytes_accessed=4 << 20, transcendentals=0),
    )(*flat)


def attend_body(mine, other, w, swap, extra, sent, saved, stats, xs, out, keep, keep_stats, sems):
    half = ROWS // 2
    loads = [
        pltpu.make_async_copy(mine, xs.at[pl.ds(0, half)], sems.at[0]),
        pltpu.make_async_copy(other, xs.at[pl.ds(half, half)], sems.at[1])]
    for load in loads:
        load.start()
    parts = []
    for i in range(2):
        loads[i].wait()
        parts.append(dot(xs[half * i:half * (i + 1), :], w[...]))
    qkv = jnp.concatenate(parts, axis=0)
    k_rows = qkv[:, HL:2 * HL].astype(BF16)
    q = (qkv[:, 0:HL] * SCALE).T.astype(BF16)
    vt = qkv[:, 2 * HL:].T.astype(BF16)
    keep[0:HL, :] = q
    keep[HL:2 * HL, :] = qkv[:, HL:2 * HL].T.astype(BF16)
    keep[2 * HL:3 * HL, :] = vt
    heads = pltpu.make_async_copy(keep.at[pl.ds(0, 3 * HL)], saved.at[pl.ds(0, 3 * HL)], sems.at[2])
    heads.start()
    dead = jnp.where(xs[:, 0:128].astype(F32)[:, 0:1] < 0.5 * DEAD, 0.0, -jnp.inf)
    ctx = []
    for i in range(3):
        cols = slice(256 * i, 256 * (i + 1))
        scores = dot(k_rows, q[:, cols]) + dead
        top = jnp.max(scores, axis=0, keepdims=True)
        expo = jnp.exp(scores - top)
        total = jnp.sum(expo, axis=0, keepdims=True)
        keep_stats[0:1, cols] = top
        keep_stats[1:2, cols] = total
        ctx.append(dot(vt, (expo / total).astype(BF16)))
    sums = pltpu.make_async_copy(keep_stats, stats, sems.at[3])
    sums.start()
    ctx = jnp.concatenate(ctx, axis=1).astype(BF16)
    out[:, 0:CAP, :] = dot_nt(swap[...], ctx).astype(BF16).reshape(16, CAP, 128)
    out[:, CAP:, :] = extra[...]
    send = pltpu.make_async_copy(out, sent, sems.at[4])
    send.start()
    keep[3 * HL:, :] = dot_nt(ctx, swap[...]).astype(BF16)
    last = pltpu.make_async_copy(keep.at[pl.ds(3 * HL, HL)], saved.at[pl.ds(3 * HL, HL)], sems.at[5])
    last.start()
    for copy in (heads, sums, send, last):
        copy.wait()


def attend(*args):
    vmem = pl.BlockSpec(memory_space=pltpu.VMEM)
    hbm = pl.BlockSpec(memory_space=pltpu.HBM)
    return pl.pallas_call(
        attend_body,
        out_shape=[pltpu.HBM((16, 64, 128), BF16), pltpu.HBM((4 * HL, ROWS), BF16), pltpu.HBM((8, ROWS), F32)],
        in_specs=[hbm, hbm, vmem, vmem, vmem],
        out_specs=[hbm, hbm, hbm],
        scratch_shapes=[pltpu.VMEM((ROWS, args[0].shape[1]), BF16), pltpu.VMEM((16, 64, 128), BF16),
                        pltpu.VMEM((4 * HL, ROWS), BF16), pltpu.VMEM((8, ROWS), F32), pltpu.SemaphoreType.DMA((6,))],
        compiler_params=pltpu.CompilerParams(vmem_limit_bytes=24 << 20),
        cost_estimate=pl.CostEstimate(flops=1700 << 20, bytes_accessed=8 << 20, transcendentals=1 << 20),
    )(*args)


def decode_body(came, weights, cot, mask, gain, table, recon, dvis, mixed, grad, w_oe, w_fc, cots, sems):
    loads = [pltpu.make_async_copy(weights.at[:, pl.ds(2 * HID, HP)], w_oe, sems.at[0])]
    loads += [
        pltpu.make_async_copy(
            weights.at[pl.ds(8 * i, 8), pl.ds(0, 2 * HID)], w_fc.at[pl.ds(8 * i, 8)], sems.at[1 + i])
        for i in range(2)]
    up = pltpu.make_async_copy(cot, cots, sems.at[3])
    for copy in (loads[0], up, *loads[1:]):
        copy.start()
    flat = came[...].reshape(16 * 64, 128)
    vis = jnp.zeros((CAP, DD), F32)
    loads[0].wait()
    for g in range(16):
        vis += dot(came[g, 0:CAP, 0:HP], w_oe[g])
    row = lax.broadcasted_iota(jnp.int32, (CAP, 1024), 0)
    col = lax.broadcasted_iota(jnp.int32, (CAP, 1024), 1)
    source = jnp.zeros((CAP, 1024), jnp.int32)
    for g in range(1, 16):
        source += (row >= SLOTS * g).astype(jnp.int32)
    slot = row - SLOTS * source
    base = 64 * source + CAP
    x_part = jnp.concatenate(
        [dot((col == base + 4 * slot + i).astype(F32).astype(BF16), flat) for i in range(4)], axis=1)
    vis = (vis + x_part).astype(BF16)
    spots = dot((col == base + 12).astype(F32).astype(BF16), flat)
    lane = lax.broadcasted_iota(jnp.int32, (CAP, 128), 1)
    spot = jnp.sum(jnp.where(lane == slot[:, 0:128], spots, 0.0), axis=1, keepdims=True)
    spot = jnp.concatenate([spot, jnp.full((128 - CAP, 1), -1.0, F32)], axis=0)
    vis = jnp.concatenate([vis.astype(F32), jnp.zeros((128 - CAP, DD), F32)], axis=0).astype(BF16)
    where_col = lax.broadcasted_iota(jnp.int32, (128, FDEV), 1).astype(F32)
    picker = (spot == where_col).astype(F32)
    placer = picker.T
    seen = jnp.sum(placer, axis=1, keepdims=True)
    dec_vis = dot(placer.astype(BF16), vis)
    dec_x = jnp.where(seen > 0.5, dec_vis, mask[...].astype(F32)) + table[...]
    mean = jnp.mean(dec_x, axis=-1, keepdims=True)
    centred = dec_x - mean
    var = jnp.mean(centred * centred, axis=-1, keepdims=True)
    inv_std = lax.rsqrt(var + 1e-06)
    normed = centred * inv_std
    dn = (normed * gain[...]).astype(BF16)
    up.wait()
    cot_b = cots[...]
    mixed[...] = dec_x
    for i in range(8):
        if i % 4 == 0:
            loads[1 + i // 4].wait()
        fin = jnp.concatenate([w_fc[2 * i, 0:HID, :], w_fc[2 * i + 1, 0:HID, :]], axis=0)
        fout = jnp.concatenate([w_fc[2 * i, HID:2 * HID, :], w_fc[2 * i + 1, HID:2 * HID, :]], axis=0)
        hidden = dot_nt(dn, fin)
        dact = dot_nt(cot_b, fout)
        cdf = 0.5 * (1.0 + lax.erf(hidden * 0.7071067811865476))
        pdf = jnp.exp(-0.5 * hidden * hidden) * 0.3989422804014327
        act = (hidden * cdf).astype(BF16)
        dhidden = (dact * (cdf + hidden * pdf)).astype(BF16)
        mixed[...] += dot(act, fout)
        if i == 0:
            grad[...] = dot(dhidden, fin)
        else:
            grad[...] += dot(dhidden, fin)
    recon[...] = mixed[...].astype(BF16)
    scaled = grad[...] * gain[...]
    first = jnp.mean(scaled, axis=-1, keepdims=True)
    second = jnp.mean(scaled * normed, axis=-1, keepdims=True)
    ddec = (cot_b.astype(F32) + inv_std * (scaled - first - normed * second)).astype(BF16)
    dvis[...] = dot(picker[0:CAP].astype(BF16), ddec).astype(BF16)


def decode(came, weights, cot, *args):
    vmem = pl.BlockSpec(memory_space=pltpu.VMEM)
    hbm = pl.BlockSpec(memory_space=pltpu.HBM)
    return pl.pallas_call(
        decode_body,
        out_shape=[jax.ShapeDtypeStruct((FDEV, DD), BF16), jax.ShapeDtypeStruct((CAP, DD), BF16)],
        in_specs=[vmem, hbm, hbm] + [vmem] * len(args),
        out_specs=[vmem, vmem],
        scratch_shapes=[pltpu.VMEM((FDEV, DD), F32), pltpu.VMEM((FDEV, DD), F32),
                        pltpu.VMEM((16, HP, DD), BF16), pltpu.VMEM((16, 2 * HID, DD), BF16),
                        pltpu.VMEM((FDEV, DD), BF16), pltpu.SemaphoreType.DMA((4,))],
        compiler_params=pltpu.CompilerParams(vmem_limit_bytes=24 << 20),
        cost_estimate=pl.CostEstimate(flops=2300 << 20, bytes_accessed=8 << 20, transcendentals=1 << 20),
    )(came, pltpu.with_memory_space_constraint(weights, pltpu.HBM),
      pltpu.with_memory_space_constraint(cot, pltpu.HBM), *args)


def back_body(dvis, w_oe, swap, saved, stats, mine, other, parts, ds_all, pb_all, keep, keep_stats, xs, sems):
    loads = [
        pltpu.make_async_copy(saved, keep, sems.at[0]),
        pltpu.make_async_copy(stats, keep_stats, sems.at[1]),
        pltpu.make_async_copy(mine, xs.at[pl.ds(0, ROWS // 2)], sems.at[2]),
        pltpu.make_async_copy(other, xs.at[pl.ds(ROWS // 2, ROWS // 2)], sems.at[3])]
    for load in loads:
        load.start()
    dctx = dot(dot_nt(w_oe[...], dvis[...]).astype(BF16), swap[...])
    dctx = jnp.concatenate([dctx, jnp.zeros((HL - HP, ROWS), F32)], axis=0).astype(BF16)
    for load in loads:
        load.wait()
    x = xs[...]
    grad_oe = dot(keep[3 * HL:, :], dvis[...])[0:HD]
    q, kt = keep[0:HL, :], keep[HL:2 * HL, :]
    k = kt.astype(F32).T.astype(BF16)
    v = keep[2 * HL:3 * HL, :].astype(F32).T.astype(BF16)
    dead = jnp.where(x[:, 0:128].astype(F32)[:, 0:1] < 0.5 * DEAD, 0.0, -jnp.inf)
    dq = []
    for i in range(3):
        cols = slice(256 * i, 256 * (i + 1))
        scores = dot(k, q[:, cols]) + dead
        probs = jnp.exp(scores - keep_stats[0:1, cols]) / keep_stats[1:2, cols]
        dprob = dot(v, dctx[:, cols])
        inner = jnp.sum(probs * dprob, axis=0, keepdims=True)
        ds = (probs * (dprob - inner)).astype(BF16)
        ds_all[:, cols] = ds
        pb_all[:, cols] = probs.astype(BF16)
        dq.append(dot(kt, ds) * SCALE)
    dq = jnp.concatenate(dq, axis=1)[0:HD]
    dk = dot_nt(q, ds_all[...])[0:HD]
    dv = dot_nt(dctx, pb_all[...])[0:HD]
    dqkv = jnp.concatenate([dq, dk, dv], axis=0).astype(BF16)
    grad = dot(dqkv, x)
    wide = grad.shape[1] // 128
    pieces = [grad[:, 128 * j:128 * (j + 1)] for j in range(wide)]
    pieces += [grad_oe[:, 128 * j:128 * (j + 1)] for j in range(DD // 128)]
    done = sum(p.shape[0] for p in pieces)
    pieces.append(jnp.zeros((GRAD_ROWS - done, 128), F32))
    parts[...] = jnp.concatenate(pieces, axis=0).astype(BF16)


def back(dvis, w_oe, swap, saved, stats, mine, other):
    vmem = pl.BlockSpec(memory_space=pltpu.VMEM)
    hbm = pl.BlockSpec(memory_space=pltpu.HBM)
    return pl.pallas_call(
        back_body,
        out_shape=jax.ShapeDtypeStruct((GRAD_ROWS, 128), BF16),
        in_specs=[vmem, vmem, vmem, hbm, hbm, hbm, hbm],
        out_specs=vmem,
        scratch_shapes=[pltpu.VMEM((ROWS, ROWS), BF16), pltpu.VMEM((ROWS, ROWS), BF16),
                        pltpu.VMEM((4 * HL, ROWS), BF16), pltpu.VMEM((8, ROWS), F32),
                        pltpu.VMEM((ROWS, mine.shape[1]), BF16), pltpu.SemaphoreType.DMA((4,))],
        compiler_params=pltpu.CompilerParams(vmem_limit_bytes=24 << 20),
        cost_estimate=pl.CostEstimate(flops=2500 << 20, bytes_accessed=8 << 20, transcendentals=1 << 20),
    )(dvis, w_oe, swap, saved, stats, mine, other)


def finish_body(total, w_e2d, grad_q, grad_o):
    rows = total[...].astype(F32)
    wide = grad_q.shape[1] // 128
    tall = 3 * HD
    for j in range(wide):
        grad_q[:, 128 * j:128 * (j + 1)] = rows[tall * j:tall * (j + 1)].astype(BF16)
    at = tall * wide
    grad_oe = jnp.concatenate([rows[at + HD * j:at + HD * (j + 1)] for j in range(DD // 128)], axis=1)
    grad_o[...] = dot_nt(grad_oe.astype(BF16), w_e2d[...]).astype(BF16)


def finish(total, w_e2d):
    width = w_e2d.shape[0]
    return call(
        finish_body, [((3 * HD, width), BF16), ((HD, width), BF16)], [], 130 << 20, 12, total, w_e2d)


def position_table(positions, width):
    half = width // 2
    freq = 10000.0 ** (-(jnp.arange(half, dtype=F32) * 2.0 / width))
    angle = positions[:, None] * freq[None, :]
    return jnp.concatenate([jnp.sin(angle), jnp.cos(angle)], axis=1)


Z_GROUPS = [[2 * z + c for z in range(NZ)] for c in range(2)]
X_GROUPS = [[NX * y + x for x in range(NX)] for y in range(NY)]
Y_GROUPS = [[NX * y + x for y in range(NY)] for x in range(NX)]


def exchange(block, axis, groups):
    return lax.all_to_all(block, axis, 0, 0, axis_index_groups=groups, tiled=True)


def spread(block, axis, groups):
    count = len(groups[0])
    copies = jnp.broadcast_to(block[None], (count,) + block.shape)
    return exchange(copies, axis, groups)


def z_shift(block, step):
    return lax.ppermute(block, "seq", [(s, (s + 2 * step) % 16) for s in range(16)])


def around(block):
    got = {0: block}
    for step in (1, -1, 2, -2):
        got[step % NZ] = z_shift(block, step)
    got[3] = z_shift(got[2], 1)
    got[5] = z_shift(got[6], -1)
    got[4] = z_shift(got[2], 2)
    return [[got[k]] for k in range(NZ)]


def swap_core(block):
    return lax.ppermute(block, "seq", [(s, s ^ 1) for s in range(16)])


def local(
    patches,
    keep_pos,
    kept_counts,
    enc_gain,
    w_qkv,
    w_out,
    w_e2d,
    mask_token,
    dec_gain,
    fc_in,
    fc_out,
    cotangent,
):
    me = lax.axis_index("seq")
    my_z, my_c = me // 2, me % 2
    fdev = cotangent.shape[1]
    cot = cotangent[0]
    cap = keep_pos.shape[1]
    rows = 16 * cap

    xn_own, x_slot, offsets = prep(keep_pos, enc_gain[None], patches[0])
    x_vis, w_oe_own, pack = pack_up(x_slot, w_out, w_e2d, fc_in, fc_out)
    weights = lax.all_gather(pack, "seq", axis=0)

    places = jnp.pad(offsets[:, 0].reshape(16, 1, SLOTS), ((0, 0), (0, 0), (0, 128 - SLOTS)))
    extra = jnp.concatenate(
        [x_vis.reshape(16, 12, 128), places, jnp.zeros((16, 3, 128), BF16)], axis=1)

    tok = jnp.arange(rows, dtype=jnp.int32)
    block = tok // cap
    source = (my_z - block % NZ) % NZ * 2 + (my_c ^ (block // NZ))
    inside = tok % cap
    dest = inside // SLOTS * cap + source * SLOTS + inside % SLOTS
    swap = (dest[None, :] == tok[:, None]).astype(BF16)
    table = position_table((me * fdev + jnp.arange(fdev, dtype=jnp.int32)).astype(F32), DD)

    w = turn(w_qkv.transpose(0, 2, 1).reshape(3 * HD, -1))
    blocks = around(xn_own)
    blocks[4][0], w, swap, extra, table = lax.optimization_barrier((blocks[4][0], w, swap, extra, table))
    mine = join(blocks)
    other = swap_core(mine)
    sent, saved, stats = attend(mine, other, w, swap, extra)
    came = lax.all_to_all(sent, "seq", 0, 0, tiled=True)
    recon, dvis_own = decode(came, weights, cot, mask_token[None], dec_gain[None], table)
    dvis = lax.all_gather(dvis_own, "seq", axis=0, tiled=True)
    parts = back(dvis, w_oe_own, swap, saved, stats, mine, other)

    parts = jnp.sum(exchange(parts.reshape(NX, 832, 128), "dp", X_GROUPS).astype(F32), axis=0).astype(BF16)
    parts = jnp.sum(exchange(parts.reshape(NY, 104, 128), "dp", Y_GROUPS).astype(F32), axis=0).astype(BF16)
    parts = spread(parts, "dp", Y_GROUPS).reshape(832, 128)
    total = spread(parts, "dp", X_GROUPS).reshape(GRAD_ROWS, 128)
    grad_q, grad_o = finish(total, w_e2d)
    grad_q = grad_q.reshape(3, HD, -1).transpose(0, 2, 1)
    return (recon[None], grad_q, grad_o)


def solution(mesh):
    placed = (
        P("dp", "seq", None),
        P("dp", "seq"),
        P("dp", None),
        P(),
        P(None, None, "seq"),
        P("seq", None),
        P(),
        P(),
        P(),
        P("seq", None),
        P("seq", None),
        P("dp", "seq", None),
    )
    return jax.shard_map(
        local,
        mesh=mesh,
        in_specs=placed,
        out_specs=(P("dp", "seq", None), P(None, None, "seq"), P("seq", None)),
        check_vma=False,
    )
```

```python
import functools

import jax
import jax.numpy as jnp
from jax import lax
from jax.experimental import pallas as pl
from jax.experimental.pallas import tpu as pltpu
from jax.sharding import Mesh
from jax.sharding import PartitionSpec as P

HD = 88
HP = 96
HL = 128
DD = 512
SEQ = ("z", "core")
NZ = 8
NX = 4
NY = 8
CAP = 48
ROWS = 768
SLOTS = 3
HID = 128
FDEV = 256
DEAD = 1024.0
GRAD_ROWS = 3328
SCALE = HD ** (-0.5)
F32 = jnp.float32
BF16 = jnp.bfloat16


def dot(a, b):
    return jnp.dot(a, b, preferred_element_type=F32)


def dot_nt(a, b):
    return lax.dot_general(a, b, (((1,), (1,)), ((), ())), preferred_element_type=F32)


def layer_norm(values, gain):
    mean = jnp.mean(values, axis=-1, keepdims=True)
    centred = values - mean
    var = jnp.mean(centred * centred, axis=-1, keepdims=True)
    return centred * lax.rsqrt(var + 1e-06) * gain


def call(body, outs, scratch, cost, grant, *args):
    return pl.pallas_call(
        body,
        out_shape=[jax.ShapeDtypeStruct(shape, dtype) for shape, dtype in outs],
        in_specs=[pl.BlockSpec(memory_space=pltpu.VMEM)] * len(args),
        out_specs=[pl.BlockSpec(memory_space=pltpu.VMEM)] * len(outs),
        scratch_shapes=scratch,
        compiler_params=pltpu.CompilerParams(vmem_limit_bytes=grant << 20),
        cost_estimate=pl.CostEstimate(flops=cost, bytes_accessed=8 << 20, transcendentals=1 << 20),
    )(*args)


def prep_body(keep, gain, patches, xn, x_slot, offsets, keep_in, gain_in, x_in, sems):
    small = pltpu.make_async_copy(keep, keep_in, sems.at[0])
    other = pltpu.make_async_copy(gain, gain_in, sems.at[1])
    fetch = pltpu.make_async_copy(patches, x_in, sems.at[2])
    for copy in (small, fetch, other):
        copy.start()
    small.wait()
    at_row = lax.broadcasted_iota(jnp.int32, (CAP, CAP), 0)
    at_col = lax.broadcasted_iota(jnp.int32, (CAP, CAP), 1)
    own = jnp.broadcast_to(keep_in[...], (CAP, CAP))
    owner = lax.shift_right_arithmetic(own, 8)
    owner_col = jnp.sum(jnp.where(at_row == at_col, owner, 0), axis=1, keepdims=True)
    same = (owner_col == owner) & (at_row < at_col)
    rank = jnp.sum(same.astype(jnp.int32), axis=0, keepdims=True)
    slot = jnp.where(own >= 0, owner * SLOTS + rank, -1)
    pick = at_row == slot
    live = jnp.sum(pick.astype(F32), axis=1, keepdims=True) > 0.5
    spot = jnp.sum(jnp.where(pick, own - owner * FDEV, 0).astype(F32), axis=1, keepdims=True)
    offsets[...] = jnp.broadcast_to(jnp.where(live, spot, -1.0), (CAP, 128)).astype(BF16)
    fetch.wait()
    other.wait()
    rows = dot(pick.astype(F32).astype(BF16), x_in[...])
    x_slot[...] = rows.astype(BF16)
    lane = lax.broadcasted_iota(jnp.int32, rows.shape, 1)
    dead_row = jnp.where(lane == 0, DEAD, 0.0)
    xn[...] = jnp.where(live, layer_norm(rows, gain_in[...].reshape(1, rows.shape[1])), dead_row).astype(BF16)


def prep(keep, gain, patches):
    cap, width = patches.shape
    vmem = pl.BlockSpec(memory_space=pltpu.VMEM)
    return pl.pallas_call(
        prep_body,
        out_shape=[jax.ShapeDtypeStruct((cap, width), BF16), jax.ShapeDtypeStruct((cap, width), BF16),
                   jax.ShapeDtypeStruct((cap, 128), BF16)],
        in_specs=[pl.BlockSpec(memory_space=pltpu.HBM)] * 3,
        out_specs=[vmem] * 3,
        scratch_shapes=[pltpu.VMEM(keep.shape, keep.dtype), pltpu.VMEM(gain.shape, F32),
                        pltpu.VMEM((cap, width), BF16), pltpu.SemaphoreType.DMA((3,))],
        compiler_params=pltpu.CompilerParams(vmem_limit_bytes=8 << 20),
        cost_estimate=pl.CostEstimate(flops=10 << 20, bytes_accessed=1 << 19, transcendentals=0),
    )(*[pltpu.with_memory_space_constraint(arg, pltpu.HBM) for arg in (keep, gain, patches)])


def pack_body(x_slot, w_out, w_e2d, fc_in, fc_out, x_vis, w_oe, pack, out_in, e2d_in, packed, sems):
    loads = [
        pltpu.make_async_copy(w_out, out_in, sems.at[0]),
        pltpu.make_async_copy(w_e2d, e2d_in, sems.at[1]),
        pltpu.make_async_copy(fc_in, packed.at[pl.ds(0, HID)], sems.at[2]),
        pltpu.make_async_copy(fc_out, packed.at[pl.ds(HID, HID)], sems.at[3])]
    for copy in loads:
        copy.start()
    for copy in loads:
        copy.wait()
    both = jnp.concatenate([dot(out_in[...], e2d_in[...]), jnp.zeros((HP - HD, DD), F32)], axis=0).astype(BF16)
    w_oe[...] = both
    packed[2 * HID:, :] = both
    done = pltpu.make_async_copy(packed, pack, sems.at[4])
    done.start()
    x_vis[...] = dot(x_slot[...], e2d_in[...]).astype(BF16)
    done.wait()


def pack_up(x_slot, *args):
    width = x_slot.shape[1]
    vmem = pl.BlockSpec(memory_space=pltpu.VMEM)
    hbm = pl.BlockSpec(memory_space=pltpu.HBM)
    return pl.pallas_call(
        pack_body,
        out_shape=[jax.ShapeDtypeStruct((CAP, DD), BF16), jax.ShapeDtypeStruct((HP, DD), BF16),
                   pltpu.HBM((2 * HID + HP, DD), BF16)],
        in_specs=[vmem] + [hbm] * len(args),
        out_specs=[vmem, vmem, hbm],
        scratch_shapes=[pltpu.VMEM((HD, width), BF16), pltpu.VMEM((width, DD), BF16),
                        pltpu.VMEM((2 * HID + HP, DD), BF16), pltpu.SemaphoreType.DMA((5,))],
        compiler_params=pltpu.CompilerParams(vmem_limit_bytes=12 << 20),
        cost_estimate=pl.CostEstimate(flops=200 << 20, bytes_accessed=3 << 20, transcendentals=0),
    )(x_slot, *[pltpu.with_memory_space_constraint(arg, pltpu.HBM) for arg in args])


def turn_body(w_t, w):
    rows = w_t[...].astype(F32)
    gap = jnp.zeros((HL - HD, rows.shape[1]), F32)
    heads = [part for i in range(3) for part in (rows[HD * i:HD * (i + 1)], gap)]
    w[...] = jnp.concatenate(heads, axis=0).T.astype(BF16)


def turn(w_t):
    return call(turn_body, [((w_t.shape[1], 3 * HL), BF16)], [], 1 << 20, 16, w_t)[0]


def join_body(*refs):
    count = len(refs) - 2
    blocks, out, sems = refs[:count], refs[count], refs[count + 1]
    copies = [pltpu.make_async_copy(blocks[k], out.at[pl.ds(CAP * k, CAP)], sems.at[k]) for k in range(count)]
    for copy in copies:
        copy.start()
    for copy in copies:
        copy.wait()


def join(blocks):
    rows, width = blocks[0].shape
    return pl.pallas_call(
        join_body,
        out_shape=jax.ShapeDtypeStruct((len(blocks) * rows, width), blocks[0].dtype),
        in_specs=[pl.BlockSpec(memory_space=pl.ANY)] * len(blocks),
        out_specs=pl.BlockSpec(memory_space=pl.ANY),
        scratch_shapes=[pltpu.SemaphoreType.DMA((len(blocks),))],
        compiler_params=pltpu.CompilerParams(vmem_limit_bytes=4 << 20),
        cost_estimate=pl.CostEstimate(flops=0, bytes_accessed=2 << 20, transcendentals=0),
    )(*blocks)


def row_loads(rows_in, xs, sems, first):
    copies = []
    for d in range(2):
        near, far = rows_in[2 * d], rows_in[2 * d + 1]
        for source, start, place, count in ((near, 0, 0, 3), (near, 3, 6, 2), (far, 0, 3, 3)):
            copies.append(pltpu.make_async_copy(
                source.at[pl.ds(CAP * start, CAP * count)],
                xs.at[pl.ds(CAP * (NZ * d + place), CAP * count)], sems.at[first + len(copies)]))
    return copies


def attend_body(w, swap, extra, *refs):
    rows_in, (sent, saved, stats, xs, out, keep, keep_stats, sems) = refs[:4], refs[4:]
    half = ROWS // 2
    loads = row_loads(rows_in, xs, sems, 6)
    for load in loads:
        load.start()
    parts = []
    for i in range(2):
        for load in loads[3 * i:3 * (i + 1)]:
            load.wait()
        parts.append(dot(xs[half * i:half * (i + 1), :], w[...]))
    qkv = jnp.concatenate(parts, axis=0)
    k_rows = qkv[:, HL:2 * HL].astype(BF16)
    q = (qkv[:, 0:HL] * SCALE).T.astype(BF16)
    vt = qkv[:, 2 * HL:].T.astype(BF16)
    keep[0:HL, :] = q
    keep[HL:2 * HL, :] = qkv[:, HL:2 * HL].T.astype(BF16)
    keep[2 * HL:3 * HL, :] = vt
    heads = pltpu.make_async_copy(keep.at[pl.ds(0, 3 * HL)], saved.at[pl.ds(0, 3 * HL)], sems.at[2])
    heads.start()
    dead = jnp.where(xs[:, 0:128].astype(F32)[:, 0:1] < 0.5 * DEAD, 0.0, -jnp.inf)
    ctx = []
    for i in range(3):
        cols = slice(256 * i, 256 * (i + 1))
        scores = dot(k_rows, q[:, cols]) + dead
        top = jnp.max(scores, axis=0, keepdims=True)
        expo = jnp.exp(scores - top)
        total = jnp.sum(expo, axis=0, keepdims=True)
        keep_stats[0:1, cols] = top
        keep_stats[1:2, cols] = total
        ctx.append(dot(vt, (expo / total).astype(BF16)))
    sums = pltpu.make_async_copy(keep_stats, stats, sems.at[3])
    sums.start()
    ctx = jnp.concatenate(ctx, axis=1).astype(BF16)
    out[...] = dot_nt(swap[...], ctx).astype(BF16).reshape(16, CAP, 128) + extra[...]
    send = pltpu.make_async_copy(out, sent, sems.at[4])
    send.start()
    keep[3 * HL:, :] = dot_nt(ctx, swap[...]).astype(BF16)
    last = pltpu.make_async_copy(keep.at[pl.ds(3 * HL, HL)], saved.at[pl.ds(3 * HL, HL)], sems.at[5])
    last.start()
    for copy in (heads, sums, send, last):
        copy.wait()


def attend(*args):
    vmem = pl.BlockSpec(memory_space=pltpu.VMEM)
    hbm = pl.BlockSpec(memory_space=pltpu.HBM)
    return pl.pallas_call(
        attend_body,
        out_shape=[pltpu.HBM((16, CAP, 128), BF16), pltpu.HBM((4 * HL, ROWS), BF16), pltpu.HBM((8, ROWS), F32)],
        in_specs=[vmem] * 3 + [hbm] * 4,
        out_specs=[hbm, hbm, hbm],
        scratch_shapes=[pltpu.VMEM((ROWS, args[0].shape[0]), BF16), pltpu.VMEM((16, CAP, 128), BF16),
                        pltpu.VMEM((4 * HL, ROWS), BF16), pltpu.VMEM((8, ROWS), F32), pltpu.SemaphoreType.DMA((12,))],
        compiler_params=pltpu.CompilerParams(vmem_limit_bytes=24 << 20),
        cost_estimate=pl.CostEstimate(flops=1700 << 20, bytes_accessed=8 << 20, transcendentals=1 << 20),
    )(*args)


def decode_body(came, weights, cot, mask, gain, table, recon, dvis, mixed, grad, w_oe, w_fc, cots, sems):
    loads = [pltpu.make_async_copy(weights.at[:, pl.ds(2 * HID, HP)], w_oe, sems.at[0])]
    loads += [
        pltpu.make_async_copy(
            weights.at[pl.ds(8 * i, 8), pl.ds(0, 2 * HID)], w_fc.at[pl.ds(8 * i, 8)], sems.at[1 + i])
        for i in range(2)]
    up = pltpu.make_async_copy(cot, cots, sems.at[3])
    for copy in (loads[0], up, *loads[1:]):
        copy.start()
    flat = came[...].reshape(16 * CAP, 128)
    vis = jnp.zeros((CAP, DD), F32)
    loads[0].wait()
    for g in range(16):
        vis += dot(came[g, 0:CAP, 0:HP], w_oe[g])
    row = lax.broadcasted_iota(jnp.int32, (CAP, 16 * CAP), 0)
    col = lax.broadcasted_iota(jnp.int32, (CAP, 16 * CAP), 1)
    own = ((col >= 16 * row) & (col < 16 * row + 16)).astype(F32).astype(BF16)
    lane_in = lax.broadcasted_iota(jnp.int32, (128, DD), 0) - HP
    lane_out = lax.broadcasted_iota(jnp.int32, (128, DD), 1)
    repeat = (lane_in == (lane_out & 31)).astype(F32).astype(BF16)
    turn_of = lax.broadcasted_iota(jnp.int32, (16 * CAP, DD), 0) & 15
    piece = lax.shift_right_logical(lax.broadcasted_iota(jnp.int32, (16 * CAP, DD), 1), 5)
    laid = jnp.where(turn_of == piece, dot(flat, repeat), 0.0).astype(BF16)
    vis = (vis + dot(own, laid)).astype(BF16)
    spots = dot((col == 16 * row).astype(F32).astype(BF16), flat)
    lane = lax.broadcasted_iota(jnp.int32, (CAP, 128), 1)
    spot = jnp.sum(jnp.where(lane == HD, spots, 0.0), axis=1, keepdims=True)
    spot = jnp.concatenate([spot, jnp.full((128 - CAP, 1), -1.0, F32)], axis=0)
    vis = jnp.concatenate([vis.astype(F32), jnp.zeros((128 - CAP, DD), F32)], axis=0).astype(BF16)
    where_col = lax.broadcasted_iota(jnp.int32, (128, FDEV), 1).astype(F32)
    picker = (spot == where_col).astype(F32)
    placer = picker.T
    seen = jnp.sum(placer, axis=1, keepdims=True)
    dec_vis = dot(placer.astype(BF16), vis)
    dec_x = jnp.where(seen > 0.5, dec_vis, mask[...].astype(F32)) + table[...]
    mean = jnp.mean(dec_x, axis=-1, keepdims=True)
    centred = dec_x - mean
    var = jnp.mean(centred * centred, axis=-1, keepdims=True)
    inv_std = lax.rsqrt(var + 1e-06)
    normed = centred * inv_std
    dn = (normed * gain[...]).astype(BF16)
    up.wait()
    cot_b = cots[...]
    mixed[...] = dec_x
    for i in range(8):
        if i % 4 == 0:
            loads[1 + i // 4].wait()
        fin = jnp.concatenate([w_fc[2 * i, 0:HID, :], w_fc[2 * i + 1, 0:HID, :]], axis=0)
        fout = jnp.concatenate([w_fc[2 * i, HID:2 * HID, :], w_fc[2 * i + 1, HID:2 * HID, :]], axis=0)
        hidden = dot_nt(dn, fin)
        dact = dot_nt(cot_b, fout)
        cdf = 0.5 * (1.0 + lax.erf(hidden * 0.7071067811865476))
        pdf = jnp.exp(-0.5 * hidden * hidden) * 0.3989422804014327
        act = (hidden * cdf).astype(BF16)
        dhidden = (dact * (cdf + hidden * pdf)).astype(BF16)
        mixed[...] += dot(act, fout)
        if i == 0:
            grad[...] = dot(dhidden, fin)
        else:
            grad[...] += dot(dhidden, fin)
    recon[...] = mixed[...].astype(BF16)
    scaled = grad[...] * gain[...]
    first = jnp.mean(scaled, axis=-1, keepdims=True)
    second = jnp.mean(scaled * normed, axis=-1, keepdims=True)
    ddec = (cot_b.astype(F32) + inv_std * (scaled - first - normed * second)).astype(BF16)
    dvis[...] = dot(picker[0:CAP].astype(BF16), ddec).astype(BF16)


def decode(came, weights, cot, *args):
    vmem = pl.BlockSpec(memory_space=pltpu.VMEM)
    hbm = pl.BlockSpec(memory_space=pltpu.HBM)
    return pl.pallas_call(
        decode_body,
        out_shape=[jax.ShapeDtypeStruct((FDEV, DD), BF16), jax.ShapeDtypeStruct((CAP, DD), BF16)],
        in_specs=[vmem, hbm, hbm] + [vmem] * len(args),
        out_specs=[vmem, vmem],
        scratch_shapes=[pltpu.VMEM((FDEV, DD), F32), pltpu.VMEM((FDEV, DD), F32),
                        pltpu.VMEM((16, HP, DD), BF16), pltpu.VMEM((16, 2 * HID, DD), BF16),
                        pltpu.VMEM((FDEV, DD), BF16), pltpu.SemaphoreType.DMA((4,))],
        compiler_params=pltpu.CompilerParams(vmem_limit_bytes=24 << 20),
        cost_estimate=pl.CostEstimate(flops=2300 << 20, bytes_accessed=8 << 20, transcendentals=1 << 20),
    )(came, pltpu.with_memory_space_constraint(weights, pltpu.HBM),
      pltpu.with_memory_space_constraint(cot, pltpu.HBM), *args)


def back_body(dvis, w_oe, swap, saved, stats, *refs):
    rows_in, (parts, ds_all, pb_all, keep, keep_stats, xs, sems) = refs[:4], refs[4:]
    loads = [
        pltpu.make_async_copy(saved, keep, sems.at[0]),
        pltpu.make_async_copy(stats, keep_stats, sems.at[1])] + row_loads(rows_in, xs, sems, 2)
    for load in loads:
        load.start()
    dctx = dot(dot_nt(w_oe[...], dvis[...]).astype(BF16), swap[...])
    dctx = jnp.concatenate([dctx, jnp.zeros((HL - HP, ROWS), F32)], axis=0).astype(BF16)
    for load in loads:
        load.wait()
    x = xs[...]
    grad_oe = dot(keep[3 * HL:, :], dvis[...])[0:HD]
    q, kt = keep[0:HL, :], keep[HL:2 * HL, :]
    k = kt.astype(F32).T.astype(BF16)
    v = keep[2 * HL:3 * HL, :].astype(F32).T.astype(BF16)
    dead = jnp.where(x[:, 0:128].astype(F32)[:, 0:1] < 0.5 * DEAD, 0.0, -jnp.inf)
    dq = []
    for i in range(3):
        cols = slice(256 * i, 256 * (i + 1))
        scores = dot(k, q[:, cols]) + dead
        probs = jnp.exp(scores - keep_stats[0:1, cols]) / keep_stats[1:2, cols]
        dprob = dot(v, dctx[:, cols])
        inner = jnp.sum(probs * dprob, axis=0, keepdims=True)
        ds = (probs * (dprob - inner)).astype(BF16)
        ds_all[:, cols] = ds
        pb_all[:, cols] = probs.astype(BF16)
        dq.append(dot(kt, ds) * SCALE)
    dq = jnp.concatenate(dq, axis=1)[0:HD]
    dk = dot_nt(q, ds_all[...])[0:HD]
    dv = dot_nt(dctx, pb_all[...])[0:HD]
    dqkv = jnp.concatenate([dq, dk, dv], axis=0).astype(BF16)
    grad = dot(dqkv, x)
    wide = grad.shape[1] // 128
    pieces = [grad[:, 128 * j:128 * (j + 1)] for j in range(wide)]
    pieces += [grad_oe[:, 128 * j:128 * (j + 1)] for j in range(DD // 128)]
    done = sum(p.shape[0] for p in pieces)
    pieces.append(jnp.zeros((GRAD_ROWS - done, 128), F32))
    parts[...] = jnp.concatenate(pieces, axis=0).astype(BF16)


def back(dvis, w_oe, swap, saved, stats, *rows_in):
    vmem = pl.BlockSpec(memory_space=pltpu.VMEM)
    hbm = pl.BlockSpec(memory_space=pltpu.HBM)
    return pl.pallas_call(
        back_body,
        out_shape=jax.ShapeDtypeStruct((GRAD_ROWS, 128), BF16),
        in_specs=[vmem, vmem, vmem] + [hbm] * 6,
        out_specs=vmem,
        scratch_shapes=[pltpu.VMEM((ROWS, ROWS), BF16), pltpu.VMEM((ROWS, ROWS), BF16),
                        pltpu.VMEM((4 * HL, ROWS), BF16), pltpu.VMEM((8, ROWS), F32),
                        pltpu.VMEM((ROWS, rows_in[0].shape[1]), BF16), pltpu.SemaphoreType.DMA((8,))],
        compiler_params=pltpu.CompilerParams(vmem_limit_bytes=24 << 20),
        cost_estimate=pl.CostEstimate(flops=2500 << 20, bytes_accessed=8 << 20, transcendentals=1 << 20),
    )(dvis, w_oe, swap, saved, stats, *rows_in)


def finish_body(total, w_e2d, grad_q, grad_o):
    rows = total[...].astype(F32)
    wide = grad_q.shape[1] // 128
    tall = 3 * HD
    for j in range(wide):
        grad_q[:, 128 * j:128 * (j + 1)] = rows[tall * j:tall * (j + 1)].astype(BF16)
    at = tall * wide
    grad_oe = jnp.concatenate([rows[at + HD * j:at + HD * (j + 1)] for j in range(DD // 128)], axis=1)
    grad_o[...] = dot_nt(grad_oe.astype(BF16), w_e2d[...]).astype(BF16)


def finish(total, w_e2d):
    width = w_e2d.shape[0]
    return call(
        finish_body, [((3 * HD, width), BF16), ((HD, width), BF16)], [], 130 << 20, 12, total, w_e2d)


def position_table(positions, width):
    half = width // 2
    freq = 10000.0 ** (-(jnp.arange(half, dtype=F32) * 2.0 / width))
    angle = positions[:, None] * freq[None, :]
    return jnp.concatenate([jnp.sin(angle), jnp.cos(angle)], axis=1)


def exchange(block, axis):
    return lax.all_to_all(block, axis, 0, 0, tiled=True)


def spread(block, axis):
    return exchange(jnp.broadcast_to(block[None], (lax.axis_size(axis),) + block.shape), axis)


def z_shift(block, step):
    return lax.ppermute(block, "z", [(z, (z + step) % NZ) for z in range(NZ)])


def around(block):
    got = {0: block}
    for step in (1, -1, 2, -2):
        got[step % NZ] = z_shift(block, step)
    got[3] = z_shift(got[2], 1)
    got[5] = z_shift(got[6], -1)
    got[4] = z_shift(got[2], 2)
    return got


def swap_core(block):
    return lax.ppermute(block, "core", [(0, 1), (1, 0)])


def local(
    patches,
    keep_pos,
    kept_counts,
    enc_gain,
    w_qkv,
    w_out,
    w_e2d,
    mask_token,
    dec_gain,
    fc_in,
    fc_out,
    cotangent,
):
    me = lax.axis_index(SEQ)
    my_z, my_c = me // 2, me % 2
    fdev = cotangent.shape[1]
    cot = cotangent[0]
    cap = keep_pos.shape[1]
    rows = 16 * cap

    xn_own, x_slot, offsets = prep(keep_pos, enc_gain, patches[0])
    x_vis, w_oe_own, pack = pack_up(x_slot, w_out, w_e2d, fc_in, fc_out)
    weights = lax.all_gather(pack, SEQ, axis=0)

    places = jnp.repeat(offsets[:, 0].reshape(16, SLOTS), 16, axis=1)[:, :, None]
    extra = jnp.concatenate(
        [jnp.zeros((16, cap, HD), BF16), places, jnp.zeros((16, cap, HP - HD - 1), BF16), x_vis.reshape(16, cap, 32)],
        axis=2)

    tok = jnp.arange(rows, dtype=jnp.int32)
    block = tok // cap
    source = (my_z - block % NZ) % NZ * 2 + (my_c ^ (block // NZ))
    inside = tok % cap
    dest = inside // SLOTS * cap + source * SLOTS + inside % SLOTS
    swap = (dest[None, :] == tok[:, None]).astype(BF16)
    table = position_table((me * fdev + jnp.arange(fdev, dtype=jnp.int32)).astype(F32), DD)

    w = turn(w_qkv.transpose(0, 2, 1).reshape(3 * HD, -1))
    got = around(xn_own)
    got[0], got[5] = lax.optimization_barrier((got[0], got[5]))
    near = join([got[k] for k in (0, 1, 2, 6, 7)])
    near_other = swap_core(near)
    got[4], w, swap, extra, table = lax.optimization_barrier((got[4], w, swap, extra, table))
    far = join([got[k] for k in (3, 4, 5)])
    rows_in = (near, far, near_other, swap_core(far))
    sent, saved, stats = attend(w, swap, extra, *rows_in)
    came = exchange(sent, SEQ)
    recon, dvis_own = decode(came, weights, cot, mask_token[None], dec_gain[None], table)
    dvis = lax.all_gather(dvis_own, SEQ, axis=0, tiled=True)
    parts = back(dvis, w_oe_own, swap, saved, stats, *rows_in)

    parts = jnp.sum(exchange(parts.reshape(NX, 832, 128), "x").astype(F32), axis=0).astype(BF16)
    parts = jnp.sum(exchange(parts.reshape(NY, 104, 128), "y").astype(F32), axis=0).astype(BF16)
    parts = spread(parts, "y").reshape(832, 128)
    total = spread(parts, "x").reshape(GRAD_ROWS, 128)
    grad_q, grad_o = finish(total, w_e2d)
    grad_q = grad_q.reshape(3, HD, -1).transpose(0, 2, 1)
    return (recon[None], grad_q, grad_o)


def solution(mesh):
    axes = Mesh(mesh.devices.reshape(NY, NX, NZ, 2), ("y", "x", "z", "core"))
    dp = ("y", "x")
    placed = (
        P(dp, SEQ, None),
        P(dp, SEQ),
        P(dp, None),
        P(),
        P(None, None, SEQ),
        P(SEQ, None),
        P(),
        P(),
        P(),
        P(SEQ, None),
        P(SEQ, None),
        P(dp, SEQ, None),
    )
    return jax.shard_map(
        local,
        mesh=axes,
        in_specs=placed,
        out_specs=(P(dp, SEQ, None), P(None, None, SEQ), P(SEQ, None)),
        check_vma=False,
    )
```

```python
import jax
import jax.numpy as jnp
from jax import lax
from jax.experimental import pallas as pl
from jax.experimental.pallas import tpu as pltpu
from jax.sharding import Mesh
from jax.sharding import PartitionSpec as P

HD = 88
HP = 96
HL = 128
DD = 512
SEQ = ("z", "core")
NZ = 8
NX = 4
NY = 8
CAP = 48
ROWS = 768
SLOTS = 3
HID = 128
FDEV = 256
DEAD = 1024.0
GRAD_ROWS = 3328
SCALE = HD ** (-0.5)
F32 = jnp.float32
BF16 = jnp.bfloat16


def dot(a, b):
    return jnp.dot(a, b, preferred_element_type=F32)


def dot_nt(a, b):
    return lax.dot_general(a, b, (((1,), (1,)), ((), ())), preferred_element_type=F32)


def layer_norm(values, gain):
    mean = jnp.mean(values, axis=-1, keepdims=True)
    centred = values - mean
    var = jnp.mean(centred * centred, axis=-1, keepdims=True)
    return centred * lax.rsqrt(var + 1e-06) * gain


def call(body, outs, scratch, cost, grant, *args):
    return pl.pallas_call(
        body,
        out_shape=[jax.ShapeDtypeStruct(shape, dtype) for shape, dtype in outs],
        in_specs=[pl.BlockSpec(memory_space=pltpu.VMEM)] * len(args),
        out_specs=[pl.BlockSpec(memory_space=pltpu.VMEM)] * len(outs),
        scratch_shapes=scratch,
        compiler_params=pltpu.CompilerParams(vmem_limit_bytes=grant << 20),
        cost_estimate=pl.CostEstimate(flops=cost, bytes_accessed=8 << 20, transcendentals=1 << 20),
    )(*args)


def prep_body(keep, gain, patches, xn, x_slot, offsets, keep_in, gain_in, x_in, sems):
    small = pltpu.make_async_copy(keep, keep_in, sems.at[0])
    other = pltpu.make_async_copy(gain, gain_in, sems.at[1])
    fetch = pltpu.make_async_copy(patches, x_in, sems.at[2])
    for copy in (small, fetch, other):
        copy.start()
    small.wait()
    at_row = lax.broadcasted_iota(jnp.int32, (CAP, CAP), 0)
    at_col = lax.broadcasted_iota(jnp.int32, (CAP, CAP), 1)
    own = jnp.broadcast_to(keep_in[...], (CAP, CAP))
    owner = lax.shift_right_arithmetic(own, 8)
    owner_col = jnp.sum(jnp.where(at_row == at_col, owner, 0), axis=1, keepdims=True)
    same = (owner_col == owner) & (at_row < at_col)
    rank = jnp.sum(same.astype(jnp.int32), axis=0, keepdims=True)
    slot = jnp.where(own >= 0, owner * SLOTS + rank, -1)
    pick = at_row == slot
    live = jnp.sum(pick.astype(F32), axis=1, keepdims=True) > 0.5
    spot = jnp.sum(jnp.where(pick, own - owner * FDEV, 0).astype(F32), axis=1, keepdims=True)
    offsets[...] = jnp.broadcast_to(jnp.where(live, spot, -1.0), (CAP, 128)).astype(BF16)
    fetch.wait()
    other.wait()
    rows = dot(pick.astype(F32).astype(BF16), x_in[...])
    x_slot[...] = rows.astype(BF16)
    lane = lax.broadcasted_iota(jnp.int32, rows.shape, 1)
    dead_row = jnp.where(lane == 0, DEAD, 0.0)
    xn[...] = jnp.where(live, layer_norm(rows, gain_in[...].reshape(1, rows.shape[1])), dead_row).astype(BF16)


def prep(keep, gain, patches):
    cap, width = patches.shape
    vmem = pl.BlockSpec(memory_space=pltpu.VMEM)
    return pl.pallas_call(
        prep_body,
        out_shape=[jax.ShapeDtypeStruct((cap, width), BF16), jax.ShapeDtypeStruct((cap, width), BF16),
                   jax.ShapeDtypeStruct((cap, 128), BF16)],
        in_specs=[pl.BlockSpec(memory_space=pltpu.HBM)] * 3,
        out_specs=[vmem] * 3,
        scratch_shapes=[pltpu.VMEM(keep.shape, keep.dtype), pltpu.VMEM(gain.shape, F32),
                        pltpu.VMEM((cap, width), BF16), pltpu.SemaphoreType.DMA((3,))],
        compiler_params=pltpu.CompilerParams(vmem_limit_bytes=8 << 20),
        cost_estimate=pl.CostEstimate(flops=10 << 20, bytes_accessed=1 << 19, transcendentals=0),
    )(*[pltpu.with_memory_space_constraint(arg, pltpu.HBM) for arg in (keep, gain, patches)])


def pack_body(x_slot, w_out, w_e2d, fc_in, fc_out, x_vis, w_oe, pack, out_in, e2d_in, packed, sems):
    loads = [
        pltpu.make_async_copy(w_out, out_in, sems.at[0]),
        pltpu.make_async_copy(w_e2d, e2d_in, sems.at[1]),
        pltpu.make_async_copy(fc_in, packed.at[pl.ds(0, HID)], sems.at[2]),
        pltpu.make_async_copy(fc_out, packed.at[pl.ds(HID, HID)], sems.at[3])]
    for copy in loads:
        copy.start()
    for copy in loads:
        copy.wait()
    both = jnp.concatenate([dot(out_in[...], e2d_in[...]), jnp.zeros((HP - HD, DD), F32)], axis=0).astype(BF16)
    w_oe[...] = both
    packed[2 * HID:, :] = both
    done = pltpu.make_async_copy(packed, pack, sems.at[4])
    done.start()
    x_vis[...] = dot(x_slot[...], e2d_in[...]).astype(BF16)
    done.wait()


def pack_up(x_slot, *args):
    width = x_slot.shape[1]
    vmem = pl.BlockSpec(memory_space=pltpu.VMEM)
    hbm = pl.BlockSpec(memory_space=pltpu.HBM)
    return pl.pallas_call(
        pack_body,
        out_shape=[jax.ShapeDtypeStruct((CAP, DD), BF16), jax.ShapeDtypeStruct((HP, DD), BF16),
                   pltpu.HBM((2 * HID + HP, DD), BF16)],
        in_specs=[vmem] + [hbm] * len(args),
        out_specs=[vmem, vmem, hbm],
        scratch_shapes=[pltpu.VMEM((HD, width), BF16), pltpu.VMEM((width, DD), BF16),
                        pltpu.VMEM((2 * HID + HP, DD), BF16), pltpu.SemaphoreType.DMA((5,))],
        compiler_params=pltpu.CompilerParams(vmem_limit_bytes=12 << 20),
        cost_estimate=pl.CostEstimate(flops=200 << 20, bytes_accessed=3 << 20, transcendentals=0),
    )(x_slot, *[pltpu.with_memory_space_constraint(arg, pltpu.HBM) for arg in args])


def turn_body(w_t, w):
    rows = w_t[...].astype(F32)
    gap = jnp.zeros((HL - HD, rows.shape[1]), F32)
    heads = [part for i in range(3) for part in (rows[HD * i:HD * (i + 1)], gap)]
    w[...] = jnp.concatenate(heads, axis=0).T.astype(BF16)


def turn(w_t):
    return call(turn_body, [((w_t.shape[1], 3 * HL), BF16)], [], 1 << 20, 16, w_t)[0]


def join_body(*refs):
    count = len(refs) - 2
    blocks, out, sems = refs[:count], refs[count], refs[count + 1]
    copies = [pltpu.make_async_copy(blocks[k], out.at[pl.ds(CAP * k, CAP)], sems.at[k]) for k in range(count)]
    for copy in copies:
        copy.start()
    for copy in copies:
        copy.wait()


def join(blocks):
    rows, width = blocks[0].shape
    return pl.pallas_call(
        join_body,
        out_shape=jax.ShapeDtypeStruct((len(blocks) * rows, width), blocks[0].dtype),
        in_specs=[pl.BlockSpec(memory_space=pl.ANY)] * len(blocks),
        out_specs=pl.BlockSpec(memory_space=pl.ANY),
        scratch_shapes=[pltpu.SemaphoreType.DMA((len(blocks),))],
        compiler_params=pltpu.CompilerParams(vmem_limit_bytes=4 << 20),
        cost_estimate=pl.CostEstimate(flops=0, bytes_accessed=2 << 20, transcendentals=0),
    )(*blocks)


def attend_body(mine, other, w, swap, extra, sent, saved, stats, xs, out, keep, keep_stats, sems):
    half = ROWS // 2
    loads = [
        pltpu.make_async_copy(mine, xs.at[pl.ds(0, half)], sems.at[0]),
        pltpu.make_async_copy(other, xs.at[pl.ds(half, half)], sems.at[1])]
    for load in loads:
        load.start()
    parts = []
    for i in range(2):
        loads[i].wait()
        parts.append(dot(xs[half * i:half * (i + 1), :], w[...]))
    qkv = jnp.concatenate(parts, axis=0)
    k_rows = qkv[:, HL:2 * HL].astype(BF16)
    q = (qkv[:, 0:HL] * SCALE).T.astype(BF16)
    vt = qkv[:, 2 * HL:].T.astype(BF16)
    keep[0:HL, :] = q
    keep[HL:2 * HL, :] = qkv[:, HL:2 * HL].T.astype(BF16)
    keep[2 * HL:3 * HL, :] = vt
    heads = pltpu.make_async_copy(keep.at[pl.ds(0, 3 * HL)], saved.at[pl.ds(0, 3 * HL)], sems.at[2])
    heads.start()
    dead = jnp.where(xs[:, 0:128].astype(F32)[:, 0:1] < 0.5 * DEAD, 0.0, -jnp.inf)
    ctx = []
    for i in range(3):
        cols = slice(256 * i, 256 * (i + 1))
        scores = dot(k_rows, q[:, cols]) + dead
        top = jnp.max(scores, axis=0, keepdims=True)
        expo = jnp.exp(scores - top)
        total = jnp.sum(expo, axis=0, keepdims=True)
        keep_stats[0:1, cols] = top
        keep_stats[1:2, cols] = total
        ctx.append(dot(vt, (expo / total).astype(BF16)))
    sums = pltpu.make_async_copy(keep_stats, stats, sems.at[3])
    sums.start()
    ctx = jnp.concatenate(ctx, axis=1).astype(BF16)
    out[:, 0:CAP, :] = dot_nt(swap[...], ctx).astype(BF16).reshape(16, CAP, 128)
    out[:, CAP:, :] = extra[...]
    send = pltpu.make_async_copy(out, sent, sems.at[4])
    send.start()
    keep[3 * HL:, :] = dot_nt(ctx, swap[...]).astype(BF16)
    last = pltpu.make_async_copy(keep.at[pl.ds(3 * HL, HL)], saved.at[pl.ds(3 * HL, HL)], sems.at[5])
    last.start()
    for copy in (heads, sums, send, last):
        copy.wait()


def attend(*args):
    vmem = pl.BlockSpec(memory_space=pltpu.VMEM)
    hbm = pl.BlockSpec(memory_space=pltpu.HBM)
    return pl.pallas_call(
        attend_body,
        out_shape=[pltpu.HBM((16, 64, 128), BF16), pltpu.HBM((4 * HL, ROWS), BF16), pltpu.HBM((8, ROWS), F32)],
        in_specs=[hbm, hbm, vmem, vmem, vmem],
        out_specs=[hbm, hbm, hbm],
        scratch_shapes=[pltpu.VMEM((ROWS, args[0].shape[1]), BF16), pltpu.VMEM((16, 64, 128), BF16),
                        pltpu.VMEM((4 * HL, ROWS), BF16), pltpu.VMEM((8, ROWS), F32), pltpu.SemaphoreType.DMA((6,))],
        compiler_params=pltpu.CompilerParams(vmem_limit_bytes=24 << 20),
        cost_estimate=pl.CostEstimate(flops=1700 << 20, bytes_accessed=8 << 20, transcendentals=1 << 20),
    )(*args)


def decode_body(came, weights, cot, mask, gain, table, recon, dvis, mixed, grad, w_oe, w_fc, cots, sems):
    loads = [pltpu.make_async_copy(weights.at[:, pl.ds(2 * HID, HP)], w_oe, sems.at[0])]
    loads += [
        pltpu.make_async_copy(
            weights.at[pl.ds(8 * i, 8), pl.ds(0, 2 * HID)], w_fc.at[pl.ds(8 * i, 8)], sems.at[1 + i])
        for i in range(2)]
    up = pltpu.make_async_copy(cot, cots, sems.at[3])
    for copy in (loads[0], up, *loads[1:]):
        copy.start()
    flat = came[...].reshape(16 * 64, 128)
    vis = jnp.zeros((CAP, DD), F32)
    loads[0].wait()
    for g in range(16):
        vis += dot(came[g, 0:CAP, 0:HP], w_oe[g])
    row = lax.broadcasted_iota(jnp.int32, (CAP, 1024), 0)
    col = lax.broadcasted_iota(jnp.int32, (CAP, 1024), 1)
    source = jnp.zeros((CAP, 1024), jnp.int32)
    for g in range(1, 16):
        source += (row >= SLOTS * g).astype(jnp.int32)
    slot = row - SLOTS * source
    base = 64 * source + CAP
    x_part = jnp.concatenate(
        [dot((col == base + 4 * slot + i).astype(F32).astype(BF16), flat) for i in range(4)], axis=1)
    vis = (vis + x_part).astype(BF16)
    spots = dot((col == base + 12).astype(F32).astype(BF16), flat)
    lane = lax.broadcasted_iota(jnp.int32, (CAP, 128), 1)
    spot = jnp.sum(jnp.where(lane == slot[:, 0:128], spots, 0.0), axis=1, keepdims=True)
    spot = jnp.concatenate([spot, jnp.full((128 - CAP, 1), -1.0, F32)], axis=0)
    vis = jnp.concatenate([vis.astype(F32), jnp.zeros((128 - CAP, DD), F32)], axis=0).astype(BF16)
    where_col = lax.broadcasted_iota(jnp.int32, (128, FDEV), 1).astype(F32)
    picker = (spot == where_col).astype(F32)
    placer = picker.T
    seen = jnp.sum(placer, axis=1, keepdims=True)
    dec_vis = dot(placer.astype(BF16), vis)
    dec_x = jnp.where(seen > 0.5, dec_vis, mask[...].astype(F32)) + table[...]
    mean = jnp.mean(dec_x, axis=-1, keepdims=True)
    centred = dec_x - mean
    var = jnp.mean(centred * centred, axis=-1, keepdims=True)
    inv_std = lax.rsqrt(var + 1e-06)
    normed = centred * inv_std
    dn = (normed * gain[...]).astype(BF16)
    up.wait()
    cot_b = cots[...]
    mixed[...] = dec_x
    for i in range(8):
        if i % 4 == 0:
            loads[1 + i // 4].wait()
        fin = jnp.concatenate([w_fc[2 * i, 0:HID, :], w_fc[2 * i + 1, 0:HID, :]], axis=0)
        fout = jnp.concatenate([w_fc[2 * i, HID:2 * HID, :], w_fc[2 * i + 1, HID:2 * HID, :]], axis=0)
        hidden = dot_nt(dn, fin)
        dact = dot_nt(cot_b, fout)
        cdf = 0.5 * (1.0 + lax.erf(hidden * 0.7071067811865476))
        pdf = jnp.exp(-0.5 * hidden * hidden) * 0.3989422804014327
        act = (hidden * cdf).astype(BF16)
        dhidden = (dact * (cdf + hidden * pdf)).astype(BF16)
        mixed[...] += dot(act, fout)
        if i == 0:
            grad[...] = dot(dhidden, fin)
        else:
            grad[...] += dot(dhidden, fin)
    recon[...] = mixed[...].astype(BF16)
    scaled = grad[...] * gain[...]
    first = jnp.mean(scaled, axis=-1, keepdims=True)
    second = jnp.mean(scaled * normed, axis=-1, keepdims=True)
    ddec = (cot_b.astype(F32) + inv_std * (scaled - first - normed * second)).astype(BF16)
    dvis[...] = dot(picker[0:CAP].astype(BF16), ddec).astype(BF16)


def decode(came, weights, cot, *args):
    vmem = pl.BlockSpec(memory_space=pltpu.VMEM)
    hbm = pl.BlockSpec(memory_space=pltpu.HBM)
    return pl.pallas_call(
        decode_body,
        out_shape=[jax.ShapeDtypeStruct((FDEV, DD), BF16), jax.ShapeDtypeStruct((CAP, DD), BF16)],
        in_specs=[vmem, hbm, hbm] + [vmem] * len(args),
        out_specs=[vmem, vmem],
        scratch_shapes=[pltpu.VMEM((FDEV, DD), F32), pltpu.VMEM((FDEV, DD), F32),
                        pltpu.VMEM((16, HP, DD), BF16), pltpu.VMEM((16, 2 * HID, DD), BF16),
                        pltpu.VMEM((FDEV, DD), BF16), pltpu.SemaphoreType.DMA((4,))],
        compiler_params=pltpu.CompilerParams(vmem_limit_bytes=24 << 20),
        cost_estimate=pl.CostEstimate(flops=2300 << 20, bytes_accessed=8 << 20, transcendentals=1 << 20),
    )(came, pltpu.with_memory_space_constraint(weights, pltpu.HBM),
      pltpu.with_memory_space_constraint(cot, pltpu.HBM), *args)


def back_body(dvis, w_oe, swap, saved, stats, mine, other, parts, ds_all, pb_all, keep, keep_stats, xs, sems):
    loads = [
        pltpu.make_async_copy(saved, keep, sems.at[0]),
        pltpu.make_async_copy(stats, keep_stats, sems.at[1]),
        pltpu.make_async_copy(mine, xs.at[pl.ds(0, ROWS // 2)], sems.at[2]),
        pltpu.make_async_copy(other, xs.at[pl.ds(ROWS // 2, ROWS // 2)], sems.at[3])]
    for load in loads:
        load.start()
    dctx = dot(dot_nt(w_oe[...], dvis[...]).astype(BF16), swap[...])
    dctx = jnp.concatenate([dctx, jnp.zeros((HL - HP, ROWS), F32)], axis=0).astype(BF16)
    for load in loads:
        load.wait()
    x = xs[...]
    grad_oe = dot(keep[3 * HL:, :], dvis[...])[0:HD]
    q, kt = keep[0:HL, :], keep[HL:2 * HL, :]
    k = kt.astype(F32).T.astype(BF16)
    v = keep[2 * HL:3 * HL, :].astype(F32).T.astype(BF16)
    dead = jnp.where(x[:, 0:128].astype(F32)[:, 0:1] < 0.5 * DEAD, 0.0, -jnp.inf)
    dq = []
    for i in range(3):
        cols = slice(256 * i, 256 * (i + 1))
        scores = dot(k, q[:, cols]) + dead
        probs = jnp.exp(scores - keep_stats[0:1, cols]) / keep_stats[1:2, cols]
        dprob = dot(v, dctx[:, cols])
        inner = jnp.sum(probs * dprob, axis=0, keepdims=True)
        ds = (probs * (dprob - inner)).astype(BF16)
        ds_all[:, cols] = ds
        pb_all[:, cols] = probs.astype(BF16)
        dq.append(dot(kt, ds) * SCALE)
    dq = jnp.concatenate(dq, axis=1)[0:HD]
    dk = dot_nt(q, ds_all[...])[0:HD]
    dv = dot_nt(dctx, pb_all[...])[0:HD]
    dqkv = jnp.concatenate([dq, dk, dv], axis=0).astype(BF16)
    grad = dot(dqkv, x)
    wide = grad.shape[1] // 128
    pieces = [grad[:, 128 * j:128 * (j + 1)] for j in range(wide)]
    pieces += [grad_oe[:, 128 * j:128 * (j + 1)] for j in range(DD // 128)]
    done = sum(p.shape[0] for p in pieces)
    pieces.append(jnp.zeros((GRAD_ROWS - done, 128), F32))
    parts[...] = jnp.concatenate(pieces, axis=0).astype(BF16)


def back(dvis, w_oe, swap, saved, stats, mine, other):
    vmem = pl.BlockSpec(memory_space=pltpu.VMEM)
    hbm = pl.BlockSpec(memory_space=pltpu.HBM)
    return pl.pallas_call(
        back_body,
        out_shape=jax.ShapeDtypeStruct((GRAD_ROWS, 128), BF16),
        in_specs=[vmem, vmem, vmem, hbm, hbm, hbm, hbm],
        out_specs=vmem,
        scratch_shapes=[pltpu.VMEM((ROWS, ROWS), BF16), pltpu.VMEM((ROWS, ROWS), BF16),
                        pltpu.VMEM((4 * HL, ROWS), BF16), pltpu.VMEM((8, ROWS), F32),
                        pltpu.VMEM((ROWS, mine.shape[1]), BF16), pltpu.SemaphoreType.DMA((4,))],
        compiler_params=pltpu.CompilerParams(vmem_limit_bytes=24 << 20),
        cost_estimate=pl.CostEstimate(flops=2500 << 20, bytes_accessed=8 << 20, transcendentals=1 << 20),
    )(dvis, w_oe, swap, saved, stats, mine, other)


def finish_body(total, w_e2d, grad_q, grad_o):
    rows = total[...].astype(F32)
    wide = grad_q.shape[1] // 128
    tall = 3 * HD
    for j in range(wide):
        grad_q[:, 128 * j:128 * (j + 1)] = rows[tall * j:tall * (j + 1)].astype(BF16)
    at = tall * wide
    grad_oe = jnp.concatenate([rows[at + HD * j:at + HD * (j + 1)] for j in range(DD // 128)], axis=1)
    grad_o[...] = dot_nt(grad_oe.astype(BF16), w_e2d[...]).astype(BF16)


def finish(total, w_e2d):
    width = w_e2d.shape[0]
    return call(
        finish_body, [((3 * HD, width), BF16), ((HD, width), BF16)], [], 130 << 20, 12, total, w_e2d)


def position_table(positions, width):
    half = width // 2
    freq = 10000.0 ** (-(jnp.arange(half, dtype=F32) * 2.0 / width))
    angle = positions[:, None] * freq[None, :]
    return jnp.concatenate([jnp.sin(angle), jnp.cos(angle)], axis=1)


def exchange(block, axis):
    return lax.all_to_all(block, axis, 0, 0, tiled=True)


def spread(block, axis):
    return exchange(jnp.broadcast_to(block[None], (lax.axis_size(axis),) + block.shape), axis)


def z_shift(block, step):
    return lax.ppermute(block, "z", [(z, (z + step) % NZ) for z in range(NZ)])


def around(block):
    got = {0: block}
    for step in (1, -1, 2, -2):
        got[step % NZ] = z_shift(block, step)
    got[3] = z_shift(got[2], 1)
    got[5] = z_shift(got[6], -1)
    got[4] = z_shift(got[2], 2)
    return [got[k] for k in range(NZ)]


def swap_core(block):
    return lax.ppermute(block, "core", [(0, 1), (1, 0)])


def local(
    patches,
    keep_pos,
    kept_counts,
    enc_gain,
    w_qkv,
    w_out,
    w_e2d,
    mask_token,
    dec_gain,
    fc_in,
    fc_out,
    cotangent,
):
    me = lax.axis_index(SEQ)
    fdev = cotangent.shape[1]
    cot = cotangent[0]
    cap = keep_pos.shape[1]
    rows = 16 * cap

    xn_own, x_slot, offsets = prep(keep_pos, enc_gain, patches[0])
    x_vis, w_oe_own, pack = pack_up(x_slot, w_out, w_e2d, fc_in, fc_out)
    weights = lax.all_gather(pack, SEQ, axis=0)

    blocks = around(xn_own)
    blocks[4], spot, x_vis, offsets = lax.optimization_barrier((blocks[4], me, x_vis, offsets))
    my_z, my_c = spot // 2, spot % 2

    places = jnp.pad(offsets[:, 0].reshape(16, 1, SLOTS), ((0, 0), (0, 0), (0, 128 - SLOTS)))
    extra = jnp.concatenate(
        [x_vis.reshape(16, 12, 128), places, jnp.zeros((16, 3, 128), BF16)], axis=1)

    tok = jnp.arange(rows, dtype=jnp.int32)
    block = tok // cap
    source = (my_z - block % NZ) % NZ * 2 + (my_c ^ (block // NZ))
    inside = tok % cap
    dest = inside // SLOTS * cap + source * SLOTS + inside % SLOTS
    swap = (dest[None, :] == tok[:, None]).astype(BF16)
    table = position_table((spot * fdev + jnp.arange(fdev, dtype=jnp.int32)).astype(F32), DD)

    w = turn(w_qkv.transpose(0, 2, 1).reshape(3 * HD, -1))
    mine = join(blocks)
    other = swap_core(mine)
    sent, saved, stats = attend(mine, other, w, swap, extra)
    came = exchange(sent, SEQ)
    recon, dvis_own = decode(came, weights, cot, mask_token[None], dec_gain[None], table)
    dvis = lax.all_gather(dvis_own, SEQ, axis=0, tiled=True)
    parts = back(dvis, w_oe_own, swap, saved, stats, mine, other)

    parts = jnp.sum(exchange(parts.reshape(NX, 832, 128), "x").astype(F32), axis=0).astype(BF16)
    parts = jnp.sum(exchange(parts.reshape(NY, 104, 128), "y").astype(F32), axis=0).astype(BF16)
    parts = spread(parts, "y").reshape(832, 128)
    total = spread(parts, "x").reshape(GRAD_ROWS, 128)
    grad_q, grad_o = finish(total, w_e2d)
    grad_q = grad_q.reshape(3, HD, -1).transpose(0, 2, 1)
    return (recon[None], grad_q, grad_o)


def solution(mesh):
    axes = Mesh(mesh.devices.reshape(NY, NX, NZ, 2), ("y", "x", "z", "core"))
    dp = ("y", "x")
    placed = (
        P(dp, SEQ, None),
        P(dp, SEQ),
        P(dp, None),
        P(),
        P(None, None, SEQ),
        P(SEQ, None),
        P(),
        P(),
        P(),
        P(SEQ, None),
        P(SEQ, None),
        P(dp, SEQ, None),
    )
    return jax.shard_map(
        local,
        mesh=axes,
        in_specs=placed,
        out_specs=(P(dp, SEQ, None), P(None, None, SEQ), P(SEQ, None)),
        check_vma=False,
    )
```

```python
import functools

import jax
import jax.numpy as jnp
from jax import lax
from jax.experimental import pallas as pl
from jax.experimental.pallas import tpu as pltpu
from jax.sharding import Mesh
from jax.sharding import PartitionSpec as P

HD = 88
HP = 96
HL = 128
DD = 512
SEQ = ("z", "core")
NZ = 8
NX = 4
NY = 8
CAP = 48
ROWS = 768
SLOTS = 3
HID = 128
FDEV = 256
DEAD = 1024.0
GRAD_ROWS = 3328
SCALE = HD ** (-0.5)
F32 = jnp.float32
BF16 = jnp.bfloat16


def dot(a, b):
    return jnp.dot(a, b, preferred_element_type=F32)


def dot_nt(a, b):
    return lax.dot_general(a, b, (((1,), (1,)), ((), ())), preferred_element_type=F32)


def layer_norm(values, gain):
    mean = jnp.mean(values, axis=-1, keepdims=True)
    centred = values - mean
    var = jnp.mean(centred * centred, axis=-1, keepdims=True)
    return centred * lax.rsqrt(var + 1e-06) * gain


def call(body, outs, scratch, cost, grant, *args):
    return pl.pallas_call(
        body,
        out_shape=[jax.ShapeDtypeStruct(shape, dtype) for shape, dtype in outs],
        in_specs=[pl.BlockSpec(memory_space=pltpu.VMEM)] * len(args),
        out_specs=[pl.BlockSpec(memory_space=pltpu.VMEM)] * len(outs),
        scratch_shapes=scratch,
        compiler_params=pltpu.CompilerParams(vmem_limit_bytes=grant << 20),
        cost_estimate=pl.CostEstimate(flops=cost, bytes_accessed=8 << 20, transcendentals=1 << 20),
    )(*args)


def prep_body(keep, gain, patches, xn, x_slot, offsets, keep_in, gain_in, x_in, sems):
    small = pltpu.make_async_copy(keep, keep_in, sems.at[0])
    other = pltpu.make_async_copy(gain, gain_in, sems.at[1])
    fetch = pltpu.make_async_copy(patches, x_in, sems.at[2])
    for copy in (small, fetch, other):
        copy.start()
    small.wait()
    at_row = lax.broadcasted_iota(jnp.int32, (CAP, CAP), 0)
    at_col = lax.broadcasted_iota(jnp.int32, (CAP, CAP), 1)
    own = jnp.broadcast_to(keep_in[...], (CAP, CAP))
    owner = lax.shift_right_arithmetic(own, 8)
    owner_col = jnp.sum(jnp.where(at_row == at_col, owner, 0), axis=1, keepdims=True)
    same = (owner_col == owner) & (at_row < at_col)
    rank = jnp.sum(same.astype(jnp.int32), axis=0, keepdims=True)
    slot = jnp.where(own >= 0, owner * SLOTS + rank, -1)
    pick = at_row == slot
    live = jnp.sum(pick.astype(F32), axis=1, keepdims=True) > 0.5
    spot = jnp.sum(jnp.where(pick, own - owner * FDEV, 0).astype(F32), axis=1, keepdims=True)
    offsets[...] = jnp.broadcast_to(jnp.where(live, spot, -1.0), (CAP, 128)).astype(BF16)
    fetch.wait()
    other.wait()
    rows = dot(pick.astype(F32).astype(BF16), x_in[...])
    x_slot[...] = rows.astype(BF16)
    lane = lax.broadcasted_iota(jnp.int32, rows.shape, 1)
    dead_row = jnp.where(lane == 0, DEAD, 0.0)
    xn[...] = jnp.where(live, layer_norm(rows, gain_in[...].reshape(1, rows.shape[1])), dead_row).astype(BF16)


def prep(keep, gain, patches):
    cap, width = patches.shape
    vmem = pl.BlockSpec(memory_space=pltpu.VMEM)
    return pl.pallas_call(
        prep_body,
        out_shape=[jax.ShapeDtypeStruct((cap, width), BF16), jax.ShapeDtypeStruct((cap, width), BF16),
                   jax.ShapeDtypeStruct((cap, 128), BF16)],
        in_specs=[pl.BlockSpec(memory_space=pltpu.HBM)] * 3,
        out_specs=[vmem] * 3,
        scratch_shapes=[pltpu.VMEM(keep.shape, keep.dtype), pltpu.VMEM(gain.shape, F32),
                        pltpu.VMEM((cap, width), BF16), pltpu.SemaphoreType.DMA((3,))],
        compiler_params=pltpu.CompilerParams(vmem_limit_bytes=8 << 20),
        cost_estimate=pl.CostEstimate(flops=10 << 20, bytes_accessed=1 << 19, transcendentals=0),
    )(*[pltpu.with_memory_space_constraint(arg, pltpu.HBM) for arg in (keep, gain, patches)])


def pack_body(x_slot, w_out, w_e2d, fc_in, fc_out, x_vis, w_oe, pack, out_in, e2d_in, packed, sems):
    loads = [
        pltpu.make_async_copy(w_out, out_in, sems.at[0]),
        pltpu.make_async_copy(w_e2d, e2d_in, sems.at[1]),
        pltpu.make_async_copy(fc_in, packed.at[pl.ds(0, HID)], sems.at[2]),
        pltpu.make_async_copy(fc_out, packed.at[pl.ds(HID, HID)], sems.at[3])]
    for copy in loads:
        copy.start()
    for copy in loads:
        copy.wait()
    both = jnp.concatenate([dot(out_in[...], e2d_in[...]), jnp.zeros((HP - HD, DD), F32)], axis=0).astype(BF16)
    w_oe[...] = both
    packed[2 * HID:, :] = both
    done = pltpu.make_async_copy(packed, pack, sems.at[4])
    done.start()
    x_vis[...] = dot(x_slot[...], e2d_in[...]).astype(BF16)
    done.wait()


def pack_up(x_slot, *args):
    width = x_slot.shape[1]
    vmem = pl.BlockSpec(memory_space=pltpu.VMEM)
    hbm = pl.BlockSpec(memory_space=pltpu.HBM)
    return pl.pallas_call(
        pack_body,
        out_shape=[jax.ShapeDtypeStruct((CAP, DD), BF16), jax.ShapeDtypeStruct((HP, DD), BF16),
                   pltpu.HBM((2 * HID + HP, DD), BF16)],
        in_specs=[vmem] + [hbm] * len(args),
        out_specs=[vmem, vmem, hbm],
        scratch_shapes=[pltpu.VMEM((HD, width), BF16), pltpu.VMEM((width, DD), BF16),
                        pltpu.VMEM((2 * HID + HP, DD), BF16), pltpu.SemaphoreType.DMA((5,))],
        compiler_params=pltpu.CompilerParams(vmem_limit_bytes=12 << 20),
        cost_estimate=pl.CostEstimate(flops=200 << 20, bytes_accessed=3 << 20, transcendentals=0),
    )(x_slot, *[pltpu.with_memory_space_constraint(arg, pltpu.HBM) for arg in args])


def turn_body(w_t, w):
    rows = w_t[...].astype(F32)
    gap = jnp.zeros((HL - HD, rows.shape[1]), F32)
    heads = [part for i in range(3) for part in (rows[HD * i:HD * (i + 1)], gap)]
    w[...] = jnp.concatenate(heads, axis=0).T.astype(BF16)


def turn(w_t):
    return call(turn_body, [((w_t.shape[1], 3 * HL), BF16)], [], 1 << 20, 16, w_t)[0]


def join_body(places, *refs):
    blocks, out, sems = refs[:len(places)], refs[len(places)], refs[len(places) + 1]
    copies = []
    for i, (k, column) in enumerate(places):
        rows, width = blocks[i].shape
        part = out.at[pl.ds(rows * k, rows), pl.ds(column, width)]
        copies.append(pltpu.make_async_copy(blocks[i], part, sems.at[i]))
    for copy in copies:
        copy.start()
    for copy in copies:
        copy.wait()


def join(blocks):
    places = []
    for k, parts in enumerate(blocks):
        column = 0
        for part in parts:
            places.append((k, column))
            column += part.shape[1]
    flat = [part for parts in blocks for part in parts]
    return pl.pallas_call(
        functools.partial(join_body, places),
        out_shape=jax.ShapeDtypeStruct((NZ * flat[0].shape[0], flat[0].shape[1]), flat[0].dtype),
        in_specs=[pl.BlockSpec(memory_space=pl.ANY)] * len(flat),
        out_specs=pl.BlockSpec(memory_space=pl.ANY),
        scratch_shapes=[pltpu.SemaphoreType.DMA((len(flat),))],
        compiler_params=pltpu.CompilerParams(vmem_limit_bytes=4 << 20),
        cost_estimate=pl.CostEstimate(flops=0, bytes_accessed=4 << 20, transcendentals=0),
    )(*flat)


def attend_body(mine, other, w, swap, extra, sent, saved, stats, xs, out, keep, keep_stats, sems):
    half = ROWS // 2
    loads = [
        pltpu.make_async_copy(mine, xs.at[pl.ds(0, half)], sems.at[0]),
        pltpu.make_async_copy(other, xs.at[pl.ds(half, half)], sems.at[1])]
    for load in loads:
        load.start()
    parts = []
    for i in range(2):
        loads[i].wait()
        parts.append(dot(xs[half * i:half * (i + 1), :], w[...]))
    qkv = jnp.concatenate(parts, axis=0)
    k_rows = qkv[:, HL:2 * HL].astype(BF16)
    q = (qkv[:, 0:HL] * SCALE).T.astype(BF16)
    vt = qkv[:, 2 * HL:].T.astype(BF16)
    keep[0:HL, :] = q
    keep[HL:2 * HL, :] = qkv[:, HL:2 * HL].T.astype(BF16)
    keep[2 * HL:3 * HL, :] = vt
    heads = pltpu.make_async_copy(keep.at[pl.ds(0, 3 * HL)], saved.at[pl.ds(0, 3 * HL)], sems.at[2])
    heads.start()
    dead = jnp.where(xs[:, 0:128].astype(F32)[:, 0:1] < 0.5 * DEAD, 0.0, -jnp.inf)
    ctx = []
    for i in range(3):
        cols = slice(256 * i, 256 * (i + 1))
        scores = dot(k_rows, q[:, cols]) + dead
        top = jnp.max(scores, axis=0, keepdims=True)
        expo = jnp.exp(scores - top)
        total = jnp.sum(expo, axis=0, keepdims=True)
        keep_stats[0:1, cols] = top
        keep_stats[1:2, cols] = total
        ctx.append(dot(vt, (expo / total).astype(BF16)))
    sums = pltpu.make_async_copy(keep_stats, stats, sems.at[3])
    sums.start()
    ctx = jnp.concatenate(ctx, axis=1).astype(BF16)
    out[:, 0:CAP, :] = dot_nt(swap[...], ctx).astype(BF16).reshape(16, CAP, 128)
    out[:, CAP:, :] = extra[...]
    send = pltpu.make_async_copy(out, sent, sems.at[4])
    send.start()
    keep[3 * HL:, :] = dot_nt(ctx, swap[...]).astype(BF16)
    last = pltpu.make_async_copy(keep.at[pl.ds(3 * HL, HL)], saved.at[pl.ds(3 * HL, HL)], sems.at[5])
    last.start()
    for copy in (heads, sums, send, last):
        copy.wait()


def attend(*args):
    vmem = pl.BlockSpec(memory_space=pltpu.VMEM)
    hbm = pl.BlockSpec(memory_space=pltpu.HBM)
    return pl.pallas_call(
        attend_body,
        out_shape=[pltpu.HBM((16, 64, 128), BF16), pltpu.HBM((4 * HL, ROWS), BF16), pltpu.HBM((8, ROWS), F32)],
        in_specs=[hbm, hbm, vmem, vmem, vmem],
        out_specs=[hbm, hbm, hbm],
        scratch_shapes=[pltpu.VMEM((ROWS, args[0].shape[1]), BF16), pltpu.VMEM((16, 64, 128), BF16),
                        pltpu.VMEM((4 * HL, ROWS), BF16), pltpu.VMEM((8, ROWS), F32), pltpu.SemaphoreType.DMA((6,))],
        compiler_params=pltpu.CompilerParams(vmem_limit_bytes=24 << 20),
        cost_estimate=pl.CostEstimate(flops=1700 << 20, bytes_accessed=8 << 20, transcendentals=1 << 20),
    )(*args)


def decode_body(came, weights, cot, mask, gain, table, recon, dvis, mixed, grad, w_oe, w_fc, cots, sems):
    loads = [pltpu.make_async_copy(weights.at[:, pl.ds(2 * HID, HP)], w_oe, sems.at[0])]
    loads += [
        pltpu.make_async_copy(
            weights.at[pl.ds(8 * i, 8), pl.ds(0, 2 * HID)], w_fc.at[pl.ds(8 * i, 8)], sems.at[1 + i])
        for i in range(2)]
    up = pltpu.make_async_copy(cot, cots, sems.at[3])
    for copy in (loads[0], up, *loads[1:]):
        copy.start()
    flat = came[...].reshape(16 * 64, 128)
    vis = jnp.zeros((CAP, DD), F32)
    loads[0].wait()
    for g in range(16):
        vis += dot(came[g, 0:CAP, 0:HP], w_oe[g])
    row = lax.broadcasted_iota(jnp.int32, (CAP, 1024), 0)
    col = lax.broadcasted_iota(jnp.int32, (CAP, 1024), 1)
    source = jnp.zeros((CAP, 1024), jnp.int32)
    for g in range(1, 16):
        source += (row >= SLOTS * g).astype(jnp.int32)
    slot = row - SLOTS * source
    base = 64 * source + CAP
    x_part = jnp.concatenate(
        [dot((col == base + 4 * slot + i).astype(F32).astype(BF16), flat) for i in range(4)], axis=1)
    vis = (vis + x_part).astype(BF16)
    spots = dot((col == base + 12).astype(F32).astype(BF16), flat)
    lane = lax.broadcasted_iota(jnp.int32, (CAP, 128), 1)
    spot = jnp.sum(jnp.where(lane == slot[:, 0:128], spots, 0.0), axis=1, keepdims=True)
    spot = jnp.concatenate([spot, jnp.full((128 - CAP, 1), -1.0, F32)], axis=0)
    vis = jnp.concatenate([vis.astype(F32), jnp.zeros((128 - CAP, DD), F32)], axis=0).astype(BF16)
    where_col = lax.broadcasted_iota(jnp.int32, (128, FDEV), 1).astype(F32)
    picker = (spot == where_col).astype(F32)
    placer = picker.T
    seen = jnp.sum(placer, axis=1, keepdims=True)
    dec_vis = dot(placer.astype(BF16), vis)
    dec_x = jnp.where(seen > 0.5, dec_vis, mask[...].astype(F32)) + table[...]
    mean = jnp.mean(dec_x, axis=-1, keepdims=True)
    centred = dec_x - mean
    var = jnp.mean(centred * centred, axis=-1, keepdims=True)
    inv_std = lax.rsqrt(var + 1e-06)
    normed = centred * inv_std
    dn = (normed * gain[...]).astype(BF16)
    up.wait()
    cot_b = cots[...]
    mixed[...] = dec_x
    for i in range(8):
        if i % 4 == 0:
            loads[1 + i // 4].wait()
        fin = jnp.concatenate([w_fc[2 * i, 0:HID, :], w_fc[2 * i + 1, 0:HID, :]], axis=0)
        fout = jnp.concatenate([w_fc[2 * i, HID:2 * HID, :], w_fc[2 * i + 1, HID:2 * HID, :]], axis=0)
        hidden = dot_nt(dn, fin)
        dact = dot_nt(cot_b, fout)
        cdf = 0.5 * (1.0 + lax.erf(hidden * 0.7071067811865476))
        pdf = jnp.exp(-0.5 * hidden * hidden) * 0.3989422804014327
        act = (hidden * cdf).astype(BF16)
        dhidden = (dact * (cdf + hidden * pdf)).astype(BF16)
        mixed[...] += dot(act, fout)
        if i == 0:
            grad[...] = dot(dhidden, fin)
        else:
            grad[...] += dot(dhidden, fin)
    recon[...] = mixed[...].astype(BF16)
    scaled = grad[...] * gain[...]
    first = jnp.mean(scaled, axis=-1, keepdims=True)
    second = jnp.mean(scaled * normed, axis=-1, keepdims=True)
    ddec = (cot_b.astype(F32) + inv_std * (scaled - first - normed * second)).astype(BF16)
    dvis[...] = dot(picker[0:CAP].astype(BF16), ddec).astype(BF16)


def decode(came, weights, cot, *args):
    vmem = pl.BlockSpec(memory_space=pltpu.VMEM)
    hbm = pl.BlockSpec(memory_space=pltpu.HBM)
    return pl.pallas_call(
        decode_body,
        out_shape=[jax.ShapeDtypeStruct((FDEV, DD), BF16), jax.ShapeDtypeStruct((CAP, DD), BF16)],
        in_specs=[vmem, hbm, hbm] + [vmem] * len(args),
        out_specs=[vmem, vmem],
        scratch_shapes=[pltpu.VMEM((FDEV, DD), F32), pltpu.VMEM((FDEV, DD), F32),
                        pltpu.VMEM((16, HP, DD), BF16), pltpu.VMEM((16, 2 * HID, DD), BF16),
                        pltpu.VMEM((FDEV, DD), BF16), pltpu.SemaphoreType.DMA((4,))],
        compiler_params=pltpu.CompilerParams(vmem_limit_bytes=24 << 20),
        cost_estimate=pl.CostEstimate(flops=2300 << 20, bytes_accessed=8 << 20, transcendentals=1 << 20),
    )(came, pltpu.with_memory_space_constraint(weights, pltpu.HBM),
      pltpu.with_memory_space_constraint(cot, pltpu.HBM), *args)


def back_body(dvis, w_oe, swap, saved, stats, mine, other, parts, ds_all, pb_all, keep, keep_stats, xs, sems):
    loads = [
        pltpu.make_async_copy(saved, keep, sems.at[0]),
        pltpu.make_async_copy(stats, keep_stats, sems.at[1]),
        pltpu.make_async_copy(mine, xs.at[pl.ds(0, ROWS // 2)], sems.at[2]),
        pltpu.make_async_copy(other, xs.at[pl.ds(ROWS // 2, ROWS // 2)], sems.at[3])]
    for load in loads:
        load.start()
    dctx = dot(dot_nt(w_oe[...], dvis[...]).astype(BF16), swap[...])
    dctx = jnp.concatenate([dctx, jnp.zeros((HL - HP, ROWS), F32)], axis=0).astype(BF16)
    for load in loads:
        load.wait()
    x = xs[...]
    grad_oe = dot(keep[3 * HL:, :], dvis[...])[0:HD]
    q, kt = keep[0:HL, :], keep[HL:2 * HL, :]
    k = kt.astype(F32).T.astype(BF16)
    v = keep[2 * HL:3 * HL, :].astype(F32).T.astype(BF16)
    dead = jnp.where(x[:, 0:128].astype(F32)[:, 0:1] < 0.5 * DEAD, 0.0, -jnp.inf)
    dq = []
    for i in range(3):
        cols = slice(256 * i, 256 * (i + 1))
        scores = dot(k, q[:, cols]) + dead
        probs = jnp.exp(scores - keep_stats[0:1, cols]) / keep_stats[1:2, cols]
        dprob = dot(v, dctx[:, cols])
        inner = jnp.sum(probs * dprob, axis=0, keepdims=True)
        ds = (probs * (dprob - inner)).astype(BF16)
        ds_all[:, cols] = ds
        pb_all[:, cols] = probs.astype(BF16)
        dq.append(dot(kt, ds) * SCALE)
    dq = jnp.concatenate(dq, axis=1)[0:HD]
    dk = dot_nt(q, ds_all[...])[0:HD]
    dv = dot_nt(dctx, pb_all[...])[0:HD]
    dqkv = jnp.concatenate([dq, dk, dv], axis=0).astype(BF16)
    grad = dot(dqkv, x)
    wide = grad.shape[1] // 128
    pieces = [grad[:, 128 * j:128 * (j + 1)] for j in range(wide)]
    pieces += [grad_oe[:, 128 * j:128 * (j + 1)] for j in range(DD // 128)]
    done = sum(p.shape[0] for p in pieces)
    pieces.append(jnp.zeros((GRAD_ROWS - done, 128), F32))
    parts[...] = jnp.concatenate(pieces, axis=0).astype(BF16)


def back(dvis, w_oe, swap, saved, stats, mine, other):
    vmem = pl.BlockSpec(memory_space=pltpu.VMEM)
    hbm = pl.BlockSpec(memory_space=pltpu.HBM)
    return pl.pallas_call(
        back_body,
        out_shape=jax.ShapeDtypeStruct((GRAD_ROWS, 128), BF16),
        in_specs=[vmem, vmem, vmem, hbm, hbm, hbm, hbm],
        out_specs=vmem,
        scratch_shapes=[pltpu.VMEM((ROWS, ROWS), BF16), pltpu.VMEM((ROWS, ROWS), BF16),
                        pltpu.VMEM((4 * HL, ROWS), BF16), pltpu.VMEM((8, ROWS), F32),
                        pltpu.VMEM((ROWS, mine.shape[1]), BF16), pltpu.SemaphoreType.DMA((4,))],
        compiler_params=pltpu.CompilerParams(vmem_limit_bytes=24 << 20),
        cost_estimate=pl.CostEstimate(flops=2500 << 20, bytes_accessed=8 << 20, transcendentals=1 << 20),
    )(dvis, w_oe, swap, saved, stats, mine, other)


def finish_body(total, w_e2d, grad_q, grad_o):
    rows = total[...].astype(F32)
    wide = grad_q.shape[1] // 128
    tall = 3 * HD
    for j in range(wide):
        grad_q[:, 128 * j:128 * (j + 1)] = rows[tall * j:tall * (j + 1)].astype(BF16)
    at = tall * wide
    grad_oe = jnp.concatenate([rows[at + HD * j:at + HD * (j + 1)] for j in range(DD // 128)], axis=1)
    grad_o[...] = dot_nt(grad_oe.astype(BF16), w_e2d[...]).astype(BF16)


def finish(total, w_e2d):
    width = w_e2d.shape[0]
    return call(
        finish_body, [((3 * HD, width), BF16), ((HD, width), BF16)], [], 130 << 20, 12, total, w_e2d)


def position_table(positions, width):
    half = width // 2
    freq = 10000.0 ** (-(jnp.arange(half, dtype=F32) * 2.0 / width))
    angle = positions[:, None] * freq[None, :]
    return jnp.concatenate([jnp.sin(angle), jnp.cos(angle)], axis=1)


def exchange(block, axis):
    return lax.all_to_all(block, axis, 0, 0, tiled=True)


def spread(block, axis):
    return exchange(jnp.broadcast_to(block[None], (lax.axis_size(axis),) + block.shape), axis)


def z_shift(block, step):
    return lax.ppermute(block, "z", [(z, (z + step) % NZ) for z in range(NZ)])


def around(block):
    got = {0: block}
    for step in (1, -1, 2, -2):
        got[step % NZ] = z_shift(block, step)
    got[3] = z_shift(got[2], 1)
    got[5] = z_shift(got[6], -1)
    got[4] = z_shift(got[2], 2)
    return [[got[k]] for k in range(NZ)]


def swap_core(block):
    return lax.ppermute(block, "core", [(0, 1), (1, 0)])


def local(
    patches,
    keep_pos,
    kept_counts,
    enc_gain,
    w_qkv,
    w_out,
    w_e2d,
    mask_token,
    dec_gain,
    fc_in,
    fc_out,
    cotangent,
):
    me = lax.axis_index(SEQ)
    my_z, my_c = me // 2, me % 2
    fdev = cotangent.shape[1]
    cot = cotangent[0]
    cap = keep_pos.shape[1]
    rows = 16 * cap

    xn_own, x_slot, offsets = prep(keep_pos, enc_gain, patches[0])
    x_vis, w_oe_own, pack = pack_up(x_slot, w_out, w_e2d, fc_in, fc_out)
    weights = lax.all_gather(pack, SEQ, axis=0)

    places = jnp.pad(offsets[:, 0].reshape(16, 1, SLOTS), ((0, 0), (0, 0), (0, 128 - SLOTS)))
    extra = jnp.concatenate(
        [x_vis.reshape(16, 12, 128), places, jnp.zeros((16, 3, 128), BF16)], axis=1)

    tok = jnp.arange(rows, dtype=jnp.int32)
    block = tok // cap
    source = (my_z - block % NZ) % NZ * 2 + (my_c ^ (block // NZ))
    inside = tok % cap
    dest = inside // SLOTS * cap + source * SLOTS + inside % SLOTS
    swap = (dest[None, :] == tok[:, None]).astype(BF16)
    table = position_table((me * fdev + jnp.arange(fdev, dtype=jnp.int32)).astype(F32), DD)

    w = turn(w_qkv.transpose(0, 2, 1).reshape(3 * HD, -1))
    blocks = around(xn_own)
    blocks[4][0], w, swap, extra = lax.optimization_barrier((blocks[4][0], w, swap, extra))
    mine = join(blocks)
    other = swap_core(mine)
    sent, saved, stats = attend(mine, other, w, swap, extra)
    came = exchange(sent, SEQ)
    recon, dvis_own = decode(came, weights, cot, mask_token[None], dec_gain[None], table)
    dvis = lax.all_gather(dvis_own, SEQ, axis=0, tiled=True)
    parts = back(dvis, w_oe_own, swap, saved, stats, mine, other)

    parts = jnp.sum(exchange(parts.reshape(NX, 832, 128), "x").astype(F32), axis=0).astype(BF16)
    parts = jnp.sum(exchange(parts.reshape(NY, 104, 128), "y").astype(F32), axis=0).astype(BF16)
    parts = spread(parts, "y").reshape(832, 128)
    total = spread(parts, "x").reshape(GRAD_ROWS, 128)
    grad_q, grad_o = finish(total, w_e2d)
    grad_q = grad_q.reshape(3, HD, -1).transpose(0, 2, 1)
    return (recon[None], grad_q, grad_o)


def solution(mesh):
    axes = Mesh(mesh.devices.reshape(NY, NX, NZ, 2), ("y", "x", "z", "core"))
    dp = ("y", "x")
    placed = (
        P(dp, SEQ, None),
        P(dp, SEQ),
        P(dp, None),
        P(),
        P(None, None, SEQ),
        P(SEQ, None),
        P(),
        P(),
        P(),
        P(SEQ, None),
        P(SEQ, None),
        P(dp, SEQ, None),
    )
    return jax.shard_map(
        local,
        mesh=axes,
        in_specs=placed,
        out_specs=(P(dp, SEQ, None), P(None, None, SEQ), P(SEQ, None)),
        check_vma=False,
    )
```

```python
import functools

import jax
import jax.numpy as jnp
from jax import lax
from jax.experimental import pallas as pl
from jax.experimental.pallas import tpu as pltpu
from jax.sharding import Mesh
from jax.sharding import PartitionSpec as P

HD = 88
HP = 96
HL = 128
CUT = 768
DD = 512
SEQ = ("z", "core")
NZ = 8
NX = 4
NY = 8
CAP = 48
ROWS = 768
SLOTS = 3
HID = 128
FDEV = 256
DEAD = 1024.0
GRAD_ROWS = 3328
SCALE = HD ** (-0.5)
F32 = jnp.float32
BF16 = jnp.bfloat16


def dot(a, b):
    return jnp.dot(a, b, preferred_element_type=F32)


def dot_nt(a, b):
    return lax.dot_general(a, b, (((1,), (1,)), ((), ())), preferred_element_type=F32)


def layer_norm(values, gain):
    mean = jnp.mean(values, axis=-1, keepdims=True)
    centred = values - mean
    var = jnp.mean(centred * centred, axis=-1, keepdims=True)
    return centred * lax.rsqrt(var + 1e-06) * gain


def call(body, outs, scratch, cost, grant, *args):
    return pl.pallas_call(
        body,
        out_shape=[jax.ShapeDtypeStruct(shape, dtype) for shape, dtype in outs],
        in_specs=[pl.BlockSpec(memory_space=pltpu.VMEM)] * len(args),
        out_specs=[pl.BlockSpec(memory_space=pltpu.VMEM)] * len(outs),
        scratch_shapes=scratch,
        compiler_params=pltpu.CompilerParams(vmem_limit_bytes=grant << 20),
        cost_estimate=pl.CostEstimate(flops=cost, bytes_accessed=8 << 20, transcendentals=1 << 20),
    )(*args)


def prep_body(keep, gain, patches, xn, x_slot, offsets, keep_in, gain_in, x_in, sems):
    small = pltpu.make_async_copy(keep, keep_in, sems.at[0])
    other = pltpu.make_async_copy(gain, gain_in, sems.at[1])
    fetch = pltpu.make_async_copy(patches, x_in, sems.at[2])
    for copy in (small, fetch, other):
        copy.start()
    small.wait()
    at_row = lax.broadcasted_iota(jnp.int32, (CAP, CAP), 0)
    at_col = lax.broadcasted_iota(jnp.int32, (CAP, CAP), 1)
    own = jnp.broadcast_to(keep_in[...], (CAP, CAP))
    owner = lax.shift_right_arithmetic(own, 8)
    owner_col = jnp.sum(jnp.where(at_row == at_col, owner, 0), axis=1, keepdims=True)
    same = (owner_col == owner) & (at_row < at_col)
    rank = jnp.sum(same.astype(jnp.int32), axis=0, keepdims=True)
    slot = jnp.where(own >= 0, owner * SLOTS + rank, -1)
    pick = at_row == slot
    live = jnp.sum(pick.astype(F32), axis=1, keepdims=True) > 0.5
    spot = jnp.sum(jnp.where(pick, own - owner * FDEV, 0).astype(F32), axis=1, keepdims=True)
    offsets[...] = jnp.broadcast_to(jnp.where(live, spot, -1.0), (CAP, 128)).astype(BF16)
    fetch.wait()
    other.wait()
    rows = dot(pick.astype(F32).astype(BF16), x_in[...])
    x_slot[...] = rows.astype(BF16)
    lane = lax.broadcasted_iota(jnp.int32, rows.shape, 1)
    dead_row = jnp.where(lane == 0, DEAD, 0.0)
    xn[...] = jnp.where(live, layer_norm(rows, gain_in[...].reshape(1, rows.shape[1])), dead_row).astype(BF16)


def prep(keep, gain, patches):
    cap, width = patches.shape
    vmem = pl.BlockSpec(memory_space=pltpu.VMEM)
    return pl.pallas_call(
        prep_body,
        out_shape=[jax.ShapeDtypeStruct((cap, width), BF16), jax.ShapeDtypeStruct((cap, width), BF16),
                   jax.ShapeDtypeStruct((cap, 128), BF16)],
        in_specs=[pl.BlockSpec(memory_space=pltpu.HBM)] * 3,
        out_specs=[vmem] * 3,
        scratch_shapes=[pltpu.VMEM(keep.shape, keep.dtype), pltpu.VMEM(gain.shape, F32),
                        pltpu.VMEM((cap, width), BF16), pltpu.SemaphoreType.DMA((3,))],
        compiler_params=pltpu.CompilerParams(vmem_limit_bytes=8 << 20),
        cost_estimate=pl.CostEstimate(flops=10 << 20, bytes_accessed=1 << 19, transcendentals=0),
    )(*[pltpu.with_memory_space_constraint(arg, pltpu.HBM) for arg in (keep, gain, patches)])


def pack_body(x_slot, w_out, w_e2d, fc_in, fc_out, x_vis, w_oe, pack, out_in, e2d_in, packed, sems):
    loads = [
        pltpu.make_async_copy(w_out, out_in, sems.at[0]),
        pltpu.make_async_copy(w_e2d, e2d_in, sems.at[1]),
        pltpu.make_async_copy(fc_in, packed.at[pl.ds(0, HID)], sems.at[2]),
        pltpu.make_async_copy(fc_out, packed.at[pl.ds(HID, HID)], sems.at[3])]
    for copy in loads:
        copy.start()
    for copy in loads:
        copy.wait()
    both = jnp.concatenate([dot(out_in[...], e2d_in[...]), jnp.zeros((HP - HD, DD), F32)], axis=0).astype(BF16)
    w_oe[...] = both
    packed[2 * HID:, :] = both
    done = pltpu.make_async_copy(packed, pack, sems.at[4])
    done.start()
    x_vis[...] = dot(x_slot[...], e2d_in[...]).astype(BF16)
    done.wait()


def pack_up(x_slot, *args):
    width = x_slot.shape[1]
    vmem = pl.BlockSpec(memory_space=pltpu.VMEM)
    hbm = pl.BlockSpec(memory_space=pltpu.HBM)
    return pl.pallas_call(
        pack_body,
        out_shape=[jax.ShapeDtypeStruct((CAP, DD), BF16), jax.ShapeDtypeStruct((HP, DD), BF16),
                   pltpu.HBM((2 * HID + HP, DD), BF16)],
        in_specs=[vmem] + [hbm] * len(args),
        out_specs=[vmem, vmem, hbm],
        scratch_shapes=[pltpu.VMEM((HD, width), BF16), pltpu.VMEM((width, DD), BF16),
                        pltpu.VMEM((2 * HID + HP, DD), BF16), pltpu.SemaphoreType.DMA((5,))],
        compiler_params=pltpu.CompilerParams(vmem_limit_bytes=12 << 20),
        cost_estimate=pl.CostEstimate(flops=200 << 20, bytes_accessed=3 << 20, transcendentals=0),
    )(x_slot, *[pltpu.with_memory_space_constraint(arg, pltpu.HBM) for arg in args])


def turn_body(w_t, w):
    rows = w_t[...].astype(F32)
    gap = jnp.zeros((HL - HD, rows.shape[1]), F32)
    heads = [part for i in range(3) for part in (rows[HD * i:HD * (i + 1)], gap)]
    w[...] = jnp.concatenate(heads, axis=0).T.astype(BF16)


def turn(w_t):
    return call(turn_body, [((w_t.shape[1], 3 * HL), BF16)], [], 1 << 20, 16, w_t)[0]


def join_body(places, *refs):
    blocks, out, sems = refs[:len(places)], refs[len(places)], refs[len(places) + 1]
    copies = []
    for i, (k, column) in enumerate(places):
        rows, width = blocks[i].shape
        part = out.at[pl.ds(rows * k, rows), pl.ds(column, width)]
        copies.append(pltpu.make_async_copy(blocks[i], part, sems.at[i]))
    for copy in copies:
        copy.start()
    for copy in copies:
        copy.wait()


def join(blocks):
    places = []
    for k, parts in enumerate(blocks):
        column = 0
        for part in parts:
            places.append((k, column))
            column += part.shape[1]
    flat = [part for parts in blocks for part in parts]
    return pl.pallas_call(
        functools.partial(join_body, places),
        out_shape=jax.ShapeDtypeStruct((NZ * flat[0].shape[0], flat[0].shape[1]), flat[0].dtype),
        in_specs=[pl.BlockSpec(memory_space=pl.ANY)] * len(flat),
        out_specs=pl.BlockSpec(memory_space=pl.ANY),
        scratch_shapes=[pltpu.SemaphoreType.DMA((len(flat),))],
        compiler_params=pltpu.CompilerParams(vmem_limit_bytes=4 << 20),
        cost_estimate=pl.CostEstimate(flops=0, bytes_accessed=4 << 20, transcendentals=0),
    )(*flat)


def attend_body(mine, other, w, swap, extra, sent, saved, stats, xs, out, keep, keep_stats, sems):
    half = ROWS // 2
    loads = [
        pltpu.make_async_copy(mine, xs.at[pl.ds(0, half)], sems.at[0]),
        pltpu.make_async_copy(other, xs.at[pl.ds(half, half)], sems.at[1])]
    for load in loads:
        load.start()
    parts = []
    for i in range(2):
        loads[i].wait()
        parts.append(dot(xs[half * i:half * (i + 1), :], w[...]))
    qkv = jnp.concatenate(parts, axis=0)
    k_rows = qkv[:, HL:2 * HL].astype(BF16)
    q = (qkv[:, 0:HL] * SCALE).T.astype(BF16)
    vt = qkv[:, 2 * HL:].T.astype(BF16)
    keep[0:HL, :] = q
    keep[HL:2 * HL, :] = qkv[:, HL:2 * HL].T.astype(BF16)
    keep[2 * HL:3 * HL, :] = vt
    heads = pltpu.make_async_copy(keep.at[pl.ds(0, 3 * HL)], saved.at[pl.ds(0, 3 * HL)], sems.at[2])
    heads.start()
    dead = jnp.where(xs[:, 0:128].astype(F32)[:, 0:1] < 0.5 * DEAD, 0.0, -jnp.inf)
    ctx = []
    for i in range(3):
        cols = slice(256 * i, 256 * (i + 1))
        scores = dot(k_rows, q[:, cols]) + dead
        top = jnp.max(scores, axis=0, keepdims=True)
        expo = jnp.exp(scores - top)
        total = jnp.sum(expo, axis=0, keepdims=True)
        keep_stats[0:1, cols] = top
        keep_stats[1:2, cols] = total
        ctx.append(dot(vt, (expo / total).astype(BF16)))
    sums = pltpu.make_async_copy(keep_stats, stats, sems.at[3])
    sums.start()
    ctx = jnp.concatenate(ctx, axis=1).astype(BF16)
    out[:, 0:CAP, :] = dot_nt(swap[...], ctx).astype(BF16).reshape(16, CAP, 128)
    out[:, CAP:, :] = extra[...]
    send = pltpu.make_async_copy(out, sent, sems.at[4])
    send.start()
    keep[3 * HL:, :] = dot_nt(ctx, swap[...]).astype(BF16)
    last = pltpu.make_async_copy(keep.at[pl.ds(3 * HL, HL)], saved.at[pl.ds(3 * HL, HL)], sems.at[5])
    last.start()
    for copy in (heads, sums, send, last):
        copy.wait()


def attend(*args):
    vmem = pl.BlockSpec(memory_space=pltpu.VMEM)
    hbm = pl.BlockSpec(memory_space=pltpu.HBM)
    return pl.pallas_call(
        attend_body,
        out_shape=[pltpu.HBM((16, 64, 128), BF16), pltpu.HBM((4 * HL, ROWS), BF16), pltpu.HBM((8, ROWS), F32)],
        in_specs=[hbm, hbm, vmem, vmem, vmem],
        out_specs=[hbm, hbm, hbm],
        scratch_shapes=[pltpu.VMEM((ROWS, args[0].shape[1]), BF16), pltpu.VMEM((16, 64, 128), BF16),
                        pltpu.VMEM((4 * HL, ROWS), BF16), pltpu.VMEM((8, ROWS), F32), pltpu.SemaphoreType.DMA((6,))],
        compiler_params=pltpu.CompilerParams(vmem_limit_bytes=24 << 20),
        cost_estimate=pl.CostEstimate(flops=1700 << 20, bytes_accessed=8 << 20, transcendentals=1 << 20),
    )(*args)


def decode_body(came, weights, cot, mask, gain, table, recon, dvis, mixed, grad, w_oe, w_fc, cots, sems):
    loads = [pltpu.make_async_copy(weights.at[:, pl.ds(2 * HID, HP)], w_oe, sems.at[0])]
    loads += [
        pltpu.make_async_copy(
            weights.at[pl.ds(8 * i, 8), pl.ds(0, 2 * HID)], w_fc.at[pl.ds(8 * i, 8)], sems.at[1 + i])
        for i in range(2)]
    up = pltpu.make_async_copy(cot, cots, sems.at[3])
    for copy in (loads[0], up, *loads[1:]):
        copy.start()
    flat = came[...].reshape(16 * 64, 128)
    vis = jnp.zeros((CAP, DD), F32)
    loads[0].wait()
    for g in range(16):
        vis += dot(came[g, 0:CAP, 0:HP], w_oe[g])
    row = lax.broadcasted_iota(jnp.int32, (CAP, 1024), 0)
    col = lax.broadcasted_iota(jnp.int32, (CAP, 1024), 1)
    source = jnp.zeros((CAP, 1024), jnp.int32)
    for g in range(1, 16):
        source += (row >= SLOTS * g).astype(jnp.int32)
    slot = row - SLOTS * source
    base = 64 * source + CAP
    x_part = jnp.concatenate(
        [dot((col == base + 4 * slot + i).astype(F32).astype(BF16), flat) for i in range(4)], axis=1)
    vis = (vis + x_part).astype(BF16)
    spots = dot((col == base + 12).astype(F32).astype(BF16), flat)
    lane = lax.broadcasted_iota(jnp.int32, (CAP, 128), 1)
    spot = jnp.sum(jnp.where(lane == slot[:, 0:128], spots, 0.0), axis=1, keepdims=True)
    spot = jnp.concatenate([spot, jnp.full((128 - CAP, 1), -1.0, F32)], axis=0)
    vis = jnp.concatenate([vis.astype(F32), jnp.zeros((128 - CAP, DD), F32)], axis=0).astype(BF16)
    where_col = lax.broadcasted_iota(jnp.int32, (128, FDEV), 1).astype(F32)
    picker = (spot == where_col).astype(F32)
    placer = picker.T
    seen = jnp.sum(placer, axis=1, keepdims=True)
    dec_vis = dot(placer.astype(BF16), vis)
    dec_x = jnp.where(seen > 0.5, dec_vis, mask[...].astype(F32)) + table[...]
    mean = jnp.mean(dec_x, axis=-1, keepdims=True)
    centred = dec_x - mean
    var = jnp.mean(centred * centred, axis=-1, keepdims=True)
    inv_std = lax.rsqrt(var + 1e-06)
    normed = centred * inv_std
    dn = (normed * gain[...]).astype(BF16)
    up.wait()
    cot_b = cots[...]
    mixed[...] = dec_x
    for i in range(8):
        if i % 4 == 0:
            loads[1 + i // 4].wait()
        fin = jnp.concatenate([w_fc[2 * i, 0:HID, :], w_fc[2 * i + 1, 0:HID, :]], axis=0)
        fout = jnp.concatenate([w_fc[2 * i, HID:2 * HID, :], w_fc[2 * i + 1, HID:2 * HID, :]], axis=0)
        hidden = dot_nt(dn, fin)
        dact = dot_nt(cot_b, fout)
        cdf = 0.5 * (1.0 + lax.erf(hidden * 0.7071067811865476))
        pdf = jnp.exp(-0.5 * hidden * hidden) * 0.3989422804014327
        act = (hidden * cdf).astype(BF16)
        dhidden = (dact * (cdf + hidden * pdf)).astype(BF16)
        mixed[...] += dot(act, fout)
        if i == 0:
            grad[...] = dot(dhidden, fin)
        else:
            grad[...] += dot(dhidden, fin)
    recon[...] = mixed[...].astype(BF16)
    scaled = grad[...] * gain[...]
    first = jnp.mean(scaled, axis=-1, keepdims=True)
    second = jnp.mean(scaled * normed, axis=-1, keepdims=True)
    ddec = (cot_b.astype(F32) + inv_std * (scaled - first - normed * second)).astype(BF16)
    dvis[...] = dot(picker[0:CAP].astype(BF16), ddec).astype(BF16)


def decode(came, weights, cot, *args):
    vmem = pl.BlockSpec(memory_space=pltpu.VMEM)
    hbm = pl.BlockSpec(memory_space=pltpu.HBM)
    return pl.pallas_call(
        decode_body,
        out_shape=[jax.ShapeDtypeStruct((FDEV, DD), BF16), jax.ShapeDtypeStruct((CAP, DD), BF16)],
        in_specs=[vmem, hbm, hbm] + [vmem] * len(args),
        out_specs=[vmem, vmem],
        scratch_shapes=[pltpu.VMEM((FDEV, DD), F32), pltpu.VMEM((FDEV, DD), F32),
                        pltpu.VMEM((16, HP, DD), BF16), pltpu.VMEM((16, 2 * HID, DD), BF16),
                        pltpu.VMEM((FDEV, DD), BF16), pltpu.SemaphoreType.DMA((4,))],
        compiler_params=pltpu.CompilerParams(vmem_limit_bytes=24 << 20),
        cost_estimate=pl.CostEstimate(flops=2300 << 20, bytes_accessed=8 << 20, transcendentals=1 << 20),
    )(came, pltpu.with_memory_space_constraint(weights, pltpu.HBM),
      pltpu.with_memory_space_constraint(cot, pltpu.HBM), *args)


def back_body(dvis, w_oe, swap, saved, stats, mine, other, parts, ds_all, pb_all, keep, keep_stats, xs, sems):
    loads = [
        pltpu.make_async_copy(saved, keep, sems.at[0]),
        pltpu.make_async_copy(stats, keep_stats, sems.at[1]),
        pltpu.make_async_copy(mine, xs.at[pl.ds(0, ROWS // 2)], sems.at[2]),
        pltpu.make_async_copy(other, xs.at[pl.ds(ROWS // 2, ROWS // 2)], sems.at[3])]
    for load in loads:
        load.start()
    dctx = dot(dot_nt(w_oe[...], dvis[...]).astype(BF16), swap[...])
    dctx = jnp.concatenate([dctx, jnp.zeros((HL - HP, ROWS), F32)], axis=0).astype(BF16)
    for load in loads:
        load.wait()
    x = xs[...]
    grad_oe = dot(keep[3 * HL:, :], dvis[...])[0:HD]
    q, kt = keep[0:HL, :], keep[HL:2 * HL, :]
    k = kt.astype(F32).T.astype(BF16)
    v = keep[2 * HL:3 * HL, :].astype(F32).T.astype(BF16)
    dead = jnp.where(x[:, 0:128].astype(F32)[:, 0:1] < 0.5 * DEAD, 0.0, -jnp.inf)
    dq = []
    for i in range(3):
        cols = slice(256 * i, 256 * (i + 1))
        scores = dot(k, q[:, cols]) + dead
        probs = jnp.exp(scores - keep_stats[0:1, cols]) / keep_stats[1:2, cols]
        dprob = dot(v, dctx[:, cols])
        inner = jnp.sum(probs * dprob, axis=0, keepdims=True)
        ds = (probs * (dprob - inner)).astype(BF16)
        ds_all[:, cols] = ds
        pb_all[:, cols] = probs.astype(BF16)
        dq.append(dot(kt, ds) * SCALE)
    dq = jnp.concatenate(dq, axis=1)[0:HD]
    dk = dot_nt(q, ds_all[...])[0:HD]
    dv = dot_nt(dctx, pb_all[...])[0:HD]
    dqkv = jnp.concatenate([dq, dk, dv], axis=0).astype(BF16)
    grad = dot(dqkv, x)
    wide = grad.shape[1] // 128
    pieces = [grad[:, 128 * j:128 * (j + 1)] for j in range(wide)]
    pieces += [grad_oe[:, 128 * j:128 * (j + 1)] for j in range(DD // 128)]
    done = sum(p.shape[0] for p in pieces)
    pieces.append(jnp.zeros((GRAD_ROWS - done, 128), F32))
    parts[...] = jnp.concatenate(pieces, axis=0).astype(BF16)


def back(dvis, w_oe, swap, saved, stats, mine, other):
    vmem = pl.BlockSpec(memory_space=pltpu.VMEM)
    hbm = pl.BlockSpec(memory_space=pltpu.HBM)
    return pl.pallas_call(
        back_body,
        out_shape=jax.ShapeDtypeStruct((GRAD_ROWS, 128), BF16),
        in_specs=[vmem, vmem, vmem, hbm, hbm, hbm, hbm],
        out_specs=vmem,
        scratch_shapes=[pltpu.VMEM((ROWS, ROWS), BF16), pltpu.VMEM((ROWS, ROWS), BF16),
                        pltpu.VMEM((4 * HL, ROWS), BF16), pltpu.VMEM((8, ROWS), F32),
                        pltpu.VMEM((ROWS, mine.shape[1]), BF16), pltpu.SemaphoreType.DMA((4,))],
        compiler_params=pltpu.CompilerParams(vmem_limit_bytes=24 << 20),
        cost_estimate=pl.CostEstimate(flops=2500 << 20, bytes_accessed=8 << 20, transcendentals=1 << 20),
    )(dvis, w_oe, swap, saved, stats, mine, other)


def finish_body(total, w_e2d, grad_q, grad_o):
    rows = total[...].astype(F32)
    wide = grad_q.shape[1] // 128
    tall = 3 * HD
    for j in range(wide):
        grad_q[:, 128 * j:128 * (j + 1)] = rows[tall * j:tall * (j + 1)].astype(BF16)
    at = tall * wide
    grad_oe = jnp.concatenate([rows[at + HD * j:at + HD * (j + 1)] for j in range(DD // 128)], axis=1)
    grad_o[...] = dot_nt(grad_oe.astype(BF16), w_e2d[...]).astype(BF16)


def finish(total, w_e2d):
    width = w_e2d.shape[0]
    return call(
        finish_body, [((3 * HD, width), BF16), ((HD, width), BF16)], [], 130 << 20, 12, total, w_e2d)


def position_table(positions, width):
    half = width // 2
    freq = 10000.0 ** (-(jnp.arange(half, dtype=F32) * 2.0 / width))
    angle = positions[:, None] * freq[None, :]
    return jnp.concatenate([jnp.sin(angle), jnp.cos(angle)], axis=1)


def exchange(block, axis):
    return lax.all_to_all(block, axis, 0, 0, tiled=True)


def spread(block, axis):
    return exchange(jnp.broadcast_to(block[None], (lax.axis_size(axis),) + block.shape), axis)


def z_shift(block, step):
    return lax.ppermute(block, "z", [(z, (z + step) % NZ) for z in range(NZ)])


def around(block):
    got = {0: block}
    for step in (1, -1, 2, -2):
        got[step % NZ] = z_shift(block, step)
    got[3] = z_shift(got[2], 1)
    got[5] = z_shift(got[6], -1)
    back_two, got[1], got[7] = lax.optimization_barrier((got[6], got[1], got[7]))
    blocks = [[got.get(k)] for k in range(NZ)]
    blocks[4] = [z_shift(got[2][:, :CUT], 2), z_shift(back_two[:, CUT:], -2)]
    return blocks


def swap_core(block):
    return lax.ppermute(block, "core", [(0, 1), (1, 0)])


def local(
    patches,
    keep_pos,
    kept_counts,
    enc_gain,
    w_qkv,
    w_out,
    w_e2d,
    mask_token,
    dec_gain,
    fc_in,
    fc_out,
    cotangent,
):
    me = lax.axis_index(SEQ)
    my_z, my_c = me // 2, me % 2
    fdev = cotangent.shape[1]
    cot = cotangent[0]
    cap = keep_pos.shape[1]
    rows = 16 * cap

    xn_own, x_slot, offsets = prep(keep_pos, enc_gain, patches[0])
    x_vis, w_oe_own, pack = pack_up(x_slot, w_out, w_e2d, fc_in, fc_out)
    weights = lax.all_gather(pack, SEQ, axis=0)

    places = jnp.pad(offsets[:, 0].reshape(16, 1, SLOTS), ((0, 0), (0, 0), (0, 128 - SLOTS)))
    extra = jnp.concatenate(
        [x_vis.reshape(16, 12, 128), places, jnp.zeros((16, 3, 128), BF16)], axis=1)

    tok = jnp.arange(rows, dtype=jnp.int32)
    block = tok // cap
    source = (my_z - block % NZ) % NZ * 2 + (my_c ^ (block // NZ))
    inside = tok % cap
    dest = inside // SLOTS * cap + source * SLOTS + inside % SLOTS
    swap = (dest[None, :] == tok[:, None]).astype(BF16)
    table = position_table((me * fdev + jnp.arange(fdev, dtype=jnp.int32)).astype(F32), DD)

    w = turn(w_qkv.transpose(0, 2, 1).reshape(3 * HD, -1))
    blocks = around(xn_own)
    blocks[4][0], w, swap, extra = lax.optimization_barrier((blocks[4][0], w, swap, extra))
    mine = join(blocks)
    other = swap_core(mine)
    sent, saved, stats = attend(mine, other, w, swap, extra)
    came = exchange(sent, SEQ)
    recon, dvis_own = decode(came, weights, cot, mask_token[None], dec_gain[None], table)
    dvis = lax.all_gather(dvis_own, SEQ, axis=0, tiled=True)
    parts = back(dvis, w_oe_own, swap, saved, stats, mine, other)

    parts = jnp.sum(exchange(parts.reshape(NX, 832, 128), "x").astype(F32), axis=0).astype(BF16)
    parts = jnp.sum(exchange(parts.reshape(NY, 104, 128), "y").astype(F32), axis=0).astype(BF16)
    parts = spread(parts, "y").reshape(832, 128)
    total = spread(parts, "x").reshape(GRAD_ROWS, 128)
    grad_q, grad_o = finish(total, w_e2d)
    grad_q = grad_q.reshape(3, HD, -1).transpose(0, 2, 1)
    return (recon[None], grad_q, grad_o)


def solution(mesh):
    axes = Mesh(mesh.devices.reshape(NY, NX, NZ, 2), ("y", "x", "z", "core"))
    dp = ("y", "x")
    placed = (
        P(dp, SEQ, None),
        P(dp, SEQ),
        P(dp, None),
        P(),
        P(None, None, SEQ),
        P(SEQ, None),
        P(),
        P(),
        P(),
        P(SEQ, None),
        P(SEQ, None),
        P(dp, SEQ, None),
    )
    return jax.shard_map(
        local,
        mesh=axes,
        in_specs=placed,
        out_specs=(P(dp, SEQ, None), P(None, None, SEQ), P(SEQ, None)),
        check_vma=False,
    )
```

```python
import functools

import jax
import jax.numpy as jnp
from jax import lax
from jax.experimental import pallas as pl
from jax.experimental.pallas import tpu as pltpu
from jax.sharding import Mesh
from jax.sharding import PartitionSpec as P

HD = 88
HP = 96
HL = 128
DD = 512
SEQ = ("z", "core")
NZ = 8
NX = 4
NY = 8
CAP = 48
ROWS = 768
SLOTS = 3
HID = 128
FDEV = 256
DEAD = 1024.0
GRAD_ROWS = 3328
SCALE = HD ** (-0.5)
F32 = jnp.float32
BF16 = jnp.bfloat16


def dot(a, b):
    return jnp.dot(a, b, preferred_element_type=F32)


def dot_nt(a, b):
    return lax.dot_general(a, b, (((1,), (1,)), ((), ())), preferred_element_type=F32)


def layer_norm(values, gain):
    mean = jnp.mean(values, axis=-1, keepdims=True)
    centred = values - mean
    var = jnp.mean(centred * centred, axis=-1, keepdims=True)
    return centred * lax.rsqrt(var + 1e-06) * gain


def call(body, outs, scratch, cost, grant, *args):
    return pl.pallas_call(
        body,
        out_shape=[jax.ShapeDtypeStruct(shape, dtype) for shape, dtype in outs],
        in_specs=[pl.BlockSpec(memory_space=pltpu.VMEM)] * len(args),
        out_specs=[pl.BlockSpec(memory_space=pltpu.VMEM)] * len(outs),
        scratch_shapes=scratch,
        compiler_params=pltpu.CompilerParams(vmem_limit_bytes=grant << 20),
        cost_estimate=pl.CostEstimate(flops=cost, bytes_accessed=8 << 20, transcendentals=1 << 20),
    )(*args)


def prep_body(keep, gain, patches, xn, x_slot, offsets, keep_in, gain_in, x_in, sems):
    small = pltpu.make_async_copy(keep, keep_in, sems.at[0])
    other = pltpu.make_async_copy(gain, gain_in, sems.at[1])
    fetch = pltpu.make_async_copy(patches, x_in, sems.at[2])
    for copy in (small, fetch, other):
        copy.start()
    small.wait()
    at_row = lax.broadcasted_iota(jnp.int32, (CAP, CAP), 0)
    at_col = lax.broadcasted_iota(jnp.int32, (CAP, CAP), 1)
    own = jnp.broadcast_to(keep_in[...], (CAP, CAP))
    owner = lax.shift_right_arithmetic(own, 8)
    owner_col = jnp.sum(jnp.where(at_row == at_col, owner, 0), axis=1, keepdims=True)
    same = (owner_col == owner) & (at_row < at_col)
    rank = jnp.sum(same.astype(jnp.int32), axis=0, keepdims=True)
    slot = jnp.where(own >= 0, owner * SLOTS + rank, -1)
    pick = at_row == slot
    live = jnp.sum(pick.astype(F32), axis=1, keepdims=True) > 0.5
    spot = jnp.sum(jnp.where(pick, own - owner * FDEV, 0).astype(F32), axis=1, keepdims=True)
    offsets[...] = jnp.broadcast_to(jnp.where(live, spot, -1.0), (CAP, 128)).astype(BF16)
    fetch.wait()
    other.wait()
    rows = dot(pick.astype(F32).astype(BF16), x_in[...])
    x_slot[...] = rows.astype(BF16)
    lane = lax.broadcasted_iota(jnp.int32, rows.shape, 1)
    dead_row = jnp.where(lane == 0, DEAD, 0.0)
    xn[...] = jnp.where(live, layer_norm(rows, gain_in[...].reshape(1, rows.shape[1])), dead_row).astype(BF16)


def prep(keep, gain, patches):
    cap, width = patches.shape
    vmem = pl.BlockSpec(memory_space=pltpu.VMEM)
    return pl.pallas_call(
        prep_body,
        out_shape=[jax.ShapeDtypeStruct((cap, width), BF16), jax.ShapeDtypeStruct((cap, width), BF16),
                   jax.ShapeDtypeStruct((cap, 128), BF16)],
        in_specs=[pl.BlockSpec(memory_space=pltpu.HBM)] * 3,
        out_specs=[vmem] * 3,
        scratch_shapes=[pltpu.VMEM(keep.shape, keep.dtype), pltpu.VMEM(gain.shape, F32),
                        pltpu.VMEM((cap, width), BF16), pltpu.SemaphoreType.DMA((3,))],
        compiler_params=pltpu.CompilerParams(vmem_limit_bytes=8 << 20),
        cost_estimate=pl.CostEstimate(flops=10 << 20, bytes_accessed=1 << 19, transcendentals=0),
    )(*[pltpu.with_memory_space_constraint(arg, pltpu.HBM) for arg in (keep, gain, patches)])


def pack_body(x_slot, w_out, w_e2d, fc_in, fc_out, x_vis, w_oe, pack, out_in, e2d_in, packed, sems):
    loads = [
        pltpu.make_async_copy(w_out, out_in, sems.at[0]),
        pltpu.make_async_copy(w_e2d, e2d_in, sems.at[1]),
        pltpu.make_async_copy(fc_in, pack.at[pl.ds(0, HID)], sems.at[2]),
        pltpu.make_async_copy(fc_out, pack.at[pl.ds(HID, HID)], sems.at[3])]
    for copy in loads:
        copy.start()
    for copy in loads[:2]:
        copy.wait()
    both = jnp.concatenate([dot(out_in[...], e2d_in[...]), jnp.zeros((HP - HD, DD), F32)], axis=0).astype(BF16)
    w_oe[...] = both
    packed[...] = both
    done = pltpu.make_async_copy(packed, pack.at[pl.ds(2 * HID, HP)], sems.at[4])
    done.start()
    x_vis[...] = dot(x_slot[...], e2d_in[...]).astype(BF16)
    for copy in (*loads[2:], done):
        copy.wait()


def pack_up(x_slot, *args):
    width = x_slot.shape[1]
    vmem = pl.BlockSpec(memory_space=pltpu.VMEM)
    hbm = pl.BlockSpec(memory_space=pltpu.HBM)
    return pl.pallas_call(
        pack_body,
        out_shape=[jax.ShapeDtypeStruct((CAP, DD), BF16), jax.ShapeDtypeStruct((HP, DD), BF16),
                   pltpu.HBM((2 * HID + HP, DD), BF16)],
        in_specs=[vmem] + [hbm] * len(args),
        out_specs=[vmem, vmem, hbm],
        scratch_shapes=[pltpu.VMEM((HD, width), BF16), pltpu.VMEM((width, DD), BF16),
                        pltpu.VMEM((HP, DD), BF16), pltpu.SemaphoreType.DMA((5,))],
        compiler_params=pltpu.CompilerParams(vmem_limit_bytes=12 << 20),
        cost_estimate=pl.CostEstimate(flops=200 << 20, bytes_accessed=3 << 20, transcendentals=0),
    )(x_slot, *[pltpu.with_memory_space_constraint(arg, pltpu.HBM) for arg in args])


def turn_body(w_t, w):
    rows = w_t[...].astype(F32)
    gap = jnp.zeros((HL - HD, rows.shape[1]), F32)
    heads = [part for i in range(3) for part in (rows[HD * i:HD * (i + 1)], gap)]
    w[...] = jnp.concatenate(heads, axis=0).T.astype(BF16)


def turn(w_t):
    return call(turn_body, [((w_t.shape[1], 3 * HL), BF16)], [], 1 << 20, 16, w_t)[0]


def join_body(places, *refs):
    blocks, out, sems = refs[:len(places)], refs[len(places)], refs[len(places) + 1]
    copies = []
    for i, (k, column) in enumerate(places):
        rows, width = blocks[i].shape
        part = out.at[pl.ds(rows * k, rows), pl.ds(column, width)]
        copies.append(pltpu.make_async_copy(blocks[i], part, sems.at[i]))
    for copy in copies:
        copy.start()
    for copy in copies:
        copy.wait()


def join(blocks):
    places = []
    for k, parts in enumerate(blocks):
        column = 0
        for part in parts:
            places.append((k, column))
            column += part.shape[1]
    flat = [part for parts in blocks for part in parts]
    return pl.pallas_call(
        functools.partial(join_body, places),
        out_shape=jax.ShapeDtypeStruct((NZ * flat[0].shape[0], flat[0].shape[1]), flat[0].dtype),
        in_specs=[pl.BlockSpec(memory_space=pl.ANY)] * len(flat),
        out_specs=pl.BlockSpec(memory_space=pl.ANY),
        scratch_shapes=[pltpu.SemaphoreType.DMA((len(flat),))],
        compiler_params=pltpu.CompilerParams(vmem_limit_bytes=4 << 20),
        cost_estimate=pl.CostEstimate(flops=0, bytes_accessed=4 << 20, transcendentals=0),
    )(*flat)


def attend_body(mine, other, w, swap, extra, sent, saved, stats, xs, out, keep, keep_stats, sems):
    half = ROWS // 2
    loads = [
        pltpu.make_async_copy(mine, xs.at[pl.ds(0, half)], sems.at[0]),
        pltpu.make_async_copy(other, xs.at[pl.ds(half, half)], sems.at[1])]
    for load in loads:
        load.start()
    parts = []
    for i in range(2):
        loads[i].wait()
        parts.append(dot(xs[half * i:half * (i + 1), :], w[...]))
    qkv = jnp.concatenate(parts, axis=0)
    k_rows = qkv[:, HL:2 * HL].astype(BF16)
    q = (qkv[:, 0:HL] * SCALE).T.astype(BF16)
    vt = qkv[:, 2 * HL:].T.astype(BF16)
    keep[0:HL, :] = q
    keep[HL:2 * HL, :] = qkv[:, HL:2 * HL].T.astype(BF16)
    keep[2 * HL:3 * HL, :] = vt
    heads = pltpu.make_async_copy(keep.at[pl.ds(0, 3 * HL)], saved.at[pl.ds(0, 3 * HL)], sems.at[2])
    heads.start()
    dead = jnp.where(xs[:, 0:128].astype(F32)[:, 0:1] < 0.5 * DEAD, 0.0, -jnp.inf)
    ctx = []
    for i in range(3):
        cols = slice(256 * i, 256 * (i + 1))
        scores = dot(k_rows, q[:, cols]) + dead
        top = jnp.max(scores, axis=0, keepdims=True)
        expo = jnp.exp(scores - top)
        total = jnp.sum(expo, axis=0, keepdims=True)
        keep_stats[0:1, cols] = top
        keep_stats[1:2, cols] = total
        ctx.append(dot(vt, (expo * (1.0 / total)).astype(BF16)))
    sums = pltpu.make_async_copy(keep_stats, stats, sems.at[3])
    sums.start()
    ctx = jnp.concatenate(ctx, axis=1).astype(BF16)
    out[:, 0:CAP, :] = dot_nt(swap[...], ctx).astype(BF16).reshape(16, CAP, 128)
    out[:, CAP:, :] = extra[...]
    send = pltpu.make_async_copy(out, sent, sems.at[4])
    send.start()
    keep[3 * HL:, :] = dot_nt(ctx, swap[...]).astype(BF16)
    last = pltpu.make_async_copy(keep.at[pl.ds(3 * HL, HL)], saved.at[pl.ds(3 * HL, HL)], sems.at[5])
    last.start()
    for copy in (heads, sums, send, last):
        copy.wait()


def attend(*args):
    vmem = pl.BlockSpec(memory_space=pltpu.VMEM)
    hbm = pl.BlockSpec(memory_space=pltpu.HBM)
    return pl.pallas_call(
        attend_body,
        out_shape=[pltpu.HBM((16, 64, 128), BF16), pltpu.HBM((4 * HL, ROWS), BF16), pltpu.HBM((8, ROWS), F32)],
        in_specs=[hbm, hbm, vmem, vmem, vmem],
        out_specs=[hbm, hbm, hbm],
        scratch_shapes=[pltpu.VMEM((ROWS, args[0].shape[1]), BF16), pltpu.VMEM((16, 64, 128), BF16),
                        pltpu.VMEM((4 * HL, ROWS), BF16), pltpu.VMEM((8, ROWS), F32), pltpu.SemaphoreType.DMA((6,))],
        compiler_params=pltpu.CompilerParams(vmem_limit_bytes=24 << 20),
        cost_estimate=pl.CostEstimate(flops=1700 << 20, bytes_accessed=8 << 20, transcendentals=1 << 20),
    )(*args)


def decode_body(came, weights, cot, mask, gain, table, recon, dvis, mixed, grad, w_oe, w_fc, cots, sems):
    loads = [pltpu.make_async_copy(weights.at[:, pl.ds(2 * HID, HP)], w_oe, sems.at[0])]
    loads += [
        pltpu.make_async_copy(
            weights.at[pl.ds(8 * i, 8), pl.ds(0, 2 * HID)], w_fc.at[pl.ds(8 * i, 8)], sems.at[1 + i])
        for i in range(2)]
    up = pltpu.make_async_copy(cot, cots, sems.at[3])
    for copy in (loads[0], up, *loads[1:]):
        copy.start()
    flat = came[...].reshape(16 * 64, 128)
    vis = jnp.zeros((CAP, DD), F32)
    loads[0].wait()
    for g in range(16):
        vis += dot(came[g, 0:CAP, 0:HP], w_oe[g])
    row = lax.broadcasted_iota(jnp.int32, (CAP, 1024), 0)
    col = lax.broadcasted_iota(jnp.int32, (CAP, 1024), 1)
    source = jnp.zeros((CAP, 1024), jnp.int32)
    for g in range(1, 16):
        source += (row >= SLOTS * g).astype(jnp.int32)
    slot = row - SLOTS * source
    base = 64 * source + CAP
    x_part = jnp.concatenate(
        [dot((col == base + 4 * slot + i).astype(F32).astype(BF16), flat) for i in range(4)], axis=1)
    vis = (vis + x_part).astype(BF16)
    spots = dot((col == base + 12).astype(F32).astype(BF16), flat)
    lane = lax.broadcasted_iota(jnp.int32, (CAP, 128), 1)
    spot = jnp.sum(jnp.where(lane == slot[:, 0:128], spots, 0.0), axis=1, keepdims=True)
    spot = jnp.concatenate([spot, jnp.full((128 - CAP, 1), -1.0, F32)], axis=0)
    vis = jnp.concatenate([vis.astype(F32), jnp.zeros((128 - CAP, DD), F32)], axis=0).astype(BF16)
    where_col = lax.broadcasted_iota(jnp.int32, (128, FDEV), 1).astype(F32)
    picker = (spot == where_col).astype(F32)
    placer = picker.T
    seen = jnp.sum(placer, axis=1, keepdims=True)
    dec_vis = dot(placer.astype(BF16), vis)
    dec_x = jnp.where(seen > 0.5, dec_vis, mask[...].astype(F32)) + table[...]
    mean = jnp.mean(dec_x, axis=-1, keepdims=True)
    centred = dec_x - mean
    var = jnp.mean(centred * centred, axis=-1, keepdims=True)
    inv_std = lax.rsqrt(var + 1e-06)
    normed = centred * inv_std
    dn = (normed * gain[...]).astype(BF16)
    up.wait()
    cot_b = cots[...]
    mixed[...] = dec_x
    for i in range(8):
        if i % 4 == 0:
            loads[1 + i // 4].wait()
        fin = jnp.concatenate([w_fc[2 * i, 0:HID, :], w_fc[2 * i + 1, 0:HID, :]], axis=0)
        fout = jnp.concatenate([w_fc[2 * i, HID:2 * HID, :], w_fc[2 * i + 1, HID:2 * HID, :]], axis=0)
        hidden = dot_nt(dn, fin)
        dact = dot_nt(cot_b, fout)
        cdf = 0.5 * (1.0 + lax.erf(hidden * 0.7071067811865476))
        pdf = jnp.exp(-0.5 * hidden * hidden) * 0.3989422804014327
        act = (hidden * cdf).astype(BF16)
        dhidden = (dact * (cdf + hidden * pdf)).astype(BF16)
        mixed[...] += dot(act, fout)
        if i == 0:
            grad[...] = dot(dhidden, fin)
        else:
            grad[...] += dot(dhidden, fin)
    recon[...] = mixed[...].astype(BF16)
    scaled = grad[...] * gain[...]
    first = jnp.mean(scaled, axis=-1, keepdims=True)
    second = jnp.mean(scaled * normed, axis=-1, keepdims=True)
    ddec = (cot_b.astype(F32) + inv_std * (scaled - first - normed * second)).astype(BF16)
    dvis[...] = dot(picker[0:CAP].astype(BF16), ddec).astype(BF16)


def decode(came, weights, cot, *args):
    vmem = pl.BlockSpec(memory_space=pltpu.VMEM)
    hbm = pl.BlockSpec(memory_space=pltpu.HBM)
    return pl.pallas_call(
        decode_body,
        out_shape=[jax.ShapeDtypeStruct((FDEV, DD), BF16), jax.ShapeDtypeStruct((CAP, DD), BF16)],
        in_specs=[vmem, hbm, hbm] + [vmem] * len(args),
        out_specs=[vmem, vmem],
        scratch_shapes=[pltpu.VMEM((FDEV, DD), F32), pltpu.VMEM((FDEV, DD), F32),
                        pltpu.VMEM((16, HP, DD), BF16), pltpu.VMEM((16, 2 * HID, DD), BF16),
                        pltpu.VMEM((FDEV, DD), BF16), pltpu.SemaphoreType.DMA((4,))],
        compiler_params=pltpu.CompilerParams(vmem_limit_bytes=24 << 20),
        cost_estimate=pl.CostEstimate(flops=2300 << 20, bytes_accessed=8 << 20, transcendentals=1 << 20),
    )(came, pltpu.with_memory_space_constraint(weights, pltpu.HBM),
      pltpu.with_memory_space_constraint(cot, pltpu.HBM), *args)


def back_body(dvis, w_oe, swap, saved, stats, mine, other, parts, ds_all, pb_all, keep, keep_stats, xs, sems):
    loads = [
        pltpu.make_async_copy(saved, keep, sems.at[0]),
        pltpu.make_async_copy(stats, keep_stats, sems.at[1]),
        pltpu.make_async_copy(mine, xs.at[pl.ds(0, ROWS // 2)], sems.at[2]),
        pltpu.make_async_copy(other, xs.at[pl.ds(ROWS // 2, ROWS // 2)], sems.at[3])]
    for load in loads:
        load.start()
    dctx = dot(dot_nt(w_oe[...], dvis[...]).astype(BF16), swap[...])
    dctx = jnp.concatenate([dctx, jnp.zeros((HL - HP, ROWS), F32)], axis=0).astype(BF16)
    for load in loads:
        load.wait()
    x = xs[...]
    grad_oe = dot(keep[3 * HL:, :], dvis[...])[0:HD]
    q, kt = keep[0:HL, :], keep[HL:2 * HL, :]
    k = kt.astype(F32).T.astype(BF16)
    v = keep[2 * HL:3 * HL, :].astype(F32).T.astype(BF16)
    dead = jnp.where(x[:, 0:128].astype(F32)[:, 0:1] < 0.5 * DEAD, 0.0, -jnp.inf)
    dq = []
    for i in range(3):
        cols = slice(256 * i, 256 * (i + 1))
        scores = dot(k, q[:, cols]) + dead
        probs = jnp.exp(scores - keep_stats[0:1, cols]) * (1.0 / keep_stats[1:2, cols])
        dprob = dot(v, dctx[:, cols])
        inner = jnp.sum(probs * dprob, axis=0, keepdims=True)
        ds = (probs * (dprob - inner)).astype(BF16)
        ds_all[:, cols] = ds
        pb_all[:, cols] = probs.astype(BF16)
        dq.append(dot(kt, ds) * SCALE)
    dq = jnp.concatenate(dq, axis=1)[0:HD]
    dk = dot_nt(q, ds_all[...])[0:HD]
    dv = dot_nt(dctx, pb_all[...])[0:HD]
    dqkv = jnp.concatenate([dq, dk, dv], axis=0).astype(BF16)
    grad = dot(dqkv, x)
    wide = grad.shape[1] // 128
    pieces = [grad[:, 128 * j:128 * (j + 1)] for j in range(wide)]
    pieces += [grad_oe[:, 128 * j:128 * (j + 1)] for j in range(DD // 128)]
    done = sum(p.shape[0] for p in pieces)
    pieces.append(jnp.zeros((GRAD_ROWS - done, 128), F32))
    parts[...] = jnp.concatenate(pieces, axis=0).astype(BF16)


def back(dvis, w_oe, swap, saved, stats, mine, other):
    vmem = pl.BlockSpec(memory_space=pltpu.VMEM)
    hbm = pl.BlockSpec(memory_space=pltpu.HBM)
    return pl.pallas_call(
        back_body,
        out_shape=jax.ShapeDtypeStruct((GRAD_ROWS, 128), BF16),
        in_specs=[vmem, vmem, vmem, hbm, hbm, hbm, hbm],
        out_specs=vmem,
        scratch_shapes=[pltpu.VMEM((ROWS, ROWS), BF16), pltpu.VMEM((ROWS, ROWS), BF16),
                        pltpu.VMEM((4 * HL, ROWS), BF16), pltpu.VMEM((8, ROWS), F32),
                        pltpu.VMEM((ROWS, mine.shape[1]), BF16), pltpu.SemaphoreType.DMA((4,))],
        compiler_params=pltpu.CompilerParams(vmem_limit_bytes=24 << 20),
        cost_estimate=pl.CostEstimate(flops=2500 << 20, bytes_accessed=8 << 20, transcendentals=1 << 20),
    )(dvis, w_oe, swap, saved, stats, mine, other)


def finish_body(total, w_e2d, grad_q, grad_o):
    rows = total[...].astype(F32)
    wide = grad_q.shape[1] // 128
    tall = 3 * HD
    for j in range(wide):
        grad_q[:, 128 * j:128 * (j + 1)] = rows[tall * j:tall * (j + 1)].astype(BF16)
    at = tall * wide
    grad_oe = jnp.concatenate([rows[at + HD * j:at + HD * (j + 1)] for j in range(DD // 128)], axis=1)
    grad_o[...] = dot_nt(grad_oe.astype(BF16), w_e2d[...]).astype(BF16)


def finish(total, w_e2d):
    width = w_e2d.shape[0]
    return call(
        finish_body, [((3 * HD, width), BF16), ((HD, width), BF16)], [], 130 << 20, 12, total, w_e2d)


def position_table(positions, width):
    half = width // 2
    freq = 10000.0 ** (-(jnp.arange(half, dtype=F32) * 2.0 / width))
    angle = positions[:, None] * freq[None, :]
    return jnp.concatenate([jnp.sin(angle), jnp.cos(angle)], axis=1)


def exchange(block, axis):
    return lax.all_to_all(block, axis, 0, 0, tiled=True)


def spread(block, axis):
    return exchange(jnp.broadcast_to(block[None], (lax.axis_size(axis),) + block.shape), axis)


def z_shift(block, step):
    return lax.ppermute(block, "z", [(z, (z + step) % NZ) for z in range(NZ)])


def around(block):
    got = {0: block}
    for step in (1, -1, 2, -2):
        got[step % NZ] = z_shift(block, step)
    got[3] = z_shift(got[2], 1)
    got[5] = z_shift(got[6], -1)
    got[4] = z_shift(got[2], 2)
    return [[got[k]] for k in range(NZ)]


def swap_core(block):
    return lax.ppermute(block, "core", [(0, 1), (1, 0)])


def local(
    patches,
    keep_pos,
    kept_counts,
    enc_gain,
    w_qkv,
    w_out,
    w_e2d,
    mask_token,
    dec_gain,
    fc_in,
    fc_out,
    cotangent,
):
    me = lax.axis_index(SEQ)
    my_z, my_c = me // 2, me % 2
    fdev = cotangent.shape[1]
    cot = cotangent[0]
    cap = keep_pos.shape[1]
    rows = 16 * cap

    xn_own, x_slot, offsets = prep(keep_pos, enc_gain, patches[0])
    x_vis, w_oe_own, pack = pack_up(x_slot, w_out, w_e2d, fc_in, fc_out)
    weights = lax.all_gather(pack, SEQ, axis=0)

    places = jnp.pad(offsets[:, 0].reshape(16, 1, SLOTS), ((0, 0), (0, 0), (0, 128 - SLOTS)))
    extra = jnp.concatenate(
        [x_vis.reshape(16, 12, 128), places, jnp.zeros((16, 3, 128), BF16)], axis=1)

    tok = jnp.arange(rows, dtype=jnp.int32)
    block = tok // cap
    source = (my_z - block % NZ) % NZ * 2 + (my_c ^ (block // NZ))
    inside = tok % cap
    dest = inside // SLOTS * cap + source * SLOTS + inside % SLOTS
    swap = (dest[None, :] == tok[:, None]).astype(BF16)
    table = position_table((me * fdev + jnp.arange(fdev, dtype=jnp.int32)).astype(F32), DD)

    w = turn(w_qkv.transpose(0, 2, 1).reshape(3 * HD, -1))
    blocks = around(xn_own)
    blocks[4][0], w, swap, extra = lax.optimization_barrier((blocks[4][0], w, swap, extra))
    mine = join(blocks)
    other = swap_core(mine)
    sent, saved, stats = attend(mine, other, w, swap, extra)
    came = exchange(sent, SEQ)
    recon, dvis_own = decode(came, weights, cot, mask_token[None], dec_gain[None], table)
    dvis = lax.all_gather(dvis_own, SEQ, axis=0, tiled=True)
    parts = back(dvis, w_oe_own, swap, saved, stats, mine, other)

    parts = jnp.sum(exchange(parts.reshape(NX, 832, 128), "x").astype(F32), axis=0).astype(BF16)
    parts = jnp.sum(exchange(parts.reshape(NY, 104, 128), "y").astype(F32), axis=0).astype(BF16)
    parts = spread(parts, "y").reshape(832, 128)
    total = spread(parts, "x").reshape(GRAD_ROWS, 128)
    grad_q, grad_o = finish(total, w_e2d)
    grad_q = grad_q.reshape(3, HD, -1).transpose(0, 2, 1)
    return (recon[None], grad_q, grad_o)


def solution(mesh):
    axes = Mesh(mesh.devices.reshape(NY, NX, NZ, 2), ("y", "x", "z", "core"))
    dp = ("y", "x")
    placed = (
        P(dp, SEQ, None),
        P(dp, SEQ),
        P(dp, None),
        P(),
        P(None, None, SEQ),
        P(SEQ, None),
        P(),
        P(),
        P(),
        P(SEQ, None),
        P(SEQ, None),
        P(dp, SEQ, None),
    )
    return jax.shard_map(
        local,
        mesh=axes,
        in_specs=placed,
        out_specs=(P(dp, SEQ, None), P(None, None, SEQ), P(SEQ, None)),
        check_vma=False,
    )
```
